256 devices in a mesh: band: 16 (over x, y), mesh: 8 (over z), rep: 2 (over core).
Axes of the slice: x: 4, y: 4, z: 8, core: 2. Of those that a mesh axis runs over, the one named last changes fastest.
Arguments:
- grid_latent: bfloat16 [2, 65536, 512], P('rep', ('band', 'mesh')), may hold values from -6 to 6
- mesh_latent: bfloat16 [2, 16384, 512], P('rep', ('band', 'mesh')), may hold values from -6 to 6
- edge_latent: bfloat16 [2, 131072, 512], P('rep', ('band', 'mesh')), may hold values from -6 to 6
- mesh_cotangent: bfloat16 [2, 16384, 512], P('rep', ('band', 'mesh')), may hold values from -6 to 6
- w_first: bfloat16 [1536, 512], replicated, may hold values from -0.15625 to 0.15625
- w_second: bfloat16 [512, 512], replicated, may hold values from -0.25 to 0.25
- norm_gain: float32 [512], replicated, may hold values from 0.1 to 1.9
- senders: int32 [131072], P(('band', 'mesh')), may hold values from 0 to 65535, as said below
- receivers: int32 [131072], P(('band', 'mesh')), may hold values from 0 to 16383, as said below
- live_counts: int32 [128], P(('band', 'mesh')), may hold values from 512 to 1024, as said below
Outputs:
- grid_grad: bfloat16 [2, 65536, 512], P('rep', ('band', 'mesh'))
- mesh_grad: float32 [2, 16384, 512], P('rep', ('band', 'mesh'))
- edge_grad: bfloat16 [2, 131072, 512], P('rep', ('band', 'mesh'))
- first_grad: float32 [1536, 512], replicated
- second_grad: float32 [512, 512], replicated
- gain_grad: float32 [512], replicated
The draws below stay inside these ranges and needn't reach their ends.
Inputs may be any that keep to these rules, and one draw needn't show every extreme that they name: `senders`: A slot of sub-band k (slots k * 1024 to (k + 1) * 1024 - 1) names a grid node of that sub-band, k * 512 to (k + 1) * 512 - 1. `receivers`: A slot of sub-band k names a mesh node of sub-bands k - 1, k or k + 1, that is (k - 1) * 128 to (k + 2) * 128 - 1, within the mesh. `live_counts`: some sub-band has all its 1024 slots live.
All inputs are finite; a program needn't handle non-finite values.
Results may differ from the reference program's by a relative error of at most 0.012.
Values may be sent and summed in bfloat16 or wider, within the bound.
No kernel may reach another device: no remote copies, remote signals or barrier semaphores. Data moves between devices by JAX's collectives and lax.ppermute only.
A program may use at most 64 MiB of HBM per device.

```python
import math
import jax
import jax.numpy as jnp
from jax import lax

D = 512
GDEV = 512
MDEV = 128
EDEV = 1024
SHARDS = 128
SAMPLES = 2
GRID = 65536
MESH = 16384
EDGE_ALL = 131072


def draw_senders(key, part):
    key = jax.random.fold_in(key, 11)
    owner = jnp.arange(SHARDS * EDEV, dtype=jnp.int32) // EDEV
    offset = jax.random.randint(key, (SHARDS * EDEV,), 0, GDEV, dtype=jnp.int32)
    offset = offset.at[0].set(0).at[SHARDS * EDEV - 1].set(GDEV - 1)
    return owner * GDEV + offset


def draw_receivers(key, part):
    key = jax.random.fold_in(key, 12)
    owner = jnp.arange(SHARDS * EDEV, dtype=jnp.int32) // EDEV
    lowest = jnp.maximum(owner - 1, 0) * MDEV
    highest = jnp.minimum(owner + 2, SHARDS) * MDEV
    picked = jax.random.randint(key, (SHARDS * EDEV,), lowest, highest, dtype=jnp.int32)
    return picked.at[0].set(0).at[SHARDS * EDEV - 1].set(MDEV * SHARDS - 1)


def draw_live_counts(key, part):
    key = jax.random.fold_in(key, 13)
    first_key, second_key = jax.random.split(key)
    counts = jax.random.randint(first_key, (SHARDS,), EDEV // 2, EDEV + 1, dtype=jnp.int32)
    fullest = jax.random.randint(second_key, (), 0, SHARDS, dtype=jnp.int32)
    return counts.at[fullest].set(EDEV)


def levels(key, dims, cuts, low, largest):
    def one(dim, shards_of):
        steps = jax.random.uniform(jax.random.fold_in(jax.random.fold_in(key, 6), dim), (shards_of,), jnp.float32, low / len(cuts), largest / len(cuts))
        return jnp.repeat(jnp.exp(steps), dims[dim] // shards_of).reshape((-1,) + (1,) * (len(dims) - dim - 1))

    level = one(*cuts[0])
    for cut in cuts[1:]:
        level = level * one(*cut)
    return level


def scatter_about(key, dims, spread, bound, cuts=(), kind=jnp.bfloat16):
    loudness = levels(key, dims, cuts, -0.22, 0.18) if cuts else 1.0
    values = jax.random.normal(key, dims, jnp.float32) * spread * loudness
    return jnp.minimum(jnp.maximum(values, -bound), bound).astype(kind)


def setup_inputs(seed: int = 0) -> dict:
    key_list = jax.random.split(jax.random.key(seed), 11)
    grid_latent = scatter_about(key_list[0], (SAMPLES, GRID, D), 1.0, 6.0, ((0, 2), (1, 128)))
    mesh_latent = scatter_about(key_list[1], (SAMPLES, MESH, D), 1.0, 6.0, ((0, 2), (1, 128)))
    edge_latent = scatter_about(key_list[2], (SAMPLES, EDGE_ALL, D), 1.0, 6.0, ((0, 2), (1, 128)))
    mesh_cotangent = scatter_about(key_list[3], (SAMPLES, MESH, D), 1.0, 6.0, ((0, 2), (1, 128)))
    w_first = scatter_about(key_list[4], (3 * D, D), (3 * D) ** -0.5, 0.15625)
    w_second = scatter_about(key_list[5], (D, D), D ** -0.5, 0.25)
    norm_gain = jnp.clip(1.0 + 0.18 * jax.random.normal(key_list[6], (D,), jnp.float32), 0.1, 1.9)
    senders = draw_senders(jax.random.fold_in(key_list[10], 71), 0)
    receivers = draw_receivers(jax.random.fold_in(key_list[10], 71), 0)
    live_counts = draw_live_counts(jax.random.fold_in(key_list[10], 71), 0)
    return dict(grid_latent=grid_latent, mesh_latent=mesh_latent, edge_latent=edge_latent, mesh_cotangent=mesh_cotangent, w_first=w_first, w_second=w_second, norm_gain=norm_gain, senders=senders, receivers=receivers, live_counts=live_counts)


NORM_EPS = 1e-05

def contract_rows(left, right):
    return lax.dot_general(left, right, (((0,), (0,)), ((), ())), preferred_element_type=jnp.float32)

def contract_cols(left, right):
    return lax.dot_general(left, right, (((1,), (1,)), ((), ())), preferred_element_type=jnp.float32)

def edge_backward(features, cotangent, live_mask, w_first, w_second, norm_gain):
    pre_act = jnp.dot(features, w_first, preferred_element_type=jnp.float32)
    hidden = jax.nn.silu(pre_act).astype(jnp.bfloat16)
    output = jnp.dot(hidden, w_second, preferred_element_type=jnp.float32)
    centered = output - lax.optimization_barrier(jnp.mean(output, axis=1, keepdims=True))
    inverse = lax.rsqrt(lax.optimization_barrier(jnp.mean(centered * centered, axis=1, keepdims=True)) + NORM_EPS)
    normed = centered * inverse
    upstream = jnp.where(live_mask[:, None], cotangent.astype(jnp.float32), jnp.float32(0.0))
    gain_term = lax.optimization_barrier(jnp.sum(upstream * normed, axis=0))
    scaled = upstream * norm_gain
    grad_output = (inverse * (scaled - lax.optimization_barrier(jnp.mean(scaled, axis=1, keepdims=True)) - normed * lax.optimization_barrier(jnp.mean(scaled * normed, axis=1, keepdims=True)))).astype(jnp.bfloat16)
    second_term = contract_rows(hidden, grad_output)
    grad_hidden = contract_cols(grad_output, w_second)
    sigmoid = jax.nn.sigmoid(pre_act)
    grad_pre = (grad_hidden * sigmoid * (1.0 + pre_act * (1.0 - sigmoid))).astype(jnp.bfloat16)
    first_term = contract_rows(features, grad_pre)
    return (grad_pre, first_term, second_term, gain_term)

def reference(grid_latent, mesh_latent, edge_latent, mesh_cotangent, w_first, w_second, norm_gain, senders, receivers, live_counts):
    shard_total = live_counts.shape[0]
    model_width = w_second.shape[0]
    rows_grid = grid_latent.shape[1] // shard_total
    rows_mesh = mesh_latent.shape[1] // shard_total
    slot_count = senders.shape[0] // shard_total
    sample_count = grid_latent.shape[0]
    factor = 1.0 / math.sqrt(senders.shape[0] * sample_count)
    first_total = jnp.zeros((3 * model_width, model_width), jnp.float32)
    second_total = jnp.zeros((model_width, model_width), jnp.float32)
    gain_total = jnp.zeros((model_width,), jnp.float32)
    grid_list, mesh_list, edge_list = ([], [], [])
    for sample in range(sample_count):
        grid_rows = grid_latent[sample]
        mesh_rows = mesh_latent[sample]
        edge_rows = edge_latent[sample]
        cot_rows = mesh_cotangent[sample]

        def shard_step(totals, shard_index):
            first_acc, second_acc, gain_acc, mesh_acc = totals
            sender_rows = lax.dynamic_slice_in_dim(senders, shard_index * slot_count, slot_count)
            receiver_rows = lax.dynamic_slice_in_dim(receivers, shard_index * slot_count, slot_count)
            own_edges = lax.dynamic_slice_in_dim(edge_rows, shard_index * slot_count, slot_count, 0)
            features = jnp.concatenate([own_edges, jnp.take(grid_rows, sender_rows, axis=0), jnp.take(mesh_rows, receiver_rows, axis=0)], axis=1)
            cotangent = jnp.take(cot_rows, receiver_rows, axis=0)
            live_mask = lax.iota(jnp.int32, slot_count) < live_counts[shard_index]
            grad_pre, first_term, second_term, gain_term = edge_backward(features, cotangent, live_mask, w_first, w_second, norm_gain)
            grad_features = contract_cols(grad_pre, w_first)
            edge_part = grad_features[:, :model_width].astype(jnp.bfloat16)
            grid_part = jax.ops.segment_sum(grad_features[:, model_width:2 * model_width], sender_rows - shard_index * rows_grid, num_segments=rows_grid).astype(jnp.bfloat16)
            nearby = jax.ops.segment_sum(grad_features[:, 2 * model_width:], receiver_rows - (shard_index - 1) * rows_mesh, num_segments=3 * rows_mesh)
            window = lax.dynamic_slice_in_dim(mesh_acc, shard_index * rows_mesh, 3 * rows_mesh, 0)
            mesh_acc = lax.dynamic_update_slice_in_dim(mesh_acc, window + nearby, shard_index * rows_mesh, 0)
            return ((first_acc + first_term, second_acc + second_term, gain_acc + gain_term, mesh_acc), (edge_part, grid_part))
        start = (first_total, second_total, gain_total, jnp.zeros(((shard_total + 2) * rows_mesh, model_width), jnp.float32))
        ended, stacked = lax.scan(shard_step, start, jnp.arange(shard_total, dtype=jnp.int32))
        first_total, second_total, gain_total, mesh_acc = ended
        edge_list.append(stacked[0].reshape(-1, model_width))
        grid_list.append(stacked[1].reshape(-1, model_width))
        mesh_list.append(mesh_acc[rows_mesh:(shard_total + 1) * rows_mesh])
    return (jnp.stack(grid_list), jnp.stack(mesh_list), jnp.stack(edge_list), first_total * factor, second_total * factor, gain_total * factor)
```

```python
import math

import jax
import jax.numpy as jnp
from jax import lax
from jax.sharding import PartitionSpec as P

NORM_EPS = 1e-05


def passed_along(value, axis, steps):
    count = lax.axis_size(axis)
    leading, last = (max(0, -steps), min(count, count - steps))
    return lax.ppermute(value, axis, [(source, source + steps) for source in range(leading, last)])


def padded(shard, sides, width):
    for axis, dim in sides:
        peers, length = (lax.axis_size(axis), shard.shape[dim])
        up = [(i, (i + 1) % peers) for i in range(peers - 1)]
        down = [(j, i) for i, j in up]
        last = lax.slice_in_dim(shard, length - width, length, axis=dim)
        leading = lax.slice_in_dim(shard, 0, width, axis=dim)
        before = lax.ppermute(last, axis, up)
        after = lax.ppermute(leading, axis, down)
        shard = jnp.concatenate([before, shard, after], axis=dim)
    return shard


def contract_rows(left, right):
    return lax.dot_general(
        left, right, (((0,), (0,)), ((), ())), preferred_element_type=jnp.float32
    )


def contract_cols(left, right, accuracy=None):
    return lax.dot_general(
        left,
        right,
        (((1,), (1,)), ((), ())),
        precision=accuracy,
        preferred_element_type=jnp.float32,
    )


def onehot_table(indices, width):
    return (indices[:, None] == lax.iota(jnp.int32, width)[None, :]).astype(jnp.bfloat16)


def pick_rows(table, rows):
    return jnp.dot(table, rows, preferred_element_type=jnp.float32).astype(jnp.bfloat16)


def gather_sums(table, terms):
    upper = terms.astype(jnp.bfloat16)
    lower = (terms - upper.astype(jnp.float32)).astype(jnp.bfloat16)
    return contract_rows(table, upper) + contract_rows(table, lower)


def edge_backward(features, cotangent, live_mask, w_first, w_second, norm_gain):
    pre_act = jnp.dot(features, w_first, preferred_element_type=jnp.float32)
    hidden = jax.nn.silu(pre_act).astype(jnp.bfloat16)
    output = jnp.dot(hidden, w_second, preferred_element_type=jnp.float32)
    centered = output - jnp.mean(output, axis=1, keepdims=True)
    inverse = lax.rsqrt(jnp.mean(centered * centered, axis=1, keepdims=True) + NORM_EPS)
    normed = centered * inverse
    upstream = jnp.where(live_mask[:, None], cotangent.astype(jnp.float32), jnp.float32(0.0))
    gain_term = jnp.sum(upstream * normed, axis=0)
    scaled = upstream * norm_gain
    grad_output = (
        inverse
        * (
            scaled
            - jnp.mean(scaled, axis=1, keepdims=True)
            - normed * jnp.mean(scaled * normed, axis=1, keepdims=True)
        )
    ).astype(jnp.bfloat16)
    second_term = contract_rows(hidden, grad_output)
    grad_hidden = contract_cols(grad_output, w_second)
    sigmoid = jax.nn.sigmoid(pre_act)
    grad_pre = (grad_hidden * sigmoid * (1.0 + pre_act * (1.0 - sigmoid))).astype(jnp.bfloat16)
    first_term = contract_rows(features, grad_pre)
    return (grad_pre, first_term, second_term, gain_term)


def return_rims(terms, rows_mesh):
    from_above = passed_along(terms[:rows_mesh].astype(jnp.bfloat16), ("band", "mesh"), -1).astype(
        jnp.float32
    )
    from_below = passed_along(
        terms[2 * rows_mesh :].astype(jnp.bfloat16), ("band", "mesh"), 1
    ).astype(jnp.float32)
    return terms[rows_mesh : 2 * rows_mesh] + from_above + from_below


def swapped(value):
    return lax.ppermute(value, "rep", [(0, 1), (1, 0)])


def summed_shares(shares):
    return jnp.sum(shares.astype(jnp.float32), axis=0)


def total_over_devices(terms, gain_term, factor):
    rows, width = terms.shape
    bands, meshes = lax.axis_size("band"), lax.axis_size("mesh")
    half = rows // 2
    part = half // bands
    piece = part // meshes
    core = lax.axis_index("rep")
    blocks = terms.reshape(2, half, width)
    kept = lax.dynamic_index_in_dim(blocks, core, 0, False)
    sent = lax.dynamic_index_in_dim(blocks, 1 - core, 0, False)

    def with_gain(shares, gain):
        upper = gain.astype(jnp.bfloat16)
        lower = (gain - upper.astype(jnp.float32)).astype(jnp.bfloat16)
        extra = jnp.concatenate(
            [upper[None], lower[None], jnp.zeros((6, width), jnp.bfloat16)], axis=0
        )
        extra = jnp.broadcast_to(extra[None], (shares.shape[0], 8, width))
        return jnp.concatenate([shares.astype(jnp.bfloat16), extra], axis=1)

    def split_gain(total, rows_here):
        return total[:rows_here], total[rows_here] + total[rows_here + 1]

    got = swapped(with_gain(sent[None], gain_term)[0]).astype(jnp.float32)
    got, gain_got = split_gain(got, half)
    total, gain = kept + got, gain_term + gain_got
    got = lax.all_to_all(with_gain(total.reshape(bands, part, width), gain), "band", 0, 0)
    total, gain = split_gain(summed_shares(got), part)
    got = lax.all_to_all(with_gain(total.reshape(meshes, piece, width), gain), "mesh", 0, 0)
    total, gain = split_gain(summed_shares(got), piece)
    total = (total * factor).astype(jnp.bfloat16)
    total = lax.all_to_all(jnp.broadcast_to(total[None], (meshes, piece, width)), "mesh", 0, 0)
    total = total.reshape(part, width)
    total = lax.all_to_all(jnp.broadcast_to(total[None], (bands, part, width)), "band", 0, 0)
    total = total.reshape(half, width)
    other = swapped(total)
    low = jnp.where(core == 0, total, other)
    high = jnp.where(core == 0, other, total)
    return jnp.concatenate([low, high], axis=0).astype(jnp.float32), gain * factor


def per_device(
    grid_latent,
    mesh_latent,
    edge_latent,
    mesh_cotangent,
    w_first,
    w_second,
    norm_gain,
    senders,
    receivers,
    live_counts,
):
    model_width = w_second.shape[0]
    rows_grid = grid_latent.shape[1]
    rows_mesh = mesh_latent.shape[1]
    slot_count = senders.shape[0]
    shard_index = lax.axis_index(("band", "mesh"))
    stacked = jnp.concatenate([mesh_latent, mesh_cotangent], axis=2)
    nearby = padded(stacked, ((("band", "mesh"), 1),), rows_mesh)[0]
    send_table = onehot_table(senders - shard_index * rows_grid, rows_grid)
    recv_table = onehot_table(receivers - (shard_index - 1) * rows_mesh, 3 * rows_mesh)
    picked = pick_rows(recv_table, nearby)
    features = jnp.concatenate(
        [edge_latent[0], pick_rows(send_table, grid_latent[0]), picked[:, :model_width]], axis=1
    )
    live_mask = lax.iota(jnp.int32, slot_count) < live_counts[0]
    grad_pre, first_term, second_term, gain_term = edge_backward(
        features, picked[:, model_width:], live_mask, w_first, w_second, norm_gain
    )
    devices = lax.axis_size("band") * lax.axis_size("mesh") * lax.axis_size("rep")
    factor = 1.0 / math.sqrt(slot_count * devices)
    weight_total, gain_total = total_over_devices(
        jnp.concatenate([first_term, second_term], axis=0), gain_term, factor
    )
    grad_features = contract_cols(grad_pre, w_first)
    grad_front = grad_features[:, : 2 * model_width]
    mesh_terms = gather_sums(recv_table, grad_features[:, 2 * model_width :])
    mesh_grad = return_rims(mesh_terms, rows_mesh)
    edge_grad = grad_front[:, :model_width].astype(jnp.bfloat16)
    grid_grad = gather_sums(send_table, grad_front[:, model_width:]).astype(jnp.bfloat16)
    return (
        grid_grad[None],
        mesh_grad[None],
        edge_grad[None],
        weight_total[: 3 * model_width],
        weight_total[3 * model_width :],
        gain_total,
    )


def solution(mesh):
    in_specs = (
        P("rep", ("band", "mesh"), None),
        P("rep", ("band", "mesh"), None),
        P("rep", ("band", "mesh"), None),
        P("rep", ("band", "mesh"), None),
        P(),
        P(),
        P(),
        P(("band", "mesh")),
        P(("band", "mesh")),
        P(("band", "mesh")),
    )
    out_specs = (
        P("rep", ("band", "mesh"), None),
        P("rep", ("band", "mesh"), None),
        P("rep", ("band", "mesh"), None),
        P(),
        P(),
        P(),
    )
    return jax.shard_map(
        per_device, mesh=mesh, in_specs=in_specs, out_specs=out_specs, check_vma=False
    )
```

```python
import functools
import math

import jax
import jax.numpy as jnp
from jax import lax
from jax.experimental import pallas as pl
from jax.experimental.pallas import tpu as pltpu
from jax.sharding import PartitionSpec as P

NORM_EPS = 1e-05
TILE = 256
LANES = 128
MIB = 1 << 20


def dot(left, right, left_dim=1, right_dim=0):
    return lax.dot_general(
        left,
        right,
        (((left_dim,), (right_dim,)), ((), ())),
        preferred_element_type=jnp.float32,
    )


def picks(row, width):
    edges = row.shape[1]
    column = jnp.transpose(jnp.broadcast_to(row, (LANES, edges)))
    lane = lax.broadcasted_iota(jnp.int32, (edges, LANES), 1)
    return jnp.concatenate(
        [(column == lane + start).astype(jnp.float32).astype(jnp.bfloat16) for start in range(0, width, LANES)],
        axis=1,
    )


def spreads(row, width):
    edges = row.shape[1]
    place = lax.broadcasted_iota(jnp.int32, (width, edges), 0)
    return (place == row).astype(jnp.float32).astype(jnp.bfloat16)


def upper_lower(value):
    upper = value.astype(jnp.bfloat16)
    return upper, (value - upper.astype(jnp.float32)).astype(jnp.bfloat16)


def gain_rows(gain):
    upper, lower = upper_lower(gain)
    place = lax.broadcasted_iota(jnp.int32, (8, gain.shape[1]), 0)
    return jnp.where(
        place == 0, upper.astype(jnp.float32), jnp.where(place == 1, lower.astype(jnp.float32), 0.0)
    )


def anywhere():
    return pl.BlockSpec(memory_space=pl.ANY)


def in_vmem():
    return pl.BlockSpec(memory_space=pltpu.VMEM)


def in_smem():
    return pl.BlockSpec(memory_space=pltpu.SMEM)


def call(kernel, name, specs, outs, operands, flops, scratch=(), limit=40 * MIB):
    size = sum(math.prod(o.shape) * o.dtype.itemsize for o in outs)
    size += sum(math.prod(o.shape) * o.dtype.itemsize for o in operands)
    return pl.pallas_call(
        kernel,
        out_shape=outs,
        in_specs=specs,
        out_specs=[in_vmem()] * len(outs),
        scratch_shapes=list(scratch),
        compiler_params=pltpu.CompilerParams(vmem_limit_bytes=limit),
        cost_estimate=pl.CostEstimate(flops=int(flops), bytes_accessed=size, transcendentals=0),
        name=name,
    )(*operands)


def near_kernel(scalars, senders, grid, edge, w_first, partial, grid_picked):
    rows_grid, width = grid.shape
    for start in range(0, edge.shape[0], TILE):
        rows = pl.ds(start, TILE)
        table = picks(senders[:, rows] - scalars[0], rows_grid)
        picked = dot(table, grid[...]).astype(jnp.bfloat16)
        grid_picked[rows, :] = picked
        partial[rows, :] = dot(edge[rows, :], w_first[0:width, :]) + dot(
            picked, w_first[width : 2 * width, :]
        )


def live_receivers(scalars, receivers, start):
    row = receivers[:, pl.ds(start, TILE)] - scalars[1]
    slot = start + lax.broadcasted_iota(jnp.int32, (1, TILE), 1)
    return jnp.where(slot < scalars[2], row, -1)


def edge_kernel(
    scalars,
    receivers,
    partial,
    grid_picked,
    edge,
    mesh_before,
    mesh_own,
    mesh_after,
    cot_before,
    cot_own,
    cot_after,
    w_first,
    w_second,
    norm_gain,
    sent,
    gain_term,
    grad_pre,
    grad_output,
    hidden,
    mesh_picked,
):
    width = w_second.shape[0]
    rows_mesh = mesh_own.shape[0]
    gain_sum = jnp.zeros((1, width), jnp.float32)
    for start in range(0, edge.shape[0], TILE):
        rows = pl.ds(start, TILE)
        table = picks(live_receivers(scalars, receivers, start), 3 * rows_mesh)

        def picked_rows(before, own, after):
            near = jnp.concatenate([before[...], own[...], after[...]], axis=0)
            return dot(table, near)

        latents = picked_rows(mesh_before, mesh_own, mesh_after).astype(jnp.bfloat16)
        upstream = picked_rows(cot_before, cot_own, cot_after)
        mesh_picked[rows, :] = latents
        pre_act = partial[rows, :] + dot(latents, w_first[2 * width : 3 * width, :])
        sigmoid = jax.nn.sigmoid(pre_act)
        hid = (pre_act * sigmoid).astype(jnp.bfloat16)
        hidden[rows, :] = hid
        output = dot(hid, w_second[...])
        centered = output - jnp.mean(output, axis=1, keepdims=True)
        inverse = lax.rsqrt(jnp.mean(centered * centered, axis=1, keepdims=True) + NORM_EPS)
        normed = centered * inverse
        gain_sum = gain_sum + jnp.sum(upstream * normed, axis=0, keepdims=True)
        scaled = upstream * norm_gain[...]
        grad_out = (
            inverse
            * (
                scaled
                - jnp.mean(scaled, axis=1, keepdims=True)
                - normed * jnp.mean(scaled * normed, axis=1, keepdims=True)
            )
        ).astype(jnp.bfloat16)
        grad_output[rows, :] = grad_out
        grad_hidden = dot(grad_out, w_second[...], 1, 1)
        grad_pre[rows, :] = (grad_hidden * sigmoid * (1.0 + pre_act * (1.0 - sigmoid))).astype(
            jnp.bfloat16
        )
    gain_term[...] = jnp.broadcast_to(gain_sum, gain_term.shape)
    sent[2 * width : 2 * width + 16, :] = jnp.concatenate(
        [gain_rows(gain_sum), jnp.zeros((8, width), jnp.float32)], axis=0
    ).astype(jnp.bfloat16)

    @pl.when(scalars[3] == 0)
    def _():
        sent[0:width, :] = dot(mesh_picked[...], grad_pre[...], 0, 0).astype(jnp.bfloat16)
        sent[width : 2 * width, :] = dot(hidden[...], grad_output[...], 0, 0).astype(jnp.bfloat16)

    @pl.when(scalars[3] != 0)
    def _():
        sent[0:width, :] = dot(edge[...], grad_pre[...], 0, 0).astype(jnp.bfloat16)
        sent[width : 2 * width, :] = dot(grid_picked[...], grad_pre[...], 0, 0).astype(jnp.bfloat16)


def kept_kernel(scalars, edge, grid_picked, mesh_picked, hidden, grad_pre, grad_output, kept):
    width = grad_pre.shape[1]

    @pl.when(scalars[3] != 0)
    def _():
        kept[0:width, :] = dot(mesh_picked[...], grad_pre[...], 0, 0)
        kept[width : 2 * width, :] = dot(hidden[...], grad_output[...], 0, 0)

    @pl.when(scalars[3] == 0)
    def _():
        kept[0:width, :] = dot(edge[...], grad_pre[...], 0, 0)
        kept[width : 2 * width, :] = dot(grid_picked[...], grad_pre[...], 0, 0)


def pack_kernel(kept, got, gain_term, packed):
    bands = packed.shape[0]
    half, width = kept.shape
    part = half // bands
    tail = got[half : half + 16, :].astype(jnp.float32)
    gain = gain_rows(gain_term[0:1, :] + tail[0:1] + tail[1:2])
    for band in range(bands):
        rows = pl.ds(band * part, part)
        data = kept[rows, :] + got[rows, :].astype(jnp.float32)
        packed[band] = jnp.concatenate([data, gain], axis=0).astype(jnp.bfloat16)


def band_sum_kernel(shares, after, packed):
    meshes, rows = packed.shape[0], packed.shape[1] - 8
    total = shares[0].astype(jnp.float32)
    for band in range(1, shares.shape[0]):
        total = total + shares[band].astype(jnp.float32)
    part = rows * meshes
    gain = gain_rows(total[part : part + 1] + total[part + 1 : part + 2])
    for place in range(meshes):
        data = total[place * rows : (place + 1) * rows]
        packed[place] = jnp.concatenate([data, gain], axis=0).astype(jnp.bfloat16)


def mesh_sum_kernel(factor, shares, copies, gain_grad):
    total = shares[0].astype(jnp.float32)
    for place in range(1, shares.shape[0]):
        total = total + shares[place].astype(jnp.float32)
    total = total * factor
    rows = copies.shape[1]
    gain_grad[...] = jnp.broadcast_to(total[rows : rows + 1] + total[rows + 1 : rows + 2], gain_grad.shape)
    data = total[0:rows].astype(jnp.bfloat16)
    for place in range(copies.shape[0]):
        copies[place] = data


def node_kernel(
    scalars,
    senders,
    receivers,
    grad_pre,
    w_first,
    after,
    edge_grad,
    grid_grad,
    mesh_own,
    to_below,
    to_above,
    done,
):
    edges, width = grad_pre.shape
    rows_grid, rows_mesh = grid_grad.shape[0], mesh_own.shape[0]

    def through(sums, first):
        upper, lower = upper_lower(sums)
        weights = w_first[first : first + width, :]
        return dot(upper, weights, 1, 1) + dot(lower, weights, 1, 1)

    near = jnp.zeros((3 * rows_mesh, width), jnp.float32)
    here = jnp.zeros((rows_grid, width), jnp.float32)
    for start in range(0, edges, TILE):
        rows = pl.ds(start, TILE)
        terms = grad_pre[rows, :]
        near = near + dot(spreads(live_receivers(scalars, receivers, start), 3 * rows_mesh), terms)
        here = here + dot(spreads(senders[:, rows] - scalars[0], rows_grid), terms)
        edge_grad[rows, :] = dot(terms, w_first[0:width, :], 1, 1).astype(jnp.bfloat16)
    mesh_terms = through(near, 2 * width)
    to_below[...] = mesh_terms[0:rows_mesh].astype(jnp.bfloat16)
    mesh_own[...] = mesh_terms[rows_mesh : 2 * rows_mesh]
    to_above[...] = mesh_terms[2 * rows_mesh : 3 * rows_mesh].astype(jnp.bfloat16)
    grid_grad[...] = through(here, width).astype(jnp.bfloat16)
    done[...] = jnp.zeros(done.shape, jnp.float32)


def final_kernel(scalars, own, other, first, second):
    step = pl.program_id(0)
    rows = pl.ds(pl.multiple_of((step % 2) * 512, 512), 512)
    mine = (step // 2) == scalars[3]

    def put(into):
        @pl.when(mine)
        def _():
            into[...] = own[rows, :].astype(jnp.float32)

        @pl.when(jnp.logical_not(mine))
        def _():
            into[...] = other[rows, :].astype(jnp.float32)

    @pl.when(step < 3)
    def _():
        put(first)

    @pl.when(step == 3)
    def _():
        put(second)


def passed_along(value, steps):
    count = lax.axis_size("band") * lax.axis_size("mesh")
    leading, last = (max(0, -steps), min(count, count - steps))
    return lax.ppermute(value, ("band", "mesh"), [(s, s + steps) for s in range(leading, last)])


def swapped(value):
    return lax.ppermute(value, "rep", [(0, 1), (1, 0)])


def everywhere(value, axis):
    count = lax.axis_size(axis)
    return lax.all_to_all(jnp.broadcast_to(value[None], (count,) + value.shape), axis, 0, 0)


def per_device(
    grid_latent,
    mesh_latent,
    edge_latent,
    mesh_cotangent,
    w_first,
    w_second,
    norm_gain,
    senders,
    receivers,
    live_counts,
):
    width = w_second.shape[0]
    rows_grid = grid_latent.shape[1]
    rows_mesh = mesh_latent.shape[1]
    slots = senders.shape[0]
    bands, meshes = lax.axis_size("band"), lax.axis_size("mesh")
    factor = 1.0 / math.sqrt(slots * bands * meshes * lax.axis_size("rep"))
    shard = lax.axis_index(("band", "mesh"))
    scalars = jnp.stack(
        [
            shard * rows_grid,
            (shard - 1) * rows_mesh,
            live_counts[0],
            lax.axis_index("rep").astype(jnp.int32),
        ]
    ).astype(jnp.int32)
    senders, receivers = senders[None], receivers[None]
    gain = norm_gain[None]
    grid, mesh, edge, cot = grid_latent[0], mesh_latent[0], edge_latent[0], mesh_cotangent[0]
    matrix = functools.partial(jax.ShapeDtypeStruct, dtype=jnp.bfloat16)
    floats = functools.partial(jax.ShapeDtypeStruct, dtype=jnp.float32)
    unit = 2.0 * slots * width * width

    mesh_before, mesh_after = passed_along(mesh, 1), passed_along(mesh, -1)
    cot_before, cot_after = passed_along(cot, 1), passed_along(cot, -1)
    partial, grid_picked = call(
        near_kernel,
        "near",
        [in_smem()] + [in_vmem()] * 4,
        [floats((slots, width)), matrix((slots, width))],
        (scalars, senders, grid, edge, w_first),
        3 * unit,
    )
    sent, gain_term, grad_pre, grad_output, hidden, mesh_picked = call(
        edge_kernel,
        "edges",
        [in_smem()] + [in_vmem()] * 13,
        [matrix((2 * width + 16, width)), floats((8, width))] + [matrix((slots, width))] * 4,
        (
            scalars,
            receivers,
            partial,
            grid_picked,
            edge,
            mesh_before,
            mesh,
            mesh_after,
            cot_before,
            cot,
            cot_after,
            w_first,
            w_second,
            gain,
        ),
        7 * unit,
    )
    got = swapped(sent)
    (kept,) = call(
        kept_kernel,
        "kept",
        [in_smem()] + [in_vmem()] * 6,
        [floats((2 * width, width))],
        (scalars, edge, grid_picked, mesh_picked, hidden, grad_pre, grad_output),
        2 * unit,
    )
    part, piece = 2 * width // bands, 2 * width // (bands * meshes)
    (packed,) = call(
        pack_kernel,
        "pack",
        [in_vmem()] * 3,
        [matrix((bands, part + 8, width))],
        (kept, got, gain_term),
        0,
    )
    edge_grad, grid_grad, mesh_own, to_below, to_above, done = call(
        node_kernel,
        "nodes",
        [in_smem()] + [in_vmem()] * 4 + [anywhere()],
        [
            matrix((slots, width)),
            matrix((rows_grid, width)),
            floats((rows_mesh, width)),
            matrix((rows_mesh, width)),
            matrix((rows_mesh, width)),
            floats((8, LANES)),
        ],
        (scalars, senders, receivers, grad_pre, w_first, packed),
        4 * unit,
    )
    shares = lax.all_to_all(packed, "band", 0, 0)
    (packed,) = call(
        band_sum_kernel,
        "band_sum",
        [in_vmem(), anywhere()],
        [matrix((meshes, piece + 8, width))],
        (shares, done),
        0,
    )
    shares = lax.all_to_all(packed, "mesh", 0, 0)
    copies, gain_grad = call(
        functools.partial(mesh_sum_kernel, factor),
        "mesh_sum",
        [in_vmem()],
        [matrix((meshes, piece, width)), floats((8, width))],
        (shares,),
        0,
    )
    total = lax.all_to_all(copies, "mesh", 0, 0).reshape(part, width)
    total = everywhere(total, "band").reshape(2 * width, width)
    other = swapped(total)
    first_grad, second_grad = pl.pallas_call(
        final_kernel,
        grid=(4,),
        out_shape=[floats((3 * width, width)), floats((width, width))],
        in_specs=[in_smem()] + [in_vmem()] * 2,
        out_specs=[
            pl.BlockSpec((width, width), lambda i: (jnp.minimum(i, 2), 0)),
            pl.BlockSpec((width, width), lambda i: (0, 0)),
        ],
        compiler_params=pltpu.CompilerParams(vmem_limit_bytes=24 * MIB),
        name="final",
    )(scalars, total, other)

    from_above = passed_along(to_below, -1).astype(jnp.float32)
    from_below = passed_along(to_above, 1).astype(jnp.float32)
    mesh_grad = mesh_own + from_above + from_below
    return (
        grid_grad[None],
        mesh_grad[None],
        edge_grad[None],
        first_grad,
        second_grad,
        gain_grad[0],
    )


def solution(mesh):
    in_specs = (
        P("rep", ("band", "mesh"), None),
        P("rep", ("band", "mesh"), None),
        P("rep", ("band", "mesh"), None),
        P("rep", ("band", "mesh"), None),
        P(),
        P(),
        P(),
        P(("band", "mesh")),
        P(("band", "mesh")),
        P(("band", "mesh")),
    )
    out_specs = (
        P("rep", ("band", "mesh"), None),
        P("rep", ("band", "mesh"), None),
        P("rep", ("band", "mesh"), None),
        P(),
        P(),
        P(),
    )
    return jax.shard_map(
        per_device, mesh=mesh, in_specs=in_specs, out_specs=out_specs, check_vma=False
    )
```

```python
import functools
import math

import jax
import jax.numpy as jnp
from jax import lax
from jax.experimental import pallas as pl
from jax.experimental.pallas import tpu as pltpu
from jax.sharding import PartitionSpec as P

NORM_EPS = 1e-05
SHARDS = ("band", "hi", "lo")
GROUP = ("band", "lo")
TILE = 256
LANES = 128
MIB = 1 << 20


def dot(left, right, left_dim=1, right_dim=0):
    return lax.dot_general(
        left,
        right,
        (((left_dim,), (right_dim,)), ((), ())),
        preferred_element_type=jnp.float32,
    )


def picks(row, width):
    edges = row.shape[1]
    column = jnp.transpose(jnp.broadcast_to(row, (LANES, edges)))
    lane = lax.broadcasted_iota(jnp.int32, (edges, LANES), 1)
    return jnp.concatenate(
        [(column == lane + start).astype(jnp.float32).astype(jnp.bfloat16) for start in range(0, width, LANES)],
        axis=1,
    )


def spreads(row, width):
    edges = row.shape[1]
    place = lax.broadcasted_iota(jnp.int32, (width, edges), 0)
    return (place == row).astype(jnp.float32).astype(jnp.bfloat16)


def upper_lower(value):
    upper = value.astype(jnp.bfloat16)
    return upper, (value - upper.astype(jnp.float32)).astype(jnp.bfloat16)


def gain_rows(gain, lanes):
    terms = [term.astype(jnp.float32) for term in upper_lower(gain)]
    count = gain.shape[1] // lanes
    return jnp.concatenate(
        [term[:, g * lanes : (g + 1) * lanes] for term in terms for g in range(count)], axis=0
    )


def gain_of(rows):
    count = rows.shape[0] // 2
    return jnp.concatenate([rows[g : g + 1] + rows[count + g : count + g + 1] for g in range(count)], axis=1)


def narrow(rows):
    return jnp.concatenate(
        [rows[:, g : g + LANES] for g in range(0, rows.shape[1], LANES)], axis=0
    )


def anywhere():
    return pl.BlockSpec(memory_space=pl.ANY)


def in_vmem():
    return pl.BlockSpec(memory_space=pltpu.VMEM)


def in_hbm():
    return pl.BlockSpec(memory_space=pltpu.HBM)


def in_smem():
    return pl.BlockSpec(memory_space=pltpu.SMEM)


def call(kernel, name, specs, outs, operands, flops, scratch=(), limit=24 * MIB):
    operands = [
        pltpu.with_memory_space_constraint(o, pltpu.HBM) if spec.memory_space == pltpu.HBM else o
        for o, spec in zip(operands, specs)
    ]
    size = sum(math.prod(o.shape) * jnp.dtype(o.dtype).itemsize for o in outs)
    size += sum(math.prod(o.shape) * jnp.dtype(o.dtype).itemsize for o in operands)
    return pl.pallas_call(
        kernel,
        out_shape=outs,
        in_specs=specs,
        out_specs=[in_vmem()] * len(outs),
        scratch_shapes=list(scratch),
        compiler_params=pltpu.CompilerParams(vmem_limit_bytes=limit),
        cost_estimate=pl.CostEstimate(flops=int(flops), bytes_accessed=size, transcendentals=0),
        name=name,
    )(*operands)


def stack_kernel(mesh, cot, stacked, sems):
    rows = mesh.shape[0]
    copies = [
        pltpu.make_async_copy(mesh, stacked.at[pl.ds(0, rows)], sems.at[0]),
        pltpu.make_async_copy(cot, stacked.at[pl.ds(rows, rows)], sems.at[1]),
    ]
    for copy in copies:
        copy.start()
    for copy in copies:
        copy.wait()


def near_kernel(
    scalars,
    senders,
    grid,
    edge,
    w_first,
    partial,
    grid_picked,
    senders_here,
    grid_here,
    edge_here,
    w_here,
    sems,
):
    rows_grid, width = grid.shape
    copies = [
        pltpu.make_async_copy(senders, senders_here, sems.at[0]),
        pltpu.make_async_copy(grid, grid_here, sems.at[1]),
        pltpu.make_async_copy(w_first.at[pl.ds(0, 2 * width)], w_here, sems.at[2]),
    ]
    tiles = range(0, edge.shape[0], TILE)
    for place, start in enumerate(tiles):
        rows = pl.ds(start, TILE)
        copies.append(pltpu.make_async_copy(edge.at[rows], edge_here.at[rows], sems.at[place + 3]))
    for copy in copies:
        copy.start()
    for copy in copies[:3]:
        copy.wait()
    for start, copy in zip(tiles, copies[3:]):
        rows = pl.ds(start, TILE)
        table = picks(senders_here[:, rows] - scalars[0], rows_grid)
        picked = dot(table, grid_here[...]).astype(jnp.bfloat16)
        grid_picked[rows, :] = picked
        copy.wait()
        partial[rows, :] = dot(edge_here[rows, :], w_here[0:width, :]) + dot(
            picked, w_here[width : 2 * width, :]
        )


def live_receivers(scalars, receivers, start):
    row = receivers[:, pl.ds(start, TILE)] - scalars[1]
    slot = start + lax.broadcasted_iota(jnp.int32, (1, TILE), 1)
    return jnp.where(slot < scalars[2], row, -1)


def edge_kernel(
    scalars,
    receivers,
    partial,
    grid_picked,
    edge,
    stack_before,
    stack_own,
    stack_after,
    w_first,
    w_second,
    norm_gain,
    sent,
    gain_term,
    grad_pre,
    grad_output,
    hidden,
    mesh_picked,
):
    width = w_second.shape[0]
    rows_mesh = stack_own.shape[0] // 2
    gain_sum = jnp.zeros((1, width), jnp.float32)
    for start in range(0, edge.shape[0], TILE):
        rows = pl.ds(start, TILE)
        table = picks(live_receivers(scalars, receivers, start), 3 * rows_mesh)

        def picked_rows(first):
            part = pl.ds(first, rows_mesh)
            near = jnp.concatenate([stack_before[part, :], stack_own[part, :], stack_after[part, :]], axis=0)
            return dot(table, near)

        latents = picked_rows(0).astype(jnp.bfloat16)
        upstream = picked_rows(rows_mesh)
        mesh_picked[rows, :] = latents
        pre_act = partial[rows, :] + dot(latents, w_first[2 * width : 3 * width, :])
        sigmoid = jax.nn.sigmoid(pre_act)
        hid = (pre_act * sigmoid).astype(jnp.bfloat16)
        hidden[rows, :] = hid
        output = dot(hid, w_second[...])
        centered = output - jnp.mean(output, axis=1, keepdims=True)
        inverse = lax.rsqrt(jnp.mean(centered * centered, axis=1, keepdims=True) + NORM_EPS)
        normed = centered * inverse
        gain_sum = gain_sum + jnp.sum(upstream * normed, axis=0, keepdims=True)
        scaled = upstream * norm_gain[...]
        grad_out = (
            inverse
            * (
                scaled
                - jnp.mean(scaled, axis=1, keepdims=True)
                - normed * jnp.mean(scaled * normed, axis=1, keepdims=True)
            )
        ).astype(jnp.bfloat16)
        grad_output[rows, :] = grad_out
        grad_hidden = dot(grad_out, w_second[...], 1, 1)
        grad_pre[rows, :] = (grad_hidden * sigmoid * (1.0 + pre_act * (1.0 - sigmoid))).astype(
            jnp.bfloat16
        )
    gain_term[...] = jnp.broadcast_to(gain_sum, gain_term.shape)
    sent[2 * width : 2 * width + 16, :] = jnp.concatenate(
        [gain_rows(gain_sum, width), jnp.zeros((14, width), jnp.float32)], axis=0
    ).astype(jnp.bfloat16)

    @pl.when(scalars[3] == 0)
    def _():
        sent[0:width, :] = dot(mesh_picked[...], grad_pre[...], 0, 0).astype(jnp.bfloat16)
        sent[width : 2 * width, :] = dot(hidden[...], grad_output[...], 0, 0).astype(jnp.bfloat16)

    @pl.when(scalars[3] != 0)
    def _():
        sent[0:width, :] = dot(edge[...], grad_pre[...], 0, 0).astype(jnp.bfloat16)
        sent[width : 2 * width, :] = dot(grid_picked[...], grad_pre[...], 0, 0).astype(jnp.bfloat16)


def kept_kernel(scalars, edge, grid_picked, mesh_picked, hidden, grad_pre, grad_output, kept):
    width = grad_pre.shape[1]

    @pl.when(scalars[3] != 0)
    def _():
        kept[0:width, :] = dot(mesh_picked[...], grad_pre[...], 0, 0)
        kept[width : 2 * width, :] = dot(hidden[...], grad_output[...], 0, 0)

    @pl.when(scalars[3] == 0)
    def _():
        kept[0:width, :] = dot(edge[...], grad_pre[...], 0, 0)
        kept[width : 2 * width, :] = dot(grid_picked[...], grad_pre[...], 0, 0)


def pack_kernel(kept, got, gain_term, packed, done):
    count = packed.shape[0]
    half, width = kept.shape
    part = half // count
    tail = got[half : half + 16, :].astype(jnp.float32)
    gain = gain_rows(gain_term[0:1, :] + gain_of(tail[0:2]), LANES)
    for place in range(count):
        rows = pl.ds(place * part, part)
        data = narrow(kept[rows, :] + got[rows, :].astype(jnp.float32))
        packed[place] = jnp.concatenate([data, gain], axis=0).astype(jnp.bfloat16)
    done[...] = jnp.zeros(done.shape, jnp.float32)


def group_sum_kernel(shares, after, copies):
    total = shares[0].astype(jnp.float32)
    for place in range(1, shares.shape[0]):
        total = total + shares[place].astype(jnp.float32)
    data = total.shape[0] - 8
    gain = gain_rows(gain_of(total[data:]), LANES)
    row = jnp.concatenate([total[:data], gain], axis=0).astype(jnp.bfloat16)
    for place in range(copies.shape[0]):
        copies[place] = row


def whole_sum_kernel(factor, shares, copies, gain_grad):
    total = shares[0].astype(jnp.float32)
    for place in range(1, shares.shape[0]):
        total = total + shares[place].astype(jnp.float32)
    total = total * factor
    data = copies.shape[1]
    gain_grad[...] = jnp.broadcast_to(gain_of(total[data:]), gain_grad.shape)
    share = total[:data].astype(jnp.bfloat16)
    for place in range(copies.shape[0]):
        copies[place] = share


def node_kernel(
    scalars,
    senders,
    receivers,
    grad_pre,
    w_first,
    after,
    edge_grad,
    grid_grad,
    mesh_own,
    to_below,
    to_above,
):
    edges, width = grad_pre.shape
    rows_grid, rows_mesh = grid_grad.shape[0], mesh_own.shape[0]

    def through(sums, first):
        upper, lower = upper_lower(sums)
        weights = w_first[first : first + width, :]
        return dot(upper, weights, 1, 1) + dot(lower, weights, 1, 1)

    near = jnp.zeros((3 * rows_mesh, width), jnp.float32)
    here = jnp.zeros((rows_grid, width), jnp.float32)
    for start in range(0, edges, TILE):
        rows = pl.ds(start, TILE)
        terms = grad_pre[rows, :]
        near = near + dot(spreads(live_receivers(scalars, receivers, start), 3 * rows_mesh), terms)
        here = here + dot(spreads(senders[:, rows] - scalars[0], rows_grid), terms)
        edge_grad[rows, :] = dot(terms, w_first[0:width, :], 1, 1).astype(jnp.bfloat16)
    mesh_terms = through(near, 2 * width)
    to_below[...] = mesh_terms[0:rows_mesh].astype(jnp.bfloat16)
    mesh_own[...] = mesh_terms[rows_mesh : 2 * rows_mesh]
    to_above[...] = mesh_terms[2 * rows_mesh : 3 * rows_mesh].astype(jnp.bfloat16)
    grid_grad[...] = through(here, width).astype(jnp.bfloat16)


def final_kernel(scalars, own, other, first, second):
    step = pl.program_id(0)
    height, width = first.shape
    part = own.shape[1] * LANES // width
    shares = height // part
    blocks = own.shape[0] // shares
    mine = (step // blocks) == scalars[3]

    def put(into):
        def put_from(half):
            for place in range(shares):
                share = half[(step % blocks) * shares + place].astype(jnp.float32)
                for g in range(width // LANES):
                    into[place * part : (place + 1) * part, g * LANES : (g + 1) * LANES] = share[
                        g * part : (g + 1) * part
                    ]

        @pl.when(mine)
        def _():
            put_from(own)

        @pl.when(jnp.logical_not(mine))
        def _():
            put_from(other)

    @pl.when(step * height < 3 * width)
    def _():
        put(first)

    @pl.when(step * height >= 3 * width)
    def _():
        put(second)


def passed_along(value, steps):
    count = lax.axis_size(SHARDS)
    leading, last = (max(0, -steps), min(count, count - steps))
    return lax.ppermute(value, SHARDS, [(s, s + steps) for s in range(leading, last)])


def swapped(value):
    return lax.ppermute(value, "rep", [(0, 1), (1, 0)])


def per_device(
    grid_latent,
    mesh_latent,
    edge_latent,
    mesh_cotangent,
    w_first,
    w_second,
    norm_gain,
    senders,
    receivers,
    live_counts,
):
    width = w_second.shape[0]
    rows_grid = grid_latent.shape[1]
    rows_mesh = mesh_latent.shape[1]
    slots = senders.shape[0]
    group, groups = lax.axis_size(GROUP), lax.axis_size("hi")
    factor = 1.0 / math.sqrt(slots * group * groups * lax.axis_size("rep"))
    shard = lax.axis_index(SHARDS)
    scalars = jnp.stack(
        [
            shard * rows_grid,
            (shard - 1) * rows_mesh,
            live_counts[0],
            lax.axis_index("rep").astype(jnp.int32),
        ]
    ).astype(jnp.int32)
    senders, receivers = senders[None], receivers[None]
    gain = norm_gain[None]
    grid, mesh, edge, cot = grid_latent[0], mesh_latent[0], edge_latent[0], mesh_cotangent[0]
    matrix = functools.partial(jax.ShapeDtypeStruct, dtype=jnp.bfloat16)
    floats = functools.partial(jax.ShapeDtypeStruct, dtype=jnp.float32)
    unit = 2.0 * slots * width * width

    (stacked,) = call(
        stack_kernel,
        "stack",
        [in_hbm()] * 2,
        [matrix((2 * rows_mesh, width))],
        (mesh, cot),
        0,
        [pltpu.SemaphoreType.DMA((2,))],
    )
    stack_before, stack_after = passed_along(stacked, 1), passed_along(stacked, -1)
    partial, grid_picked = call(
        near_kernel,
        "near",
        [in_smem()] + [in_hbm()] * 4,
        [floats((slots, width)), matrix((slots, width))],
        (scalars, senders, grid, edge, w_first),
        3 * unit,
        [
            pltpu.VMEM((1, slots), jnp.int32),
            pltpu.VMEM((rows_grid, width), jnp.bfloat16),
            pltpu.VMEM((slots, width), jnp.bfloat16),
            pltpu.VMEM((2 * width, width), jnp.bfloat16),
            pltpu.SemaphoreType.DMA((3 + slots // TILE,)),
        ],
    )
    sent, gain_term, grad_pre, grad_output, hidden, mesh_picked = call(
        edge_kernel,
        "edges",
        [in_smem()] + [in_vmem()] * 10,
        [
            matrix((2 * width + 16, width)),
            floats((8, width)),
            pltpu.VMEM((slots, width), jnp.bfloat16),
        ]
        + [matrix((slots, width))] * 3,
        (
            scalars,
            receivers,
            partial,
            grid_picked,
            edge,
            stack_before,
            stacked,
            stack_after,
            w_first,
            w_second,
            gain,
        ),
        7 * unit,
    )
    got = swapped(sent)
    (kept,) = call(
        kept_kernel,
        "kept",
        [in_smem()] + [in_vmem()] * 6,
        [floats((2 * width, width))],
        (scalars, edge, grid_picked, mesh_picked, hidden, grad_pre, grad_output),
        2 * unit,
    )
    part = 2 * width // group * width // LANES
    extra = 2 * width // LANES
    packed, done = call(
        pack_kernel,
        "pack",
        [in_vmem()] * 3,
        [matrix((group, part + extra, LANES)), floats((8, LANES))],
        (kept, got, gain_term),
        0,
    )
    edge_grad, grid_grad, mesh_own, to_below, to_above = call(
        node_kernel,
        "nodes",
        [in_smem()] + [in_vmem()] * 4 + [anywhere()],
        [
            matrix((slots, width)),
            matrix((rows_grid, width)),
            floats((rows_mesh, width)),
            matrix((rows_mesh, width)),
            matrix((rows_mesh, width)),
        ],
        (scalars, senders, receivers, grad_pre, w_first, done),
        4 * unit,
    )
    from_above = passed_along(to_below, -1).astype(jnp.float32)
    from_below = passed_along(to_above, 1).astype(jnp.float32)
    mesh_grad = mesh_own + from_above + from_below
    shares = lax.all_to_all(packed, GROUP, 0, 0)
    (copies,) = call(
        group_sum_kernel,
        "group_sum",
        [in_vmem(), anywhere()],
        [matrix((groups, part + extra, LANES))],
        (shares, mesh_grad),
        0,
    )
    shares = lax.all_to_all(copies, "hi", 0, 0)
    copies, gain_grad = call(
        functools.partial(whole_sum_kernel, factor),
        "whole_sum",
        [in_vmem()],
        [matrix((group, part, LANES)), floats((8, width))],
        (shares,),
        0,
    )
    total = lax.all_to_all(copies, GROUP, 0, 0)
    other = swapped(total)
    steps, height = 8, width // 2
    first_grad, second_grad = pl.pallas_call(
        final_kernel,
        grid=(steps,),
        out_shape=[floats((3 * width, width)), floats((width, width))],
        in_specs=[in_smem()] + [in_vmem()] * 2,
        out_specs=[
            pl.BlockSpec((height, width), lambda i: (jnp.minimum(i, 5), 0)),
            pl.BlockSpec((height, width), lambda i: (jnp.maximum(i - 6, 0), 0)),
        ],
        compiler_params=pltpu.CompilerParams(vmem_limit_bytes=24 * MIB),
        name="final",
    )(scalars, total, other)
    return (
        grid_grad[None],
        mesh_grad[None],
        edge_grad[None],
        first_grad,
        second_grad,
        gain_grad[0],
    )


def solution(mesh):
    bands, meshes, cores = mesh.devices.shape
    mesh = jax.sharding.Mesh(
        mesh.devices.reshape(bands, meshes // 2, 2, cores), ("band", "hi", "lo", "rep")
    )
    in_specs = (
        P("rep", SHARDS, None),
        P("rep", SHARDS, None),
        P("rep", SHARDS, None),
        P("rep", SHARDS, None),
        P(),
        P(),
        P(),
        P(SHARDS),
        P(SHARDS),
        P(SHARDS),
    )
    out_specs = (
        P("rep", SHARDS, None),
        P("rep", SHARDS, None),
        P("rep", SHARDS, None),
        P(),
        P(),
        P(),
    )
    return jax.shard_map(
        per_device, mesh=mesh, in_specs=in_specs, out_specs=out_specs, check_vma=False
    )
```

```python
import functools
import math

import jax
import jax.numpy as jnp
from jax import lax
from jax.experimental import pallas as pl
from jax.experimental.pallas import tpu as pltpu
from jax.sharding import PartitionSpec as P

NORM_EPS = 1e-05
SHARDS = ("band", "hi", "lo")
GROUP = ("band", "lo")
TILE = 256
LANES = 128
MIB = 1 << 20


def dot(left, right, left_dim=1, right_dim=0):
    return lax.dot_general(
        left,
        right,
        (((left_dim,), (right_dim,)), ((), ())),
        preferred_element_type=jnp.float32,
    )


def picks(row, width):
    edges = row.shape[1]
    column = jnp.transpose(jnp.broadcast_to(row, (LANES, edges)))
    lane = lax.broadcasted_iota(jnp.int32, (edges, LANES), 1)
    return jnp.concatenate(
        [(column == lane + start).astype(jnp.float32).astype(jnp.bfloat16) for start in range(0, width, LANES)],
        axis=1,
    )


def spreads(row, width):
    edges = row.shape[1]
    place = lax.broadcasted_iota(jnp.int32, (width, edges), 0)
    return (place == row).astype(jnp.float32).astype(jnp.bfloat16)


def upper_lower(value):
    upper = value.astype(jnp.bfloat16)
    return upper, (value - upper.astype(jnp.float32)).astype(jnp.bfloat16)


def gain_rows(gain, lanes):
    terms = [term.astype(jnp.float32) for term in upper_lower(gain)]
    count = gain.shape[1] // lanes
    return jnp.concatenate(
        [term[:, g * lanes : (g + 1) * lanes] for term in terms for g in range(count)], axis=0
    )


def gain_of(rows):
    count = rows.shape[0] // 2
    return jnp.concatenate([rows[g : g + 1] + rows[count + g : count + g + 1] for g in range(count)], axis=1)


def narrow(rows):
    return jnp.concatenate(
        [rows[:, g : g + LANES] for g in range(0, rows.shape[1], LANES)], axis=0
    )


def anywhere():
    return pl.BlockSpec(memory_space=pl.ANY)


def in_vmem():
    return pl.BlockSpec(memory_space=pltpu.VMEM)


def in_hbm():
    return pl.BlockSpec(memory_space=pltpu.HBM)


def in_smem():
    return pl.BlockSpec(memory_space=pltpu.SMEM)


def call(kernel, name, specs, outs, operands, flops, scratch=(), limit=24 * MIB):
    operands = [
        pltpu.with_memory_space_constraint(o, pltpu.HBM) if spec.memory_space == pltpu.HBM else o
        for o, spec in zip(operands, specs)
    ]
    size = sum(math.prod(o.shape) * jnp.dtype(o.dtype).itemsize for o in outs)
    size += sum(math.prod(o.shape) * jnp.dtype(o.dtype).itemsize for o in operands)
    return pl.pallas_call(
        kernel,
        out_shape=outs,
        in_specs=specs,
        out_specs=[in_vmem()] * len(outs),
        scratch_shapes=list(scratch),
        compiler_params=pltpu.CompilerParams(vmem_limit_bytes=limit),
        cost_estimate=pl.CostEstimate(flops=int(flops), bytes_accessed=size, transcendentals=0),
        name=name,
    )(*operands)


def stack_kernel(mesh, cot, stacked, sems):
    rows = mesh.shape[0]
    copies = [
        pltpu.make_async_copy(mesh, stacked.at[pl.ds(0, rows)], sems.at[0]),
        pltpu.make_async_copy(cot, stacked.at[pl.ds(rows, rows)], sems.at[1]),
    ]
    for copy in copies:
        copy.start()
    for copy in copies:
        copy.wait()


def near_kernel(
    scalars,
    senders,
    grid,
    edge,
    w_first,
    w_second,
    partial,
    grid_picked,
    edge_here,
    w_first_here,
    w_second_here,
    senders_here,
    grid_here,
    sems,
):
    rows_grid, width = grid.shape
    tiles = range(0, edge.shape[0], TILE)
    pairs = [(senders, senders_here), (grid, grid_here)]
    for first in (width, 0):
        rows = pl.ds(first, width)
        pairs.append((w_first.at[rows], w_first_here.at[rows]))
    for start in tiles:
        rows = pl.ds(start, TILE)
        pairs.append((edge.at[rows], edge_here.at[rows]))
    rows = pl.ds(2 * width, width)
    pairs += [(w_first.at[rows], w_first_here.at[rows]), (w_second, w_second_here)]
    copies = [
        pltpu.make_async_copy(source, target, sems.at[place])
        for place, (source, target) in enumerate(pairs)
    ]
    for copy in copies:
        copy.start()
    for copy in copies[:4]:
        copy.wait()
    for start, copy in zip(tiles, copies[4:]):
        rows = pl.ds(start, TILE)
        table = picks(senders_here[:, rows] - scalars[0], rows_grid)
        picked = dot(table, grid_here[...]).astype(jnp.bfloat16)
        grid_picked[rows, :] = picked
        copy.wait()
        partial[rows, :] = dot(edge_here[rows, :], w_first_here[0:width, :]) + dot(
            picked, w_first_here[width : 2 * width, :]
        )
    for copy in copies[-2:]:
        copy.wait()


def live_receivers(scalars, receivers, start):
    row = receivers[:, pl.ds(start, TILE)] - scalars[1]
    slot = start + lax.broadcasted_iota(jnp.int32, (1, TILE), 1)
    return jnp.where(slot < scalars[2], row, -1)


def edge_kernel(
    scalars,
    receivers,
    partial,
    grid_picked,
    edge,
    stack_before,
    stack_own,
    stack_after,
    w_first,
    w_second,
    norm_gain,
    sent,
    gain_term,
    grad_pre,
    grad_output,
    hidden,
    mesh_picked,
):
    width = w_second.shape[0]
    rows_mesh = stack_own.shape[0] // 2
    gain_sum = jnp.zeros((1, width), jnp.float32)
    for start in range(0, edge.shape[0], TILE):
        rows = pl.ds(start, TILE)
        table = picks(live_receivers(scalars, receivers, start), 3 * rows_mesh)

        def picked_rows(first):
            part = pl.ds(first, rows_mesh)
            near = jnp.concatenate([stack_before[part, :], stack_own[part, :], stack_after[part, :]], axis=0)
            return dot(table, near)

        latents = picked_rows(0).astype(jnp.bfloat16)
        upstream = picked_rows(rows_mesh)
        mesh_picked[rows, :] = latents
        pre_act = partial[rows, :] + dot(latents, w_first[2 * width : 3 * width, :])
        sigmoid = jax.nn.sigmoid(pre_act)
        hid = (pre_act * sigmoid).astype(jnp.bfloat16)
        hidden[rows, :] = hid
        output = dot(hid, w_second[...])
        centered = output - jnp.mean(output, axis=1, keepdims=True)
        inverse = lax.rsqrt(jnp.mean(centered * centered, axis=1, keepdims=True) + NORM_EPS)
        normed = centered * inverse
        gain_sum = gain_sum + jnp.sum(upstream * normed, axis=0, keepdims=True)
        scaled = upstream * norm_gain[...]
        grad_out = (
            inverse
            * (
                scaled
                - jnp.mean(scaled, axis=1, keepdims=True)
                - normed * jnp.mean(scaled * normed, axis=1, keepdims=True)
            )
        ).astype(jnp.bfloat16)
        grad_output[rows, :] = grad_out
        grad_hidden = dot(grad_out, w_second[...], 1, 1)
        grad_pre[rows, :] = (grad_hidden * sigmoid * (1.0 + pre_act * (1.0 - sigmoid))).astype(
            jnp.bfloat16
        )
    gain_term[...] = jnp.broadcast_to(gain_sum, gain_term.shape)
    sent[2 * width : 2 * width + 16, :] = jnp.concatenate(
        [gain_rows(gain_sum, width), jnp.zeros((14, width), jnp.float32)], axis=0
    ).astype(jnp.bfloat16)

    @pl.when(scalars[3] == 0)
    def _():
        sent[0:width, :] = dot(mesh_picked[...], grad_pre[...], 0, 0).astype(jnp.bfloat16)
        sent[width : 2 * width, :] = dot(hidden[...], grad_output[...], 0, 0).astype(jnp.bfloat16)

    @pl.when(scalars[3] != 0)
    def _():
        sent[0:width, :] = dot(edge[...], grad_pre[...], 0, 0).astype(jnp.bfloat16)
        sent[width : 2 * width, :] = dot(grid_picked[...], grad_pre[...], 0, 0).astype(jnp.bfloat16)


def kept_kernel(scalars, edge, grid_picked, mesh_picked, hidden, grad_pre, grad_output, kept):
    width = grad_pre.shape[1]

    @pl.when(scalars[3] != 0)
    def _():
        kept[0:width, :] = dot(mesh_picked[...], grad_pre[...], 0, 0)
        kept[width : 2 * width, :] = dot(hidden[...], grad_output[...], 0, 0)

    @pl.when(scalars[3] == 0)
    def _():
        kept[0:width, :] = dot(edge[...], grad_pre[...], 0, 0)
        kept[width : 2 * width, :] = dot(grid_picked[...], grad_pre[...], 0, 0)


def pack_kernel(kept, got, gain_term, packed, done):
    count = packed.shape[0]
    half, width = kept.shape
    part = half // count
    tail = got[half : half + 16, :].astype(jnp.float32)
    gain = gain_rows(gain_term[0:1, :] + gain_of(tail[0:2]), LANES)
    for place in range(count):
        rows = pl.ds(place * part, part)
        data = narrow(kept[rows, :] + got[rows, :].astype(jnp.float32))
        packed[place] = jnp.concatenate([data, gain], axis=0).astype(jnp.bfloat16)
    done[...] = jnp.zeros(done.shape, jnp.float32)


def group_sum_kernel(shares, after, copies):
    total = shares[0].astype(jnp.float32)
    for place in range(1, shares.shape[0]):
        total = total + shares[place].astype(jnp.float32)
    data = total.shape[0] - 8
    gain = gain_rows(gain_of(total[data:]), LANES)
    row = jnp.concatenate([total[:data], gain], axis=0).astype(jnp.bfloat16)
    for place in range(copies.shape[0]):
        copies[place] = row


def whole_sum_kernel(factor, shares, after, copies, gain_grad):
    total = shares[0].astype(jnp.float32)
    for place in range(1, shares.shape[0]):
        total = total + shares[place].astype(jnp.float32)
    total = total * factor
    data = copies.shape[1]
    gain_grad[...] = jnp.broadcast_to(gain_of(total[data:]), gain_grad.shape)
    share = total[:data].astype(jnp.bfloat16)
    for place in range(copies.shape[0]):
        copies[place] = share


def node_kernel(
    scalars,
    senders,
    receivers,
    grad_pre,
    w_first,
    after,
    edge_grad,
    grid_grad,
    mesh_own,
    to_below,
    to_above,
):
    edges, width = grad_pre.shape
    rows_grid, rows_mesh = grid_grad.shape[0], mesh_own.shape[0]

    def through(sums, first):
        upper, lower = upper_lower(sums)
        weights = w_first[first : first + width, :]
        return dot(upper, weights, 1, 1) + dot(lower, weights, 1, 1)

    near = jnp.zeros((3 * rows_mesh, width), jnp.float32)
    here = jnp.zeros((rows_grid, width), jnp.float32)
    for start in range(0, edges, TILE):
        rows = pl.ds(start, TILE)
        terms = grad_pre[rows, :]
        near = near + dot(spreads(live_receivers(scalars, receivers, start), 3 * rows_mesh), terms)
        here = here + dot(spreads(senders[:, rows] - scalars[0], rows_grid), terms)
        edge_grad[rows, :] = dot(terms, w_first[0:width, :], 1, 1).astype(jnp.bfloat16)
    mesh_terms = through(near, 2 * width)
    to_below[...] = mesh_terms[0:rows_mesh].astype(jnp.bfloat16)
    mesh_own[...] = mesh_terms[rows_mesh : 2 * rows_mesh]
    to_above[...] = mesh_terms[2 * rows_mesh : 3 * rows_mesh].astype(jnp.bfloat16)
    grid_grad[...] = through(here, width).astype(jnp.bfloat16)


def put_half(scalars, flip, shares, first, second, wide, sems):
    half, width = wide.shape
    count = shares.shape[0]
    part = half // count
    half_index = 1 - scalars[3] if flip else scalars[3]
    size = sems.shape[0]
    rows = half // size

    def each(place, act):
        source = wide.at[pl.ds(place * rows, rows)]

        @pl.when(half_index == 0)
        def _():
            act(pltpu.make_async_copy(source, first.at[pl.ds(place * rows, rows)], sems.at[place]))

        @pl.when(half_index != 0)
        def _():
            start = half + place * rows
            if start < first.shape[0]:
                target = first.at[pl.ds(start, rows)]
            else:
                target = second.at[pl.ds(start - first.shape[0], rows)]
            act(pltpu.make_async_copy(source, target, sems.at[place]))

    for place in range(size):
        for index in range(place * count // size, (place + 1) * count // size):
            share = shares[index].astype(jnp.float32)
            for g in range(width // LANES):
                wide[index * part : (index + 1) * part, g * LANES : (g + 1) * LANES] = share[
                    g * part : (g + 1) * part
                ]
        each(place, lambda copy: copy.start())
    for place in range(size):
        each(place, lambda copy: copy.wait())


def own_half_kernel(scalars, shares, first, second, wide, sems):
    put_half(scalars, False, shares, first, second, wide, sems)


def other_half_kernel(scalars, shares, first_in, second_in, first, second, wide, sems):
    put_half(scalars, True, shares, first, second, wide, sems)


def passed_along(value, steps):
    count = lax.axis_size(SHARDS)
    leading, last = (max(0, -steps), min(count, count - steps))
    return lax.ppermute(value, SHARDS, [(s, s + steps) for s in range(leading, last)])


def swapped(value):
    return lax.ppermute(value, "rep", [(0, 1), (1, 0)])


def per_device(
    grid_latent,
    mesh_latent,
    edge_latent,
    mesh_cotangent,
    w_first,
    w_second,
    norm_gain,
    senders,
    receivers,
    live_counts,
):
    width = w_second.shape[0]
    rows_grid = grid_latent.shape[1]
    rows_mesh = mesh_latent.shape[1]
    slots = senders.shape[0]
    group, groups = lax.axis_size(GROUP), lax.axis_size("hi")
    factor = 1.0 / math.sqrt(slots * group * groups * lax.axis_size("rep"))
    shard = lax.axis_index(SHARDS)
    scalars = jnp.stack(
        [
            shard * rows_grid,
            (shard - 1) * rows_mesh,
            live_counts[0],
            lax.axis_index("rep").astype(jnp.int32),
        ]
    ).astype(jnp.int32)
    senders, receivers = senders[None], receivers[None]
    gain = norm_gain[None]
    grid, mesh, edge, cot = grid_latent[0], mesh_latent[0], edge_latent[0], mesh_cotangent[0]
    matrix = functools.partial(jax.ShapeDtypeStruct, dtype=jnp.bfloat16)
    floats = functools.partial(jax.ShapeDtypeStruct, dtype=jnp.float32)
    unit = 2.0 * slots * width * width

    (stacked,) = call(
        stack_kernel,
        "stack",
        [in_hbm()] * 2,
        [matrix((2 * rows_mesh, width))],
        (mesh, cot),
        0,
        [pltpu.SemaphoreType.DMA((2,))],
    )
    stack_before, stack_after = passed_along(stacked, 1), passed_along(stacked, -1)
    partial, grid_picked, edge, w_first, w_second = call(
        near_kernel,
        "near",
        [in_smem()] + [in_hbm()] * 5,
        [
            floats((slots, width)),
            matrix((slots, width)),
            pltpu.VMEM((slots, width), jnp.bfloat16),
            pltpu.VMEM((3 * width, width), jnp.bfloat16),
            pltpu.VMEM((width, width), jnp.bfloat16),
        ],
        (scalars, senders, grid, edge, w_first, w_second),
        3 * unit,
        [
            pltpu.VMEM((1, slots), jnp.int32),
            pltpu.VMEM((rows_grid, width), jnp.bfloat16),
            pltpu.SemaphoreType.DMA((6 + slots // TILE,)),
        ],
    )
    sent, gain_term, grad_pre, grad_output, hidden, mesh_picked = call(
        edge_kernel,
        "edges",
        [in_smem()] + [in_vmem()] * 10,
        [
            matrix((2 * width + 16, width)),
            floats((8, width)),
            pltpu.VMEM((slots, width), jnp.bfloat16),
        ]
        + [matrix((slots, width))] * 3,
        (
            scalars,
            receivers,
            partial,
            grid_picked,
            edge,
            stack_before,
            stacked,
            stack_after,
            w_first,
            w_second,
            gain,
        ),
        7 * unit,
    )
    got = swapped(sent)
    (kept,) = call(
        kept_kernel,
        "kept",
        [in_smem()] + [in_vmem()] * 6,
        [floats((2 * width, width))],
        (scalars, edge, grid_picked, mesh_picked, hidden, grad_pre, grad_output),
        2 * unit,
    )
    part = 2 * width // group * width // LANES
    extra = 2 * width // LANES
    packed, done = call(
        pack_kernel,
        "pack",
        [in_vmem()] * 3,
        [matrix((group, part + extra, LANES)), floats((8, LANES))],
        (kept, got, gain_term),
        0,
    )
    edge_grad, grid_grad, mesh_own, to_below, to_above = call(
        node_kernel,
        "nodes",
        [in_smem()] + [in_vmem()] * 4 + [anywhere()],
        [
            matrix((slots, width)),
            matrix((rows_grid, width)),
            floats((rows_mesh, width)),
            matrix((rows_mesh, width)),
            matrix((rows_mesh, width)),
        ],
        (scalars, senders, receivers, grad_pre, w_first, done),
        4 * unit,
    )
    from_above = passed_along(to_below, -1).astype(jnp.float32)
    from_below = passed_along(to_above, 1).astype(jnp.float32)
    mesh_grad = mesh_own + from_above + from_below
    shares = lax.all_to_all(packed, GROUP, 0, 0)
    (copies,) = call(
        group_sum_kernel,
        "group_sum",
        [in_vmem(), anywhere()],
        [matrix((groups, part + extra, LANES))],
        (shares, mesh_own),
        0,
    )
    shares = lax.all_to_all(copies, "hi", 0, 0)
    copies, gain_grad = call(
        functools.partial(whole_sum_kernel, factor),
        "whole_sum",
        [in_vmem(), anywhere()],
        [matrix((group, part, LANES)), floats((8, width))],
        (shares, mesh_grad),
        0,
    )
    total = lax.all_to_all(copies, GROUP, 0, 0)
    other = swapped(total)
    outs = [floats((3 * width, width)), floats((width, width))]
    halves = functools.partial(
        pl.pallas_call,
        out_shape=outs,
        out_specs=[in_hbm()] * 2,
        scratch_shapes=[
            pltpu.VMEM((2 * width, width), jnp.float32),
            pltpu.SemaphoreType.DMA((8,)),
        ],
        compiler_params=pltpu.CompilerParams(vmem_limit_bytes=24 * MIB),
        cost_estimate=pl.CostEstimate(flops=0, bytes_accessed=6 * MIB, transcendentals=0),
    )
    written = halves(own_half_kernel, in_specs=[in_smem(), in_vmem()], name="own_half")(scalars, total)
    first_grad, second_grad = halves(
        other_half_kernel,
        in_specs=[in_smem(), in_vmem()] + [in_hbm()] * 2,
        input_output_aliases={2: 0, 3: 1},
        name="other_half",
    )(scalars, other, *written)
    return (
        grid_grad[None],
        mesh_grad[None],
        edge_grad[None],
        first_grad,
        second_grad,
        gain_grad[0],
    )


def solution(mesh):
    bands, meshes, cores = mesh.devices.shape
    mesh = jax.sharding.Mesh(
        mesh.devices.reshape(bands, meshes // 2, 2, cores), ("band", "hi", "lo", "rep")
    )
    in_specs = (
        P("rep", SHARDS, None),
        P("rep", SHARDS, None),
        P("rep", SHARDS, None),
        P("rep", SHARDS, None),
        P(),
        P(),
        P(),
        P(SHARDS),
        P(SHARDS),
        P(SHARDS),
    )
    out_specs = (
        P("rep", SHARDS, None),
        P("rep", SHARDS, None),
        P("rep", SHARDS, None),
        P(),
        P(),
        P(),
    )
    return jax.shard_map(
        per_device, mesh=mesh, in_specs=in_specs, out_specs=out_specs, check_vma=False
    )
```

```python
import functools
import math

import jax
import jax.numpy as jnp
from jax import lax
from jax.experimental import pallas as pl
from jax.experimental.pallas import tpu as pltpu
from jax.sharding import PartitionSpec as P

NORM_EPS = 1e-05
SHARDS = ("band", "hi", "lo")
GROUP = ("band", "lo")
TILE = 256
LANES = 128
MIB = 1 << 20


def dot(left, right, left_dim=1, right_dim=0):
    return lax.dot_general(
        left,
        right,
        (((left_dim,), (right_dim,)), ((), ())),
        preferred_element_type=jnp.float32,
    )


def picks(row, width):
    edges = row.shape[1]
    column = jnp.transpose(jnp.broadcast_to(row, (LANES, edges)))
    lane = lax.broadcasted_iota(jnp.int32, (edges, LANES), 1)
    return jnp.concatenate(
        [(column == lane + start).astype(jnp.float32).astype(jnp.bfloat16) for start in range(0, width, LANES)],
        axis=1,
    )


def spreads(row, width):
    edges = row.shape[1]
    place = lax.broadcasted_iota(jnp.int32, (width, edges), 0)
    return (place == row).astype(jnp.float32).astype(jnp.bfloat16)


def upper_lower(value):
    upper = value.astype(jnp.bfloat16)
    return upper, (value - upper.astype(jnp.float32)).astype(jnp.bfloat16)


def gain_rows(gain, lanes):
    terms = [term.astype(jnp.float32) for term in upper_lower(gain)]
    count = gain.shape[1] // lanes
    return jnp.concatenate(
        [term[:, g * lanes : (g + 1) * lanes] for term in terms for g in range(count)], axis=0
    )


def gain_of(rows):
    count = rows.shape[0] // 2
    return jnp.concatenate([rows[g : g + 1] + rows[count + g : count + g + 1] for g in range(count)], axis=1)


def narrow(rows):
    return jnp.concatenate(
        [rows[:, g : g + LANES] for g in range(0, rows.shape[1], LANES)], axis=0
    )


def anywhere():
    return pl.BlockSpec(memory_space=pl.ANY)


def in_vmem():
    return pl.BlockSpec(memory_space=pltpu.VMEM)


def in_hbm():
    return pl.BlockSpec(memory_space=pltpu.HBM)


def in_smem():
    return pl.BlockSpec(memory_space=pltpu.SMEM)


def call(kernel, name, specs, outs, operands, flops, scratch=(), limit=24 * MIB):
    operands = [
        pltpu.with_memory_space_constraint(o, pltpu.HBM) if spec.memory_space == pltpu.HBM else o
        for o, spec in zip(operands, specs)
    ]
    size = sum(math.prod(o.shape) * jnp.dtype(o.dtype).itemsize for o in outs)
    size += sum(math.prod(o.shape) * jnp.dtype(o.dtype).itemsize for o in operands)
    return pl.pallas_call(
        kernel,
        out_shape=outs,
        in_specs=specs,
        out_specs=[in_vmem()] * len(outs),
        scratch_shapes=list(scratch),
        compiler_params=pltpu.CompilerParams(vmem_limit_bytes=limit),
        cost_estimate=pl.CostEstimate(flops=int(flops), bytes_accessed=size, transcendentals=0),
        name=name,
    )(*operands)


def stack_kernel(mesh, cot, stacked, sems):
    rows = mesh.shape[0]
    copies = [
        pltpu.make_async_copy(mesh, stacked.at[pl.ds(0, rows)], sems.at[0]),
        pltpu.make_async_copy(cot, stacked.at[pl.ds(rows, rows)], sems.at[1]),
    ]
    for copy in copies:
        copy.start()
    for copy in copies:
        copy.wait()


def near_kernel(
    scalars,
    senders,
    grid,
    edge,
    w_first,
    w_second,
    partial,
    grid_picked,
    edge_here,
    w_first_here,
    w_second_here,
    senders_here,
    grid_here,
    sems,
):
    rows_grid, width = grid.shape
    tiles = range(0, edge.shape[0], TILE)
    pairs = [(senders, senders_here), (grid, grid_here)]
    for first in (width, 0):
        rows = pl.ds(first, width)
        pairs.append((w_first.at[rows], w_first_here.at[rows]))
    for start in tiles:
        rows = pl.ds(start, TILE)
        pairs.append((edge.at[rows], edge_here.at[rows]))
    rows = pl.ds(2 * width, width)
    pairs += [(w_first.at[rows], w_first_here.at[rows]), (w_second, w_second_here)]
    copies = [
        pltpu.make_async_copy(source, target, sems.at[place])
        for place, (source, target) in enumerate(pairs)
    ]
    for copy in copies:
        copy.start()
    for copy in copies[:4]:
        copy.wait()
    for start, copy in zip(tiles, copies[4:]):
        rows = pl.ds(start, TILE)
        table = picks(senders_here[:, rows] - scalars[0], rows_grid)
        picked = dot(table, grid_here[...]).astype(jnp.bfloat16)
        grid_picked[rows, :] = picked
        copy.wait()
        partial[rows, :] = dot(edge_here[rows, :], w_first_here[0:width, :]) + dot(
            picked, w_first_here[width : 2 * width, :]
        )
    for copy in copies[-2:]:
        copy.wait()


def live_receivers(scalars, receivers, start, rows_mesh):
    row = receivers[:, pl.ds(start, TILE)] - scalars[1]
    row = jnp.where(
        row < rows_mesh,
        row + scalars[4],
        jnp.where(row >= 2 * rows_mesh, row - scalars[4], row),
    )
    slot = start + lax.broadcasted_iota(jnp.int32, (1, TILE), 1)
    return jnp.where(slot < scalars[2], row, -1)


def edge_kernel(
    scalars,
    receivers,
    partial,
    grid_picked,
    edge,
    stack_first,
    stack_own,
    stack_second,
    w_first,
    w_second,
    norm_gain,
    sent,
    gain_term,
    grad_pre,
    grad_output,
    hidden,
    mesh_picked,
):
    width = w_second.shape[0]
    rows_mesh = stack_own.shape[0] // 2
    gain_sum = jnp.zeros((1, width), jnp.float32)
    for start in range(0, edge.shape[0], TILE):
        rows = pl.ds(start, TILE)
        table = picks(live_receivers(scalars, receivers, start, rows_mesh), 3 * rows_mesh)

        def picked_rows(first):
            part = pl.ds(first, rows_mesh)
            near = jnp.concatenate([stack_first[part, :], stack_own[part, :], stack_second[part, :]], axis=0)
            return dot(table, near)

        latents = picked_rows(0).astype(jnp.bfloat16)
        upstream = picked_rows(rows_mesh)
        mesh_picked[rows, :] = latents
        pre_act = partial[rows, :] + dot(latents, w_first[2 * width : 3 * width, :])
        sigmoid = 0.5 * jnp.tanh(0.5 * pre_act) + 0.5
        hid = (pre_act * sigmoid).astype(jnp.bfloat16)
        hidden[rows, :] = hid
        output = dot(hid, w_second[...])
        centered = output - jnp.mean(output, axis=1, keepdims=True)
        inverse = lax.rsqrt(jnp.mean(centered * centered, axis=1, keepdims=True) + NORM_EPS)
        normed = centered * inverse
        gain_sum = gain_sum + jnp.sum(upstream * normed, axis=0, keepdims=True)
        scaled = upstream * norm_gain[...]
        grad_out = (
            inverse
            * (
                scaled
                - jnp.mean(scaled, axis=1, keepdims=True)
                - normed * jnp.mean(scaled * normed, axis=1, keepdims=True)
            )
        ).astype(jnp.bfloat16)
        grad_output[rows, :] = grad_out
        grad_hidden = dot(grad_out, w_second[...], 1, 1)
        grad_pre[rows, :] = (grad_hidden * sigmoid * (1.0 + pre_act * (1.0 - sigmoid))).astype(
            jnp.bfloat16
        )
    gain_term[...] = jnp.broadcast_to(gain_sum, gain_term.shape)
    sent[2 * width : 2 * width + 16, :] = jnp.concatenate(
        [gain_rows(gain_sum, width), jnp.zeros((14, width), jnp.float32)], axis=0
    ).astype(jnp.bfloat16)

    @pl.when(scalars[3] == 0)
    def _():
        sent[0:width, :] = dot(mesh_picked[...], grad_pre[...], 0, 0).astype(jnp.bfloat16)
        sent[width : 2 * width, :] = dot(hidden[...], grad_output[...], 0, 0).astype(jnp.bfloat16)

    @pl.when(scalars[3] != 0)
    def _():
        sent[0:width, :] = dot(edge[...], grad_pre[...], 0, 0).astype(jnp.bfloat16)
        sent[width : 2 * width, :] = dot(grid_picked[...], grad_pre[...], 0, 0).astype(jnp.bfloat16)


def kept_kernel(scalars, edge, grid_picked, mesh_picked, hidden, grad_pre, grad_output, kept):
    width = grad_pre.shape[1]

    @pl.when(scalars[3] != 0)
    def _():
        kept[0:width, :] = dot(mesh_picked[...], grad_pre[...], 0, 0)
        kept[width : 2 * width, :] = dot(hidden[...], grad_output[...], 0, 0)

    @pl.when(scalars[3] == 0)
    def _():
        kept[0:width, :] = dot(edge[...], grad_pre[...], 0, 0)
        kept[width : 2 * width, :] = dot(grid_picked[...], grad_pre[...], 0, 0)


def pack_kernel(kept, got, gain_term, packed, done):
    count = packed.shape[0]
    half, width = kept.shape
    part = half // count
    tail = got[half : half + 16, :].astype(jnp.float32)
    gain = gain_rows(gain_term[0:1, :] + gain_of(tail[0:2]), LANES)
    for place in range(count):
        rows = pl.ds(place * part, part)
        data = narrow(kept[rows, :] + got[rows, :].astype(jnp.float32))
        packed[place] = jnp.concatenate([data, gain], axis=0).astype(jnp.bfloat16)
    done[...] = jnp.zeros(done.shape, jnp.float32)


def group_sum_kernel(shares, after, copies):
    total = shares[0].astype(jnp.float32)
    for place in range(1, shares.shape[0]):
        total = total + shares[place].astype(jnp.float32)
    data = total.shape[0] - 8
    gain = gain_rows(gain_of(total[data:]), LANES)
    row = jnp.concatenate([total[:data], gain], axis=0).astype(jnp.bfloat16)
    for place in range(copies.shape[0]):
        copies[place] = row


def whole_sum_kernel(factor, shares, after, copies, gain_grad):
    total = shares[0].astype(jnp.float32)
    for place in range(1, shares.shape[0]):
        total = total + shares[place].astype(jnp.float32)
    total = total * factor
    data = copies.shape[1]
    gain_grad[...] = jnp.broadcast_to(gain_of(total[data:]), gain_grad.shape)
    share = total[:data].astype(jnp.bfloat16)
    for place in range(copies.shape[0]):
        copies[place] = share


def node_kernel(
    scalars,
    senders,
    receivers,
    grad_pre,
    w_first,
    after,
    edge_grad,
    grid_grad,
    mesh_own,
    to_first,
    to_second,
):
    edges, width = grad_pre.shape
    rows_grid, rows_mesh = grid_grad.shape[0], mesh_own.shape[0]

    def through(sums, first):
        upper, lower = upper_lower(sums)
        weights = w_first[first : first + width, :]
        return dot(upper, weights, 1, 1) + dot(lower, weights, 1, 1)

    near = jnp.zeros((3 * rows_mesh, width), jnp.float32)
    here = jnp.zeros((rows_grid, width), jnp.float32)
    for start in range(0, edges, TILE):
        rows = pl.ds(start, TILE)
        terms = grad_pre[rows, :]
        near = near + dot(
            spreads(live_receivers(scalars, receivers, start, rows_mesh), 3 * rows_mesh), terms
        )
        here = here + dot(spreads(senders[:, rows] - scalars[0], rows_grid), terms)
        edge_grad[rows, :] = dot(terms, w_first[0:width, :], 1, 1).astype(jnp.bfloat16)
    mesh_terms = through(near, 2 * width)
    to_first[...] = mesh_terms[0:rows_mesh].astype(jnp.bfloat16)
    mesh_own[...] = mesh_terms[rows_mesh : 2 * rows_mesh]
    to_second[...] = mesh_terms[2 * rows_mesh : 3 * rows_mesh].astype(jnp.bfloat16)
    grid_grad[...] = through(here, width).astype(jnp.bfloat16)


def put_half(scalars, flip, shares, first, second, wide, sems):
    half, width = wide.shape
    count = shares.shape[0]
    part = half // count
    half_index = 1 - scalars[3] if flip else scalars[3]
    size = sems.shape[0]
    rows = half // size

    def each(place, act):
        source = wide.at[pl.ds(place * rows, rows)]

        @pl.when(half_index == 0)
        def _():
            act(pltpu.make_async_copy(source, first.at[pl.ds(place * rows, rows)], sems.at[place]))

        @pl.when(half_index != 0)
        def _():
            start = half + place * rows
            if start < first.shape[0]:
                target = first.at[pl.ds(start, rows)]
            else:
                target = second.at[pl.ds(start - first.shape[0], rows)]
            act(pltpu.make_async_copy(source, target, sems.at[place]))

    for place in range(size):
        for index in range(place * count // size, (place + 1) * count // size):
            share = shares[index].astype(jnp.float32)
            for g in range(width // LANES):
                wide[index * part : (index + 1) * part, g * LANES : (g + 1) * LANES] = share[
                    g * part : (g + 1) * part
                ]
        each(place, lambda copy: copy.start())
    for place in range(size):
        each(place, lambda copy: copy.wait())


def own_half_kernel(scalars, shares, first, second, wide, sems):
    put_half(scalars, False, shares, first, second, wide, sems)


def other_half_kernel(scalars, shares, first_in, second_in, first, second, wide, sems):
    put_half(scalars, True, shares, first, second, wide, sems)


def exchanged(value, turn):
    count = lax.axis_size(SHARDS)
    pairs = [(s, s + 1) for s in range(turn, count - 1, 2)]
    return lax.ppermute(value, SHARDS, pairs + [(d, s) for s, d in pairs])


def swapped(value):
    return lax.ppermute(value, "rep", [(0, 1), (1, 0)])


def per_device(
    grid_latent,
    mesh_latent,
    edge_latent,
    mesh_cotangent,
    w_first,
    w_second,
    norm_gain,
    senders,
    receivers,
    live_counts,
):
    width = w_second.shape[0]
    rows_grid = grid_latent.shape[1]
    rows_mesh = mesh_latent.shape[1]
    slots = senders.shape[0]
    group, groups = lax.axis_size(GROUP), lax.axis_size("hi")
    factor = 1.0 / math.sqrt(slots * group * groups * lax.axis_size("rep"))
    shard = lax.axis_index(SHARDS)
    scalars = jnp.stack(
        [
            shard * rows_grid,
            (shard - 1) * rows_mesh,
            live_counts[0],
            lax.axis_index("rep").astype(jnp.int32),
            jnp.where(shard % 2 == 0, 2 * rows_mesh, 0),
        ]
    ).astype(jnp.int32)
    senders, receivers = senders[None], receivers[None]
    gain = norm_gain[None]
    grid, mesh, edge, cot = grid_latent[0], mesh_latent[0], edge_latent[0], mesh_cotangent[0]
    matrix = functools.partial(jax.ShapeDtypeStruct, dtype=jnp.bfloat16)
    floats = functools.partial(jax.ShapeDtypeStruct, dtype=jnp.float32)
    unit = 2.0 * slots * width * width

    (stacked,) = call(
        stack_kernel,
        "stack",
        [in_hbm()] * 2,
        [matrix((2 * rows_mesh, width))],
        (mesh, cot),
        0,
        [pltpu.SemaphoreType.DMA((2,))],
    )
    stack_first, stack_second = exchanged(stacked, 0), exchanged(stacked, 1)
    partial, grid_picked, edge, w_first, w_second = call(
        near_kernel,
        "near",
        [in_smem()] + [in_hbm()] * 5,
        [
            floats((slots, width)),
            matrix((slots, width)),
            pltpu.VMEM((slots, width), jnp.bfloat16),
            pltpu.VMEM((3 * width, width), jnp.bfloat16),
            pltpu.VMEM((width, width), jnp.bfloat16),
        ],
        (scalars, senders, grid, edge, w_first, w_second),
        3 * unit,
        [
            pltpu.VMEM((1, slots), jnp.int32),
            pltpu.VMEM((rows_grid, width), jnp.bfloat16),
            pltpu.SemaphoreType.DMA((6 + slots // TILE,)),
        ],
    )
    sent, gain_term, grad_pre, grad_output, hidden, mesh_picked = call(
        edge_kernel,
        "edges",
        [in_smem()] + [in_vmem()] * 10,
        [
            matrix((2 * width + 16, width)),
            floats((8, width)),
            pltpu.VMEM((slots, width), jnp.bfloat16),
        ]
        + [matrix((slots, width))] * 3,
        (
            scalars,
            receivers,
            partial,
            grid_picked,
            edge,
            stack_first,
            stacked,
            stack_second,
            w_first,
            w_second,
            gain,
        ),
        7 * unit,
    )
    got = swapped(sent)
    (kept,) = call(
        kept_kernel,
        "kept",
        [in_smem()] + [in_vmem()] * 6,
        [floats((2 * width, width))],
        (scalars, edge, grid_picked, mesh_picked, hidden, grad_pre, grad_output),
        2 * unit,
    )
    part = 2 * width // group * width // LANES
    extra = 2 * width // LANES
    packed, done = call(
        pack_kernel,
        "pack",
        [in_vmem()] * 3,
        [matrix((group, part + extra, LANES)), floats((8, LANES))],
        (kept, got, gain_term),
        0,
    )
    edge_grad, grid_grad, mesh_own, to_first, to_second = call(
        node_kernel,
        "nodes",
        [in_smem()] + [in_vmem()] * 4 + [anywhere()],
        [
            matrix((slots, width)),
            matrix((rows_grid, width)),
            floats((rows_mesh, width)),
            matrix((rows_mesh, width)),
            matrix((rows_mesh, width)),
        ],
        (scalars, senders, receivers, grad_pre, w_first, done),
        4 * unit,
    )
    from_first = exchanged(to_first, 0).astype(jnp.float32)
    from_second = exchanged(to_second, 1).astype(jnp.float32)
    mesh_grad = mesh_own + from_first + from_second
    shares = lax.all_to_all(packed, GROUP, 0, 0)
    (copies,) = call(
        group_sum_kernel,
        "group_sum",
        [in_vmem(), anywhere()],
        [matrix((groups, part + extra, LANES))],
        (shares, mesh_own),
        0,
    )
    shares = lax.all_to_all(copies, "hi", 0, 0)
    copies, gain_grad = call(
        functools.partial(whole_sum_kernel, factor),
        "whole_sum",
        [in_vmem(), anywhere()],
        [matrix((group, part, LANES)), floats((8, width))],
        (shares, mesh_grad),
        0,
    )
    total = lax.all_to_all(copies, GROUP, 0, 0)
    other = swapped(total)
    outs = [floats((3 * width, width)), floats((width, width))]
    halves = functools.partial(
        pl.pallas_call,
        out_shape=outs,
        out_specs=[in_hbm()] * 2,
        scratch_shapes=[
            pltpu.VMEM((2 * width, width), jnp.float32),
            pltpu.SemaphoreType.DMA((8,)),
        ],
        compiler_params=pltpu.CompilerParams(vmem_limit_bytes=24 * MIB),
        cost_estimate=pl.CostEstimate(flops=0, bytes_accessed=6 * MIB, transcendentals=0),
    )
    written = halves(own_half_kernel, in_specs=[in_smem(), in_vmem()], name="own_half")(scalars, total)
    first_grad, second_grad = halves(
        other_half_kernel,
        in_specs=[in_smem(), in_vmem()] + [in_hbm()] * 2,
        input_output_aliases={2: 0, 3: 1},
        name="other_half",
    )(scalars, other, *written)
    return (
        grid_grad[None],
        mesh_grad[None],
        edge_grad[None],
        first_grad,
        second_grad,
        gain_grad[0],
    )


def solution(mesh):
    bands, meshes, cores = mesh.devices.shape
    mesh = jax.sharding.Mesh(
        mesh.devices.reshape(bands, meshes // 2, 2, cores), ("band", "hi", "lo", "rep")
    )
    in_specs = (
        P("rep", SHARDS, None),
        P("rep", SHARDS, None),
        P("rep", SHARDS, None),
        P("rep", SHARDS, None),
        P(),
        P(),
        P(),
        P(SHARDS),
        P(SHARDS),
        P(SHARDS),
    )
    out_specs = (
        P("rep", SHARDS, None),
        P("rep", SHARDS, None),
        P("rep", SHARDS, None),
        P(),
        P(),
        P(),
    )
    return jax.shard_map(
        per_device, mesh=mesh, in_specs=in_specs, out_specs=out_specs, check_vma=False
    )
```

```python
import functools
import math

import jax
import jax.numpy as jnp
from jax import lax
from jax.experimental import pallas as pl
from jax.experimental.pallas import tpu as pltpu
from jax.sharding import PartitionSpec as P

NORM_EPS = 1e-05
SHARDS = ("band", "hi", "lo")
GROUP = ("band", "lo")
TILE = 256
LANES = 128
MIB = 1 << 20


def dot(left, right, left_dim=1, right_dim=0):
    return lax.dot_general(
        left,
        right,
        (((left_dim,), (right_dim,)), ((), ())),
        preferred_element_type=jnp.float32,
    )


def picks(row, width):
    edges = row.shape[1]
    column = jnp.transpose(jnp.broadcast_to(row, (LANES, edges)))
    lane = lax.broadcasted_iota(jnp.int32, (edges, LANES), 1)
    return jnp.concatenate(
        [(column == lane + start).astype(jnp.float32).astype(jnp.bfloat16) for start in range(0, width, LANES)],
        axis=1,
    )


def spreads(row, width):
    edges = row.shape[1]
    place = lax.broadcasted_iota(jnp.int32, (width, edges), 0)
    return (place == row).astype(jnp.float32).astype(jnp.bfloat16)


def upper_lower(value):
    upper = value.astype(jnp.bfloat16)
    return upper, (value - upper.astype(jnp.float32)).astype(jnp.bfloat16)


def gain_rows(gain, lanes):
    terms = [term.astype(jnp.float32) for term in upper_lower(gain)]
    count = gain.shape[1] // lanes
    return jnp.concatenate(
        [term[:, g * lanes : (g + 1) * lanes] for term in terms for g in range(count)], axis=0
    )


def gain_of(rows):
    count = rows.shape[0] // 2
    return jnp.concatenate([rows[g : g + 1] + rows[count + g : count + g + 1] for g in range(count)], axis=1)


def narrow(rows):
    return jnp.concatenate(
        [rows[:, g : g + LANES] for g in range(0, rows.shape[1], LANES)], axis=0
    )


def anywhere():
    return pl.BlockSpec(memory_space=pl.ANY)


def in_vmem():
    return pl.BlockSpec(memory_space=pltpu.VMEM)


def in_hbm():
    return pl.BlockSpec(memory_space=pltpu.HBM)


def in_smem():
    return pl.BlockSpec(memory_space=pltpu.SMEM)


def call(kernel, name, specs, outs, operands, flops, scratch=(), limit=24 * MIB):
    operands = [
        pltpu.with_memory_space_constraint(o, pltpu.HBM) if spec.memory_space == pltpu.HBM else o
        for o, spec in zip(operands, specs)
    ]
    size = sum(math.prod(o.shape) * jnp.dtype(o.dtype).itemsize for o in outs)
    size += sum(math.prod(o.shape) * jnp.dtype(o.dtype).itemsize for o in operands)
    return pl.pallas_call(
        kernel,
        out_shape=outs,
        in_specs=specs,
        out_specs=[in_vmem()] * len(outs),
        scratch_shapes=list(scratch),
        compiler_params=pltpu.CompilerParams(vmem_limit_bytes=limit),
        cost_estimate=pl.CostEstimate(flops=int(flops), bytes_accessed=size, transcendentals=0),
        name=name,
    )(*operands)


def stack_kernel(mesh, cot, stacked, sems):
    rows = mesh.shape[0]
    copies = [
        pltpu.make_async_copy(mesh, stacked.at[pl.ds(0, rows)], sems.at[0]),
        pltpu.make_async_copy(cot, stacked.at[pl.ds(rows, rows)], sems.at[1]),
    ]
    for copy in copies:
        copy.start()
    for copy in copies:
        copy.wait()


def near_kernel(
    scalars,
    senders,
    grid,
    edge,
    w_first,
    w_second,
    partial,
    grid_picked,
    edge_here,
    w_first_here,
    w_second_here,
    senders_here,
    grid_here,
    sems,
):
    rows_grid, width = grid.shape
    tiles = range(0, edge.shape[0], TILE)
    pairs = [(senders, senders_here), (grid, grid_here)]
    for first in (width, 0):
        rows = pl.ds(first, width)
        pairs.append((w_first.at[rows], w_first_here.at[rows]))
    for start in tiles:
        rows = pl.ds(start, TILE)
        pairs.append((edge.at[rows], edge_here.at[rows]))
    rows = pl.ds(2 * width, width)
    pairs += [(w_first.at[rows], w_first_here.at[rows]), (w_second, w_second_here)]
    copies = [
        pltpu.make_async_copy(source, target, sems.at[place])
        for place, (source, target) in enumerate(pairs)
    ]
    for copy in copies:
        copy.start()
    for copy in copies[:4]:
        copy.wait()
    for start, copy in zip(tiles, copies[4:]):
        rows = pl.ds(start, TILE)
        table = picks(senders_here[:, rows] - scalars[0], rows_grid)
        picked = dot(table, grid_here[...]).astype(jnp.bfloat16)
        grid_picked[rows, :] = picked
        copy.wait()
        partial[rows, :] = dot(edge_here[rows, :], w_first_here[0:width, :]) + dot(
            picked, w_first_here[width : 2 * width, :]
        )
    for copy in copies[-2:]:
        copy.wait()


def live_receivers(scalars, receivers, start, rows_mesh):
    row = receivers[:, pl.ds(start, TILE)] - scalars[1]
    row = jnp.where(
        row < rows_mesh,
        row + scalars[4],
        jnp.where(row >= 2 * rows_mesh, row - scalars[4], row),
    )
    slot = start + lax.broadcasted_iota(jnp.int32, (1, TILE), 1)
    return jnp.where(slot < scalars[2], row, -1)


def edge_kernel(
    scalars,
    receivers,
    partial,
    grid_picked,
    edge,
    stack_first,
    stack_own,
    stack_second,
    w_first,
    w_second,
    norm_gain,
    sent,
    gain_term,
    grad_pre,
    grad_output,
    hidden,
    mesh_picked,
):
    width = w_second.shape[0]
    rows_mesh = stack_own.shape[0] // 2
    gain_sum = jnp.zeros((1, width), jnp.float32)
    for start in range(0, edge.shape[0], TILE):
        rows = pl.ds(start, TILE)
        table = picks(live_receivers(scalars, receivers, start, rows_mesh), 3 * rows_mesh)

        def picked_rows(first):
            part = pl.ds(first, rows_mesh)
            near = jnp.concatenate([stack_first[part, :], stack_own[part, :], stack_second[part, :]], axis=0)
            return dot(table, near)

        latents = picked_rows(0).astype(jnp.bfloat16)
        upstream = picked_rows(rows_mesh)
        mesh_picked[rows, :] = latents
        pre_act = partial[rows, :] + dot(latents, w_first[2 * width : 3 * width, :])
        sigmoid = 0.5 * jnp.tanh(0.5 * pre_act) + 0.5
        hid = (pre_act * sigmoid).astype(jnp.bfloat16)
        hidden[rows, :] = hid
        output = dot(hid, w_second[...])
        centered = output - jnp.mean(output, axis=1, keepdims=True)
        inverse = lax.rsqrt(jnp.mean(centered * centered, axis=1, keepdims=True) + NORM_EPS)
        normed = centered * inverse
        gain_sum = gain_sum + jnp.sum(upstream * normed, axis=0, keepdims=True)
        scaled = upstream * norm_gain[...]
        grad_out = (
            inverse
            * (
                scaled
                - jnp.mean(scaled, axis=1, keepdims=True)
                - normed * jnp.mean(scaled * normed, axis=1, keepdims=True)
            )
        ).astype(jnp.bfloat16)
        grad_output[rows, :] = grad_out
        grad_hidden = dot(grad_out, w_second[...], 1, 1)
        grad_pre[rows, :] = (grad_hidden * sigmoid * (1.0 + pre_act * (1.0 - sigmoid))).astype(
            jnp.bfloat16
        )
    gain_term[...] = jnp.broadcast_to(gain_sum, gain_term.shape)
    sent[2 * width : 2 * width + 16, :] = jnp.concatenate(
        [gain_rows(gain_sum, width), jnp.zeros((14, width), jnp.float32)], axis=0
    ).astype(jnp.bfloat16)

    @pl.when(scalars[3] == 0)
    def _():
        sent[0:width, :] = dot(mesh_picked[...], grad_pre[...], 0, 0).astype(jnp.bfloat16)
        sent[width : 2 * width, :] = dot(hidden[...], grad_output[...], 0, 0).astype(jnp.bfloat16)

    @pl.when(scalars[3] != 0)
    def _():
        sent[0:width, :] = dot(edge[...], grad_pre[...], 0, 0).astype(jnp.bfloat16)
        sent[width : 2 * width, :] = dot(grid_picked[...], grad_pre[...], 0, 0).astype(jnp.bfloat16)


def kept_kernel(scalars, edge, grid_picked, mesh_picked, hidden, grad_pre, grad_output, kept):
    width = grad_pre.shape[1]

    @pl.when(scalars[3] != 0)
    def _():
        kept[0:width, :] = dot(mesh_picked[...], grad_pre[...], 0, 0)
        kept[width : 2 * width, :] = dot(hidden[...], grad_output[...], 0, 0)

    @pl.when(scalars[3] == 0)
    def _():
        kept[0:width, :] = dot(edge[...], grad_pre[...], 0, 0)
        kept[width : 2 * width, :] = dot(grid_picked[...], grad_pre[...], 0, 0)


def pack_kernel(kept, got, gain_term, packed, done):
    count = packed.shape[0]
    half, width = kept.shape
    part = half // count
    tail = got[half : half + 16, :].astype(jnp.float32)
    gain = gain_rows(gain_term[0:1, :] + gain_of(tail[0:2]), LANES)
    for place in range(count):
        rows = pl.ds(place * part, part)
        data = narrow(kept[rows, :] + got[rows, :].astype(jnp.float32))
        packed[place] = jnp.concatenate([data, gain], axis=0).astype(jnp.bfloat16)
    done[...] = jnp.zeros(done.shape, jnp.float32)


def group_sum_kernel(shares, after, packed):
    total = shares[0].astype(jnp.float32)
    for place in range(1, shares.shape[0]):
        total = total + shares[place].astype(jnp.float32)
    data = total.shape[0] - 8
    gain = gain_rows(gain_of(total[data:]), LANES)
    packed[...] = jnp.concatenate([total[:data], gain], axis=0).astype(jnp.bfloat16)


def whole_sum_kernel(factor, own, ahead, across, behind, after, copies, gain_grad):
    own, ahead, across, behind = [part[...].astype(jnp.float32) for part in (own, ahead, across, behind)]
    total = ((own + across) + (ahead + behind)) * factor
    data = copies.shape[1]
    gain_grad[...] = jnp.broadcast_to(gain_of(total[data:]), gain_grad.shape)
    share = total[:data].astype(jnp.bfloat16)
    for place in range(copies.shape[0]):
        copies[place] = share


def node_kernel(
    scalars,
    senders,
    receivers,
    grad_pre,
    w_first,
    after,
    edge_grad,
    grid_grad,
    mesh_own,
    to_first,
    to_second,
):
    edges, width = grad_pre.shape
    rows_grid, rows_mesh = grid_grad.shape[0], mesh_own.shape[0]

    def through(sums, first):
        upper, lower = upper_lower(sums)
        weights = w_first[first : first + width, :]
        return dot(upper, weights, 1, 1) + dot(lower, weights, 1, 1)

    near = jnp.zeros((3 * rows_mesh, width), jnp.float32)
    here = jnp.zeros((rows_grid, width), jnp.float32)
    for start in range(0, edges, TILE):
        rows = pl.ds(start, TILE)
        terms = grad_pre[rows, :]
        near = near + dot(
            spreads(live_receivers(scalars, receivers, start, rows_mesh), 3 * rows_mesh), terms
        )
        here = here + dot(spreads(senders[:, rows] - scalars[0], rows_grid), terms)
        edge_grad[rows, :] = dot(terms, w_first[0:width, :], 1, 1).astype(jnp.bfloat16)
    mesh_terms = through(near, 2 * width)
    to_first[...] = mesh_terms[0:rows_mesh].astype(jnp.bfloat16)
    mesh_own[...] = mesh_terms[rows_mesh : 2 * rows_mesh]
    to_second[...] = mesh_terms[2 * rows_mesh : 3 * rows_mesh].astype(jnp.bfloat16)
    grid_grad[...] = through(here, width).astype(jnp.bfloat16)


def put_half(scalars, flip, shares, first, second, wide, sems):
    half, width = wide.shape
    count = shares.shape[0]
    part = half // count
    half_index = 1 - scalars[3] if flip else scalars[3]
    size = sems.shape[0]
    rows = half // size

    def each(place, act):
        source = wide.at[pl.ds(place * rows, rows)]

        @pl.when(half_index == 0)
        def _():
            act(pltpu.make_async_copy(source, first.at[pl.ds(place * rows, rows)], sems.at[place]))

        @pl.when(half_index != 0)
        def _():
            start = half + place * rows
            if start < first.shape[0]:
                target = first.at[pl.ds(start, rows)]
            else:
                target = second.at[pl.ds(start - first.shape[0], rows)]
            act(pltpu.make_async_copy(source, target, sems.at[place]))

    for place in range(size):
        for index in range(place * count // size, (place + 1) * count // size):
            share = shares[index].astype(jnp.float32)
            for g in range(width // LANES):
                wide[index * part : (index + 1) * part, g * LANES : (g + 1) * LANES] = share[
                    g * part : (g + 1) * part
                ]
        each(place, lambda copy: copy.start())
    for place in range(size):
        each(place, lambda copy: copy.wait())


def own_half_kernel(scalars, shares, first, second, wide, sems):
    put_half(scalars, False, shares, first, second, wide, sems)


def other_half_kernel(scalars, shares, first_in, second_in, first, second, wide, sems):
    put_half(scalars, True, shares, first, second, wide, sems)


def exchanged(value, turn):
    count = lax.axis_size(SHARDS)
    pairs = [(s, s + 1) for s in range(turn, count - 1, 2)]
    return lax.ppermute(value, SHARDS, pairs + [(d, s) for s, d in pairs])


def swapped(value):
    return lax.ppermute(value, "rep", [(0, 1), (1, 0)])


def per_device(
    grid_latent,
    mesh_latent,
    edge_latent,
    mesh_cotangent,
    w_first,
    w_second,
    norm_gain,
    senders,
    receivers,
    live_counts,
):
    width = w_second.shape[0]
    rows_grid = grid_latent.shape[1]
    rows_mesh = mesh_latent.shape[1]
    slots = senders.shape[0]
    group, groups = lax.axis_size(GROUP), lax.axis_size("hi")
    factor = 1.0 / math.sqrt(slots * group * groups * lax.axis_size("rep"))
    shard = lax.axis_index(SHARDS)
    scalars = jnp.stack(
        [
            shard * rows_grid,
            (shard - 1) * rows_mesh,
            live_counts[0],
            lax.axis_index("rep").astype(jnp.int32),
            jnp.where(shard % 2 == 0, 2 * rows_mesh, 0),
        ]
    ).astype(jnp.int32)
    senders, receivers = senders[None], receivers[None]
    gain = norm_gain[None]
    grid, mesh, edge, cot = grid_latent[0], mesh_latent[0], edge_latent[0], mesh_cotangent[0]
    matrix = functools.partial(jax.ShapeDtypeStruct, dtype=jnp.bfloat16)
    floats = functools.partial(jax.ShapeDtypeStruct, dtype=jnp.float32)
    unit = 2.0 * slots * width * width

    (stacked,) = call(
        stack_kernel,
        "stack",
        [in_hbm()] * 2,
        [matrix((2 * rows_mesh, width))],
        (mesh, cot),
        0,
        [pltpu.SemaphoreType.DMA((2,))],
    )
    stack_first, stack_second = exchanged(stacked, 0), exchanged(stacked, 1)
    partial, grid_picked, edge, w_first, w_second = call(
        near_kernel,
        "near",
        [in_smem()] + [in_hbm()] * 5,
        [
            floats((slots, width)),
            matrix((slots, width)),
            pltpu.VMEM((slots, width), jnp.bfloat16),
            pltpu.VMEM((3 * width, width), jnp.bfloat16),
            pltpu.VMEM((width, width), jnp.bfloat16),
        ],
        (scalars, senders, grid, edge, w_first, w_second),
        3 * unit,
        [
            pltpu.VMEM((1, slots), jnp.int32),
            pltpu.VMEM((rows_grid, width), jnp.bfloat16),
            pltpu.SemaphoreType.DMA((6 + slots // TILE,)),
        ],
    )
    sent, gain_term, grad_pre, grad_output, hidden, mesh_picked = call(
        edge_kernel,
        "edges",
        [in_smem()] + [in_vmem()] * 10,
        [
            matrix((2 * width + 16, width)),
            floats((8, width)),
            pltpu.VMEM((slots, width), jnp.bfloat16),
        ]
        + [matrix((slots, width))] * 3,
        (
            scalars,
            receivers,
            partial,
            grid_picked,
            edge,
            stack_first,
            stacked,
            stack_second,
            w_first,
            w_second,
            gain,
        ),
        7 * unit,
    )
    got = swapped(sent)
    (kept,) = call(
        kept_kernel,
        "kept",
        [in_smem()] + [in_vmem()] * 6,
        [floats((2 * width, width))],
        (scalars, edge, grid_picked, mesh_picked, hidden, grad_pre, grad_output),
        2 * unit,
    )
    part = 2 * width // group * width // LANES
    extra = 2 * width // LANES
    packed, done = call(
        pack_kernel,
        "pack",
        [in_vmem()] * 3,
        [matrix((group, part + extra, LANES)), floats((8, LANES))],
        (kept, got, gain_term),
        0,
    )
    edge_grad, grid_grad, mesh_own, to_first, to_second = call(
        node_kernel,
        "nodes",
        [in_smem()] + [in_vmem()] * 4 + [anywhere()],
        [
            matrix((slots, width)),
            matrix((rows_grid, width)),
            floats((rows_mesh, width)),
            matrix((rows_mesh, width)),
            matrix((rows_mesh, width)),
        ],
        (scalars, senders, receivers, grad_pre, w_first, done),
        4 * unit,
    )
    from_first = exchanged(to_first, 0).astype(jnp.float32)
    from_second = exchanged(to_second, 1).astype(jnp.float32)
    mesh_grad = mesh_own + from_first + from_second
    shares = lax.all_to_all(packed, GROUP, 0, 0)
    (packed,) = call(
        group_sum_kernel,
        "group_sum",
        [in_vmem(), anywhere()],
        [matrix((part + extra, LANES))],
        (shares, mesh_own),
        0,
    )
    turns = [
        lax.ppermute(packed, "hi", [(i, (i + turn) % groups) for i in range(groups)])
        for turn in (1, 2, 3)
    ]
    copies, gain_grad = call(
        functools.partial(whole_sum_kernel, factor),
        "whole_sum",
        [in_vmem()] * 4 + [anywhere()],
        [matrix((group, part, LANES)), floats((8, width))],
        (packed, *turns, mesh_grad),
        0,
    )
    total = lax.all_to_all(copies, GROUP, 0, 0)
    other = swapped(total)
    outs = [floats((3 * width, width)), floats((width, width))]
    halves = functools.partial(
        pl.pallas_call,
        out_shape=outs,
        out_specs=[in_hbm()] * 2,
        scratch_shapes=[
            pltpu.VMEM((2 * width, width), jnp.float32),
            pltpu.SemaphoreType.DMA((8,)),
        ],
        compiler_params=pltpu.CompilerParams(vmem_limit_bytes=24 * MIB),
        cost_estimate=pl.CostEstimate(flops=0, bytes_accessed=6 * MIB, transcendentals=0),
    )
    written = halves(own_half_kernel, in_specs=[in_smem(), in_vmem()], name="own_half")(scalars, total)
    first_grad, second_grad = halves(
        other_half_kernel,
        in_specs=[in_smem(), in_vmem()] + [in_hbm()] * 2,
        input_output_aliases={2: 0, 3: 1},
        name="other_half",
    )(scalars, other, *written)
    return (
        grid_grad[None],
        mesh_grad[None],
        edge_grad[None],
        first_grad,
        second_grad,
        gain_grad[0],
    )


def solution(mesh):
    bands, meshes, cores = mesh.devices.shape
    mesh = jax.sharding.Mesh(
        mesh.devices.reshape(bands, 4, meshes // 4, cores), ("band", "hi", "lo", "rep")
    )
    in_specs = (
        P("rep", SHARDS, None),
        P("rep", SHARDS, None),
        P("rep", SHARDS, None),
        P("rep", SHARDS, None),
        P(),
        P(),
        P(),
        P(SHARDS),
        P(SHARDS),
        P(SHARDS),
    )
    out_specs = (
        P("rep", SHARDS, None),
        P("rep", SHARDS, None),
        P("rep", SHARDS, None),
        P(),
        P(),
        P(),
    )
    return jax.shard_map(
        per_device, mesh=mesh, in_specs=in_specs, out_specs=out_specs, check_vma=False
    )
```

```python
import functools
import math

import jax
import jax.numpy as jnp
from jax import lax
from jax.experimental import pallas as pl
from jax.experimental.pallas import tpu as pltpu
from jax.sharding import PartitionSpec as P

NORM_EPS = 1e-05
SHARDS = ("band", "hi", "lo")
GROUP = ("band", "lo")
TILE = 256
LANES = 128
MIB = 1 << 20


def dot(left, right, left_dim=1, right_dim=0):
    return lax.dot_general(
        left,
        right,
        (((left_dim,), (right_dim,)), ((), ())),
        preferred_element_type=jnp.float32,
    )


def picks(row, width):
    edges = row.shape[1]
    column = jnp.transpose(jnp.broadcast_to(row, (LANES, edges)))
    lane = lax.broadcasted_iota(jnp.int32, (edges, LANES), 1)
    return jnp.concatenate(
        [(column == lane + start).astype(jnp.float32).astype(jnp.bfloat16) for start in range(0, width, LANES)],
        axis=1,
    )


def spreads(row, width):
    edges = row.shape[1]
    place = lax.broadcasted_iota(jnp.int32, (width, edges), 0)
    return (place == row).astype(jnp.float32).astype(jnp.bfloat16)


def upper_lower(value):
    upper = value.astype(jnp.bfloat16)
    return upper, (value - upper.astype(jnp.float32)).astype(jnp.bfloat16)


def gain_rows(gain, lanes):
    terms = [term.astype(jnp.float32) for term in upper_lower(gain)]
    count = gain.shape[1] // lanes
    return jnp.concatenate(
        [term[:, g * lanes : (g + 1) * lanes] for term in terms for g in range(count)], axis=0
    )


def gain_of(rows):
    count = rows.shape[0] // 2
    return jnp.concatenate([rows[g : g + 1] + rows[count + g : count + g + 1] for g in range(count)], axis=1)


def narrow(rows):
    return jnp.concatenate(
        [rows[:, g : g + LANES] for g in range(0, rows.shape[1], LANES)], axis=0
    )


def anywhere():
    return pl.BlockSpec(memory_space=pl.ANY)


def in_vmem():
    return pl.BlockSpec(memory_space=pltpu.VMEM)


def in_hbm():
    return pl.BlockSpec(memory_space=pltpu.HBM)


def in_smem():
    return pl.BlockSpec(memory_space=pltpu.SMEM)


def call(kernel, name, specs, outs, operands, flops, scratch=(), limit=24 * MIB):
    operands = [
        pltpu.with_memory_space_constraint(o, pltpu.HBM) if spec.memory_space == pltpu.HBM else o
        for o, spec in zip(operands, specs)
    ]
    size = sum(math.prod(o.shape) * jnp.dtype(o.dtype).itemsize for o in outs)
    size += sum(math.prod(o.shape) * jnp.dtype(o.dtype).itemsize for o in operands)
    return pl.pallas_call(
        kernel,
        out_shape=outs,
        in_specs=specs,
        out_specs=[in_vmem()] * len(outs),
        scratch_shapes=list(scratch),
        compiler_params=pltpu.CompilerParams(vmem_limit_bytes=limit),
        cost_estimate=pl.CostEstimate(flops=int(flops), bytes_accessed=size, transcendentals=0),
        name=name,
    )(*operands)


def near_kernel(
    scalars,
    senders,
    grid,
    edge,
    w_first,
    w_second,
    partial,
    grid_picked,
    edge_here,
    w_first_here,
    w_second_here,
    senders_here,
    grid_here,
    sems,
):
    rows_grid, width = grid.shape
    tiles = range(0, edge.shape[0], TILE)
    pairs = [(senders, senders_here), (grid, grid_here)]
    for first in (width, 0):
        rows = pl.ds(first, width)
        pairs.append((w_first.at[rows], w_first_here.at[rows]))
    for start in tiles:
        rows = pl.ds(start, TILE)
        pairs.append((edge.at[rows], edge_here.at[rows]))
    rows = pl.ds(2 * width, width)
    pairs += [(w_first.at[rows], w_first_here.at[rows]), (w_second, w_second_here)]
    copies = [
        pltpu.make_async_copy(source, target, sems.at[place])
        for place, (source, target) in enumerate(pairs)
    ]
    for copy in copies:
        copy.start()
    for copy in copies[:4]:
        copy.wait()
    for start, copy in zip(tiles, copies[4:]):
        rows = pl.ds(start, TILE)
        table = picks(senders_here[:, rows] - scalars[0], rows_grid)
        picked = dot(table, grid_here[...]).astype(jnp.bfloat16)
        grid_picked[rows, :] = picked
        copy.wait()
        partial[rows, :] = dot(edge_here[rows, :], w_first_here[0:width, :]) + dot(
            picked, w_first_here[width : 2 * width, :]
        )
    for copy in copies[-2:]:
        copy.wait()


def live_receivers(scalars, receivers, start, tile, rows_mesh):
    row = receivers[:, pl.ds(start, tile)] - scalars[1]
    row = jnp.where(
        row < rows_mesh,
        row + scalars[4],
        jnp.where(row >= 2 * rows_mesh, row - scalars[4], row),
    )
    slot = start + lax.broadcasted_iota(jnp.int32, (1, tile), 1)
    return jnp.where(slot < scalars[2], row, -1)


def picked_near(scalars, receivers, first, own, second):
    rows_mesh = own.shape[0]
    table = picks(live_receivers(scalars, receivers, 0, receivers.shape[1], rows_mesh), 3 * rows_mesh)
    return dot(table, jnp.concatenate([first[...], own[...], second[...]], axis=0))


def forward_kernel(
    scalars,
    receivers,
    partial,
    mesh_first,
    mesh_own,
    mesh_second,
    w_first,
    w_second,
    pre_act,
    output,
    hidden,
    mesh_picked,
):
    width = w_second.shape[0]
    latents = picked_near(scalars, receivers, mesh_first, mesh_own, mesh_second).astype(jnp.bfloat16)
    mesh_picked[...] = latents
    pre = partial[...] + dot(latents, w_first[2 * width : 3 * width, :])
    pre_act[...] = pre
    hid = (pre * (0.5 * jnp.tanh(0.5 * pre) + 0.5)).astype(jnp.bfloat16)
    hidden[...] = hid
    output[...] = dot(hid, w_second[...])


def backward_kernel(
    scalars,
    receivers,
    cot_first,
    cot_own,
    cot_second,
    pre_act,
    output,
    hidden,
    mesh_picked,
    grid_picked,
    edge,
    w_second,
    norm_gain,
    sent,
    gain_term,
    grad_pre,
    grad_output,
):
    width = w_second.shape[0]
    upstream = picked_near(scalars, receivers, cot_first, cot_own, cot_second)
    out = output[...]
    centered = out - jnp.mean(out, axis=1, keepdims=True)
    inverse = lax.rsqrt(jnp.mean(centered * centered, axis=1, keepdims=True) + NORM_EPS)
    normed = centered * inverse
    gain_sum = jnp.sum(upstream * normed, axis=0, keepdims=True)
    scaled = upstream * norm_gain[...]
    grad_out = (
        inverse
        * (
            scaled
            - jnp.mean(scaled, axis=1, keepdims=True)
            - normed * jnp.mean(scaled * normed, axis=1, keepdims=True)
        )
    ).astype(jnp.bfloat16)
    grad_output[...] = grad_out
    grad_hidden = dot(grad_out, w_second[...], 1, 1)
    pre = pre_act[...]
    sigmoid = 0.5 * jnp.tanh(0.5 * pre) + 0.5
    grad_pre[...] = (grad_hidden * sigmoid * (1.0 + pre * (1.0 - sigmoid))).astype(jnp.bfloat16)
    gain_term[...] = jnp.broadcast_to(gain_sum, gain_term.shape)
    sent[2 * width : 2 * width + 16, :] = jnp.concatenate(
        [gain_rows(gain_sum, width), jnp.zeros((14, width), jnp.float32)], axis=0
    ).astype(jnp.bfloat16)

    @pl.when(scalars[3] == 0)
    def _():
        sent[0:width, :] = dot(mesh_picked[...], grad_pre[...], 0, 0).astype(jnp.bfloat16)
        sent[width : 2 * width, :] = dot(hidden[...], grad_output[...], 0, 0).astype(jnp.bfloat16)

    @pl.when(scalars[3] != 0)
    def _():
        sent[0:width, :] = dot(edge[...], grad_pre[...], 0, 0).astype(jnp.bfloat16)
        sent[width : 2 * width, :] = dot(grid_picked[...], grad_pre[...], 0, 0).astype(jnp.bfloat16)


def kept_kernel(scalars, edge, grid_picked, mesh_picked, hidden, grad_pre, grad_output, kept):
    width = grad_pre.shape[1]

    @pl.when(scalars[3] != 0)
    def _():
        kept[0:width, :] = dot(mesh_picked[...], grad_pre[...], 0, 0)
        kept[width : 2 * width, :] = dot(hidden[...], grad_output[...], 0, 0)

    @pl.when(scalars[3] == 0)
    def _():
        kept[0:width, :] = dot(edge[...], grad_pre[...], 0, 0)
        kept[width : 2 * width, :] = dot(grid_picked[...], grad_pre[...], 0, 0)


def pack_kernel(kept, got, gain_term, packed, done):
    count = packed.shape[0]
    half, width = kept.shape
    part = half // count
    tail = got[half : half + 16, :].astype(jnp.float32)
    gain = gain_rows(gain_term[0:1, :] + gain_of(tail[0:2]), LANES)
    for place in range(count):
        rows = pl.ds(place * part, part)
        data = narrow(kept[rows, :] + got[rows, :].astype(jnp.float32))
        packed[place] = jnp.concatenate([data, gain], axis=0).astype(jnp.bfloat16)
    done[...] = jnp.zeros(done.shape, jnp.float32)


def group_sum_kernel(shares, after, packed):
    total = shares[0].astype(jnp.float32)
    for place in range(1, shares.shape[0]):
        total = total + shares[place].astype(jnp.float32)
    data = total.shape[0] - 8
    gain = gain_rows(gain_of(total[data:]), LANES)
    packed[...] = jnp.concatenate([total[:data], gain], axis=0).astype(jnp.bfloat16)


def pair_sum_kernel(own, other, packed):
    total = own[...].astype(jnp.float32) + other[...].astype(jnp.float32)
    data = total.shape[0] - 8
    gain = gain_rows(gain_of(total[data:]), LANES)
    packed[...] = jnp.concatenate([total[:data], gain], axis=0).astype(jnp.bfloat16)


def whole_sum_kernel(factor, own, other, after, copies, gain_grad):
    total = (own[...].astype(jnp.float32) + other[...].astype(jnp.float32)) * factor
    data = copies.shape[1]
    gain_grad[...] = jnp.broadcast_to(gain_of(total[data:]), gain_grad.shape)
    share = total[:data].astype(jnp.bfloat16)
    for place in range(copies.shape[0]):
        copies[place] = share


def node_kernel(
    scalars,
    senders,
    receivers,
    grad_pre,
    w_first,
    after,
    edge_grad,
    grid_grad,
    mesh_own,
    to_first,
    to_second,
):
    edges, width = grad_pre.shape
    rows_grid, rows_mesh = grid_grad.shape[0], mesh_own.shape[0]

    def through(sums, first):
        upper, lower = upper_lower(sums)
        weights = w_first[first : first + width, :]
        return dot(upper, weights, 1, 1) + dot(lower, weights, 1, 1)

    near = jnp.zeros((3 * rows_mesh, width), jnp.float32)
    here = jnp.zeros((rows_grid, width), jnp.float32)
    for start in range(0, edges, TILE):
        rows = pl.ds(start, TILE)
        terms = grad_pre[rows, :]
        near = near + dot(
            spreads(live_receivers(scalars, receivers, start, TILE, rows_mesh), 3 * rows_mesh), terms
        )
        here = here + dot(spreads(senders[:, rows] - scalars[0], rows_grid), terms)
        edge_grad[rows, :] = dot(terms, w_first[0:width, :], 1, 1).astype(jnp.bfloat16)
    mesh_terms = through(near, 2 * width)
    to_first[...] = mesh_terms[0:rows_mesh].astype(jnp.bfloat16)
    mesh_own[...] = mesh_terms[rows_mesh : 2 * rows_mesh]
    to_second[...] = mesh_terms[2 * rows_mesh : 3 * rows_mesh].astype(jnp.bfloat16)
    grid_grad[...] = through(here, width).astype(jnp.bfloat16)


def put_half(scalars, flip, shares, first, second, wide, sems):
    half, width = wide.shape
    count = shares.shape[0]
    part = half // count
    half_index = 1 - scalars[3] if flip else scalars[3]
    size = sems.shape[0]
    rows = half // size

    def each(place, act):
        source = wide.at[pl.ds(place * rows, rows)]

        @pl.when(half_index == 0)
        def _():
            act(pltpu.make_async_copy(source, first.at[pl.ds(place * rows, rows)], sems.at[place]))

        @pl.when(half_index != 0)
        def _():
            start = half + place * rows
            if start < first.shape[0]:
                target = first.at[pl.ds(start, rows)]
            else:
                target = second.at[pl.ds(start - first.shape[0], rows)]
            act(pltpu.make_async_copy(source, target, sems.at[place]))

    for place in range(size):
        for index in range(place * count // size, (place + 1) * count // size):
            share = shares[index].astype(jnp.float32)
            for g in range(width // LANES):
                wide[index * part : (index + 1) * part, g * LANES : (g + 1) * LANES] = share[
                    g * part : (g + 1) * part
                ]
        each(place, lambda copy: copy.start())
    for place in range(size):
        each(place, lambda copy: copy.wait())


def own_half_kernel(scalars, shares, first, second, wide, sems):
    put_half(scalars, False, shares, first, second, wide, sems)


def other_half_kernel(scalars, shares, first_in, second_in, first, second, wide, sems):
    put_half(scalars, True, shares, first, second, wide, sems)


def swap_pairs(value, axis, pairs):
    return lax.ppermute(value, axis, pairs + [(d, s) for s, d in pairs])


def exchanged(value, turn):
    count = lax.axis_size(SHARDS)
    return swap_pairs(value, SHARDS, [(s, s + 1) for s in range(turn, count - 1, 2)])


def swapped(value):
    return swap_pairs(value, "rep", [(0, 1)])


def per_device(
    grid_latent,
    mesh_latent,
    edge_latent,
    mesh_cotangent,
    w_first,
    w_second,
    norm_gain,
    senders,
    receivers,
    live_counts,
):
    width = w_second.shape[0]
    rows_grid = grid_latent.shape[1]
    rows_mesh = mesh_latent.shape[1]
    slots = senders.shape[0]
    group, groups = lax.axis_size(GROUP), lax.axis_size("hi")
    factor = 1.0 / math.sqrt(slots * group * groups * lax.axis_size("rep"))
    shard = lax.axis_index(SHARDS)
    scalars = jnp.stack(
        [
            shard * rows_grid,
            (shard - 1) * rows_mesh,
            live_counts[0],
            lax.axis_index("rep").astype(jnp.int32),
            jnp.where(shard % 2 == 0, 2 * rows_mesh, 0),
        ]
    ).astype(jnp.int32)
    senders, receivers = senders[None], receivers[None]
    gain = norm_gain[None]
    grid, mesh, edge, cot = grid_latent[0], mesh_latent[0], edge_latent[0], mesh_cotangent[0]
    matrix = functools.partial(jax.ShapeDtypeStruct, dtype=jnp.bfloat16)
    floats = functools.partial(jax.ShapeDtypeStruct, dtype=jnp.float32)
    unit = 2.0 * slots * width * width

    mesh_second, mesh_first = exchanged(mesh, 1), exchanged(mesh, 0)
    cot_second, cot_first = exchanged(cot, 1), exchanged(cot, 0)
    partial, grid_picked, edge, w_first, w_second = call(
        near_kernel,
        "near",
        [in_smem()] + [in_hbm()] * 5,
        [
            floats((slots, width)),
            matrix((slots, width)),
            pltpu.VMEM((slots, width), jnp.bfloat16),
            pltpu.VMEM((3 * width, width), jnp.bfloat16),
            pltpu.VMEM((width, width), jnp.bfloat16),
        ],
        (scalars, senders, grid, edge, w_first, w_second),
        3 * unit,
        [
            pltpu.VMEM((1, slots), jnp.int32),
            pltpu.VMEM((rows_grid, width), jnp.bfloat16),
            pltpu.SemaphoreType.DMA((6 + slots // TILE,)),
        ],
    )
    pre_act, output, hidden, mesh_picked = call(
        forward_kernel,
        "forward",
        [in_smem()] + [in_vmem()] * 7,
        [floats((slots, width))] * 2 + [matrix((slots, width))] * 2,
        (scalars, receivers, partial, mesh_first, mesh, mesh_second, w_first, w_second),
        3 * unit,
    )
    sent, gain_term, grad_pre, grad_output = call(
        backward_kernel,
        "backward",
        [in_smem()] + [in_vmem()] * 12,
        [
            matrix((2 * width + 16, width)),
            floats((8, width)),
            pltpu.VMEM((slots, width), jnp.bfloat16),
            matrix((slots, width)),
        ],
        (
            scalars,
            receivers,
            cot_first,
            cot,
            cot_second,
            pre_act,
            output,
            hidden,
            mesh_picked,
            grid_picked,
            edge,
            w_second,
            gain,
        ),
        4 * unit,
    )
    got = swapped(sent)
    (kept,) = call(
        kept_kernel,
        "kept",
        [in_smem()] + [in_vmem()] * 6,
        [floats((2 * width, width))],
        (scalars, edge, grid_picked, mesh_picked, hidden, grad_pre, grad_output),
        2 * unit,
    )
    part = 2 * width // group * width // LANES
    extra = 2 * width // LANES
    packed, done = call(
        pack_kernel,
        "pack",
        [in_vmem()] * 3,
        [matrix((group, part + extra, LANES)), floats((8, LANES))],
        (kept, got, gain_term),
        0,
    )
    edge_grad, grid_grad, mesh_own, to_first, to_second = call(
        node_kernel,
        "nodes",
        [in_smem()] + [in_vmem()] * 4 + [anywhere()],
        [
            matrix((slots, width)),
            matrix((rows_grid, width)),
            floats((rows_mesh, width)),
            matrix((rows_mesh, width)),
            matrix((rows_mesh, width)),
        ],
        (scalars, senders, receivers, grad_pre, w_first, done),
        4 * unit,
    )
    from_first = exchanged(to_first, 0).astype(jnp.float32)
    from_second = exchanged(to_second, 1).astype(jnp.float32)
    mesh_grad = mesh_own + from_first + from_second
    shares = lax.all_to_all(packed, GROUP, 0, 0)
    (packed,) = call(
        group_sum_kernel,
        "group_sum",
        [in_vmem(), anywhere()],
        [matrix((part + extra, LANES))],
        (shares, mesh_own),
        0,
    )
    met = swap_pairs(packed, "hi", [(0, 1), (2, 3)])
    (packed,) = call(
        pair_sum_kernel, "pair_sum", [in_vmem()] * 2, [matrix((part + extra, LANES))], (packed, met), 0
    )
    met = swap_pairs(packed, "hi", [(0, 3), (1, 2)])
    copies, gain_grad = call(
        functools.partial(whole_sum_kernel, factor),
        "whole_sum",
        [in_vmem()] * 2 + [anywhere()],
        [matrix((group, part, LANES)), floats((8, width))],
        (packed, met, mesh_grad),
        0,
    )
    total = lax.all_to_all(copies, GROUP, 0, 0)
    other = swapped(total)
    outs = [floats((3 * width, width)), floats((width, width))]
    halves = functools.partial(
        pl.pallas_call,
        out_shape=outs,
        out_specs=[in_hbm()] * 2,
        scratch_shapes=[
            pltpu.VMEM((2 * width, width), jnp.float32),
            pltpu.SemaphoreType.DMA((8,)),
        ],
        compiler_params=pltpu.CompilerParams(vmem_limit_bytes=24 * MIB),
        cost_estimate=pl.CostEstimate(flops=0, bytes_accessed=6 * MIB, transcendentals=0),
    )
    written = halves(own_half_kernel, in_specs=[in_smem(), in_vmem()], name="own_half")(scalars, total)
    first_grad, second_grad = halves(
        other_half_kernel,
        in_specs=[in_smem(), in_vmem()] + [in_hbm()] * 2,
        input_output_aliases={2: 0, 3: 1},
        name="other_half",
    )(scalars, other, *written)
    return (
        grid_grad[None],
        mesh_grad[None],
        edge_grad[None],
        first_grad,
        second_grad,
        gain_grad[0],
    )


def solution(mesh):
    bands, meshes, cores = mesh.devices.shape
    mesh = jax.sharding.Mesh(
        mesh.devices.reshape(bands, 4, meshes // 4, cores), ("band", "hi", "lo", "rep")
    )
    in_specs = (
        P("rep", SHARDS, None),
        P("rep", SHARDS, None),
        P("rep", SHARDS, None),
        P("rep", SHARDS, None),
        P(),
        P(),
        P(),
        P(SHARDS),
        P(SHARDS),
        P(SHARDS),
    )
    out_specs = (
        P("rep", SHARDS, None),
        P("rep", SHARDS, None),
        P("rep", SHARDS, None),
        P(),
        P(),
        P(),
    )
    return jax.shard_map(
        per_device, mesh=mesh, in_specs=in_specs, out_specs=out_specs, check_vma=False
    )
```

```python
import functools
import math

import jax
import jax.numpy as jnp
from jax import lax
from jax.experimental import pallas as pl
from jax.experimental.pallas import tpu as pltpu
from jax.sharding import PartitionSpec as P

NORM_EPS = 1e-05
SHARDS = ("band", "hi", "lo")
GROUP = ("band", "lo")
TILE = 256
EDGE_TILE = 1024
LANES = 128
MIB = 1 << 20


def dot(left, right, left_dim=1, right_dim=0):
    return lax.dot_general(
        left,
        right,
        (((left_dim,), (right_dim,)), ((), ())),
        preferred_element_type=jnp.float32,
    )


def picks(row, width):
    edges = row.shape[1]
    column = jnp.transpose(jnp.broadcast_to(row, (LANES, edges)))
    lane = lax.broadcasted_iota(jnp.int32, (edges, LANES), 1)
    return jnp.concatenate(
        [(column == lane + start).astype(jnp.float32).astype(jnp.bfloat16) for start in range(0, width, LANES)],
        axis=1,
    )


def spreads(row, width):
    edges = row.shape[1]
    place = lax.broadcasted_iota(jnp.int32, (width, edges), 0)
    return (place == row).astype(jnp.float32).astype(jnp.bfloat16)


def upper_lower(value):
    upper = value.astype(jnp.bfloat16)
    return upper, (value - upper.astype(jnp.float32)).astype(jnp.bfloat16)


def gain_rows(gain, lanes):
    terms = [term.astype(jnp.float32) for term in upper_lower(gain)]
    count = gain.shape[1] // lanes
    return jnp.concatenate(
        [term[:, g * lanes : (g + 1) * lanes] for term in terms for g in range(count)], axis=0
    )


def gain_of(rows):
    count = rows.shape[0] // 2
    return jnp.concatenate([rows[g : g + 1] + rows[count + g : count + g + 1] for g in range(count)], axis=1)


def narrow(rows):
    return jnp.concatenate(
        [rows[:, g : g + LANES] for g in range(0, rows.shape[1], LANES)], axis=0
    )


def anywhere():
    return pl.BlockSpec(memory_space=pl.ANY)


def in_vmem():
    return pl.BlockSpec(memory_space=pltpu.VMEM)


def in_hbm():
    return pl.BlockSpec(memory_space=pltpu.HBM)


def in_smem():
    return pl.BlockSpec(memory_space=pltpu.SMEM)


def call(kernel, name, specs, outs, operands, flops, scratch=(), limit=24 * MIB):
    operands = [
        pltpu.with_memory_space_constraint(o, pltpu.HBM) if spec.memory_space == pltpu.HBM else o
        for o, spec in zip(operands, specs)
    ]
    size = sum(math.prod(o.shape) * jnp.dtype(o.dtype).itemsize for o in outs)
    size += sum(math.prod(o.shape) * jnp.dtype(o.dtype).itemsize for o in operands)
    return pl.pallas_call(
        kernel,
        out_shape=outs,
        in_specs=specs,
        out_specs=[in_vmem()] * len(outs),
        scratch_shapes=list(scratch),
        compiler_params=pltpu.CompilerParams(vmem_limit_bytes=limit),
        cost_estimate=pl.CostEstimate(flops=int(flops), bytes_accessed=size, transcendentals=0),
        name=name,
    )(*operands)


def stack_kernel(mesh, cot, stacked, sems):
    rows = mesh.shape[0]
    copies = [
        pltpu.make_async_copy(mesh, stacked.at[pl.ds(0, rows)], sems.at[0]),
        pltpu.make_async_copy(cot, stacked.at[pl.ds(rows, rows)], sems.at[1]),
    ]
    for copy in copies:
        copy.start()
    for copy in copies:
        copy.wait()


def near_kernel(
    scalars,
    senders,
    grid,
    edge,
    w_first,
    w_second,
    partial,
    grid_picked,
    edge_here,
    w_first_here,
    w_second_here,
    senders_here,
    grid_here,
    sems,
):
    rows_grid, width = grid.shape
    tiles = range(0, edge.shape[0], TILE)
    pairs = [(senders, senders_here), (grid, grid_here)]
    for first in (width, 0):
        rows = pl.ds(first, width)
        pairs.append((w_first.at[rows], w_first_here.at[rows]))
    for start in tiles:
        rows = pl.ds(start, TILE)
        pairs.append((edge.at[rows], edge_here.at[rows]))
    rows = pl.ds(2 * width, width)
    pairs += [(w_first.at[rows], w_first_here.at[rows]), (w_second, w_second_here)]
    copies = [
        pltpu.make_async_copy(source, target, sems.at[place])
        for place, (source, target) in enumerate(pairs)
    ]
    for copy in copies:
        copy.start()
    for copy in copies[:4]:
        copy.wait()
    for start, copy in zip(tiles, copies[4:]):
        rows = pl.ds(start, TILE)
        table = picks(senders_here[:, rows] - scalars[0], rows_grid)
        picked = dot(table, grid_here[...]).astype(jnp.bfloat16)
        grid_picked[rows, :] = picked
        copy.wait()
        partial[rows, :] = dot(edge_here[rows, :], w_first_here[0:width, :]) + dot(
            picked, w_first_here[width : 2 * width, :]
        )
    for copy in copies[-2:]:
        copy.wait()


def live_receivers(scalars, receivers, start, tile, rows_mesh):
    row = receivers[:, pl.ds(start, tile)] - scalars[1]
    row = jnp.where(
        row < rows_mesh,
        row + scalars[4],
        jnp.where(row >= 2 * rows_mesh, row - scalars[4], row),
    )
    slot = start + lax.broadcasted_iota(jnp.int32, (1, tile), 1)
    return jnp.where(slot < scalars[2], row, -1)


def edge_kernel(
    scalars,
    receivers,
    partial,
    grid_picked,
    edge,
    stack_first,
    stack_own,
    stack_second,
    w_first,
    w_second,
    norm_gain,
    sent,
    gain_term,
    grad_pre,
    grad_output,
    hidden,
    mesh_picked,
):
    width = w_second.shape[0]
    rows_mesh = stack_own.shape[0] // 2
    gain_sum = jnp.zeros((1, width), jnp.float32)
    for start in range(0, edge.shape[0], EDGE_TILE):
        rows = pl.ds(start, EDGE_TILE)
        table = picks(live_receivers(scalars, receivers, start, EDGE_TILE, rows_mesh), 3 * rows_mesh)

        def picked_rows(first):
            part = pl.ds(first, rows_mesh)
            near = jnp.concatenate([stack_first[part, :], stack_own[part, :], stack_second[part, :]], axis=0)
            return dot(table, near)

        latents = picked_rows(0).astype(jnp.bfloat16)
        upstream = picked_rows(rows_mesh)
        mesh_picked[rows, :] = latents
        pre_act = partial[rows, :] + dot(latents, w_first[2 * width : 3 * width, :])
        sigmoid = 0.5 * jnp.tanh(0.5 * pre_act) + 0.5
        hid = (pre_act * sigmoid).astype(jnp.bfloat16)
        hidden[rows, :] = hid
        output = dot(hid, w_second[...])
        centered = output - jnp.mean(output, axis=1, keepdims=True)
        inverse = lax.rsqrt(jnp.mean(centered * centered, axis=1, keepdims=True) + NORM_EPS)
        normed = centered * inverse
        gain_sum = gain_sum + jnp.sum(upstream * normed, axis=0, keepdims=True)
        scaled = upstream * norm_gain[...]
        grad_out = (
            inverse
            * (
                scaled
                - jnp.mean(scaled, axis=1, keepdims=True)
                - normed * jnp.mean(scaled * normed, axis=1, keepdims=True)
            )
        ).astype(jnp.bfloat16)
        grad_output[rows, :] = grad_out
        grad_hidden = dot(grad_out, w_second[...], 1, 1)
        grad_pre[rows, :] = (grad_hidden * sigmoid * (1.0 + pre_act * (1.0 - sigmoid))).astype(
            jnp.bfloat16
        )
    gain_term[...] = jnp.broadcast_to(gain_sum, gain_term.shape)
    sent[2 * width : 2 * width + 16, :] = jnp.concatenate(
        [gain_rows(gain_sum, width), jnp.zeros((14, width), jnp.float32)], axis=0
    ).astype(jnp.bfloat16)

    @pl.when(scalars[3] == 0)
    def _():
        sent[0:width, :] = dot(mesh_picked[...], grad_pre[...], 0, 0).astype(jnp.bfloat16)
        sent[width : 2 * width, :] = dot(hidden[...], grad_output[...], 0, 0).astype(jnp.bfloat16)

    @pl.when(scalars[3] != 0)
    def _():
        sent[0:width, :] = dot(edge[...], grad_pre[...], 0, 0).astype(jnp.bfloat16)
        sent[width : 2 * width, :] = dot(grid_picked[...], grad_pre[...], 0, 0).astype(jnp.bfloat16)


def kept_kernel(scalars, edge, grid_picked, mesh_picked, hidden, grad_pre, grad_output, kept):
    width = grad_pre.shape[1]

    @pl.when(scalars[3] != 0)
    def _():
        kept[0:width, :] = dot(mesh_picked[...], grad_pre[...], 0, 0)
        kept[width : 2 * width, :] = dot(hidden[...], grad_output[...], 0, 0)

    @pl.when(scalars[3] == 0)
    def _():
        kept[0:width, :] = dot(edge[...], grad_pre[...], 0, 0)
        kept[width : 2 * width, :] = dot(grid_picked[...], grad_pre[...], 0, 0)


def pack_kernel(kept, got, gain_term, packed, done):
    count = packed.shape[0]
    half, width = kept.shape
    part = half // count
    tail = got[half : half + 16, :].astype(jnp.float32)
    gain = gain_rows(gain_term[0:1, :] + gain_of(tail[0:2]), LANES)
    for place in range(count):
        rows = pl.ds(place * part, part)
        data = narrow(kept[rows, :] + got[rows, :].astype(jnp.float32))
        packed[place] = jnp.concatenate([data, gain], axis=0).astype(jnp.bfloat16)
    done[...] = jnp.zeros(done.shape, jnp.float32)


def group_sum_kernel(shares, after, packed):
    total = shares[0].astype(jnp.float32)
    for place in range(1, shares.shape[0]):
        total = total + shares[place].astype(jnp.float32)
    data = total.shape[0] - 8
    gain = gain_rows(gain_of(total[data:]), LANES)
    packed[...] = jnp.concatenate([total[:data], gain], axis=0).astype(jnp.bfloat16)


def whole_sum_kernel(factor, own, near, across, far, after, copies, gain_grad):
    own, near, across, far = [part[...].astype(jnp.float32) for part in (own, near, across, far)]
    total = ((own + across) + (near + far)) * factor
    data = copies.shape[1]
    gain_grad[...] = jnp.broadcast_to(gain_of(total[data:]), gain_grad.shape)
    share = total[:data].astype(jnp.bfloat16)
    for place in range(copies.shape[0]):
        copies[place] = share


def node_kernel(
    scalars,
    senders,
    receivers,
    grad_pre,
    w_first,
    after,
    edge_grad,
    grid_grad,
    mesh_own,
    to_first,
    to_second,
):
    edges, width = grad_pre.shape
    rows_grid, rows_mesh = grid_grad.shape[0], mesh_own.shape[0]

    def through(sums, first):
        upper, lower = upper_lower(sums)
        weights = w_first[first : first + width, :]
        return dot(upper, weights, 1, 1) + dot(lower, weights, 1, 1)

    near = jnp.zeros((3 * rows_mesh, width), jnp.float32)
    here = jnp.zeros((rows_grid, width), jnp.float32)
    for start in range(0, edges, TILE):
        rows = pl.ds(start, TILE)
        terms = grad_pre[rows, :]
        near = near + dot(
            spreads(live_receivers(scalars, receivers, start, TILE, rows_mesh), 3 * rows_mesh), terms
        )
        here = here + dot(spreads(senders[:, rows] - scalars[0], rows_grid), terms)
        edge_grad[rows, :] = dot(terms, w_first[0:width, :], 1, 1).astype(jnp.bfloat16)
    mesh_terms = through(near, 2 * width)
    to_first[...] = mesh_terms[0:rows_mesh].astype(jnp.bfloat16)
    mesh_own[...] = mesh_terms[rows_mesh : 2 * rows_mesh]
    to_second[...] = mesh_terms[2 * rows_mesh : 3 * rows_mesh].astype(jnp.bfloat16)
    grid_grad[...] = through(here, width).astype(jnp.bfloat16)


def put_half(scalars, flip, shares, first, second, wide, sems):
    half, width = wide.shape
    count = shares.shape[0]
    part = half // count
    half_index = 1 - scalars[3] if flip else scalars[3]
    size = sems.shape[0]
    rows = half // size

    def each(place, act):
        source = wide.at[pl.ds(place * rows, rows)]

        @pl.when(half_index == 0)
        def _():
            act(pltpu.make_async_copy(source, first.at[pl.ds(place * rows, rows)], sems.at[place]))

        @pl.when(half_index != 0)
        def _():
            start = half + place * rows
            if start < first.shape[0]:
                target = first.at[pl.ds(start, rows)]
            else:
                target = second.at[pl.ds(start - first.shape[0], rows)]
            act(pltpu.make_async_copy(source, target, sems.at[place]))

    for place in range(size):
        for index in range(place * count // size, (place + 1) * count // size):
            share = shares[index].astype(jnp.float32)
            for g in range(width // LANES):
                wide[index * part : (index + 1) * part, g * LANES : (g + 1) * LANES] = share[
                    g * part : (g + 1) * part
                ]
        each(place, lambda copy: copy.start())
    for place in range(size):
        each(place, lambda copy: copy.wait())


def own_half_kernel(scalars, shares, first, second, wide, sems):
    put_half(scalars, False, shares, first, second, wide, sems)


def other_half_kernel(scalars, shares, first_in, second_in, first, second, wide, sems):
    put_half(scalars, True, shares, first, second, wide, sems)


def swap_pairs(value, axis, pairs):
    return lax.ppermute(value, axis, pairs + [(d, s) for s, d in pairs])


def exchanged(value, turn):
    count = lax.axis_size(SHARDS)
    return swap_pairs(value, SHARDS, [(s, s + 1) for s in range(turn, count - 1, 2)])


def swapped(value):
    return swap_pairs(value, "rep", [(0, 1)])


def per_device(
    grid_latent,
    mesh_latent,
    edge_latent,
    mesh_cotangent,
    w_first,
    w_second,
    norm_gain,
    senders,
    receivers,
    live_counts,
):
    width = w_second.shape[0]
    rows_grid = grid_latent.shape[1]
    rows_mesh = mesh_latent.shape[1]
    slots = senders.shape[0]
    group, groups = lax.axis_size(GROUP), lax.axis_size("hi")
    factor = 1.0 / math.sqrt(slots * group * groups * lax.axis_size("rep"))
    shard = lax.axis_index(SHARDS)
    scalars = jnp.stack(
        [
            shard * rows_grid,
            (shard - 1) * rows_mesh,
            live_counts[0],
            lax.axis_index("rep").astype(jnp.int32),
            jnp.where(shard % 2 == 0, 2 * rows_mesh, 0),
        ]
    ).astype(jnp.int32)
    senders, receivers = senders[None], receivers[None]
    gain = norm_gain[None]
    grid, mesh, edge, cot = grid_latent[0], mesh_latent[0], edge_latent[0], mesh_cotangent[0]
    matrix = functools.partial(jax.ShapeDtypeStruct, dtype=jnp.bfloat16)
    floats = functools.partial(jax.ShapeDtypeStruct, dtype=jnp.float32)
    unit = 2.0 * slots * width * width

    (stacked,) = call(
        stack_kernel,
        "stack",
        [in_hbm()] * 2,
        [matrix((2 * rows_mesh, width))],
        (mesh, cot),
        0,
        [pltpu.SemaphoreType.DMA((2,))],
    )
    stack_first, stack_second = exchanged(stacked, 0), exchanged(stacked, 1)
    partial, grid_picked, edge, w_first, w_second = call(
        near_kernel,
        "near",
        [in_smem()] + [in_hbm()] * 5,
        [
            floats((slots, width)),
            matrix((slots, width)),
            pltpu.VMEM((slots, width), jnp.bfloat16),
            pltpu.VMEM((3 * width, width), jnp.bfloat16),
            pltpu.VMEM((width, width), jnp.bfloat16),
        ],
        (scalars, senders, grid, edge, w_first, w_second),
        3 * unit,
        [
            pltpu.VMEM((1, slots), jnp.int32),
            pltpu.VMEM((rows_grid, width), jnp.bfloat16),
            pltpu.SemaphoreType.DMA((6 + slots // TILE,)),
        ],
    )
    sent, gain_term, grad_pre, grad_output, hidden, mesh_picked = call(
        edge_kernel,
        "edges",
        [in_smem()] + [in_vmem()] * 10,
        [
            matrix((2 * width + 16, width)),
            floats((8, width)),
            pltpu.VMEM((slots, width), jnp.bfloat16),
        ]
        + [matrix((slots, width))] * 3,
        (
            scalars,
            receivers,
            partial,
            grid_picked,
            edge,
            stack_first,
            stacked,
            stack_second,
            w_first,
            w_second,
            gain,
        ),
        7 * unit,
    )
    got = swapped(sent)
    (kept,) = call(
        kept_kernel,
        "kept",
        [in_smem()] + [in_vmem()] * 6,
        [floats((2 * width, width))],
        (scalars, edge, grid_picked, mesh_picked, hidden, grad_pre, grad_output),
        2 * unit,
    )
    part = 2 * width // group * width // LANES
    extra = 2 * width // LANES
    packed, done = call(
        pack_kernel,
        "pack",
        [in_vmem()] * 3,
        [matrix((group, part + extra, LANES)), floats((8, LANES))],
        (kept, got, gain_term),
        0,
    )
    edge_grad, grid_grad, mesh_own, to_first, to_second = call(
        node_kernel,
        "nodes",
        [in_smem()] + [in_vmem()] * 4 + [anywhere()],
        [
            matrix((slots, width)),
            matrix((rows_grid, width)),
            floats((rows_mesh, width)),
            matrix((rows_mesh, width)),
            matrix((rows_mesh, width)),
        ],
        (scalars, senders, receivers, grad_pre, w_first, done),
        4 * unit,
    )
    from_first = exchanged(to_first, 0).astype(jnp.float32)
    from_second = exchanged(to_second, 1).astype(jnp.float32)
    mesh_grad = mesh_own + from_first + from_second
    shares = lax.all_to_all(packed, GROUP, 0, 0)
    (packed,) = call(
        group_sum_kernel,
        "group_sum",
        [in_vmem(), anywhere()],
        [matrix((part + extra, LANES))],
        (shares, mesh_own),
        0,
    )
    turns = [
        swap_pairs(packed, "hi", pairs)
        for pairs in ([(0, 1), (2, 3)], [(0, 2), (1, 3)], [(0, 3), (1, 2)])
    ]
    copies, gain_grad = call(
        functools.partial(whole_sum_kernel, factor),
        "whole_sum",
        [in_vmem()] * 4 + [anywhere()],
        [matrix((group, part, LANES)), floats((8, width))],
        (packed, *turns, mesh_grad),
        0,
    )
    total = lax.all_to_all(copies, GROUP, 0, 0)
    other = swapped(total)
    outs = [floats((3 * width, width)), floats((width, width))]
    halves = functools.partial(
        pl.pallas_call,
        out_shape=outs,
        out_specs=[in_hbm()] * 2,
        scratch_shapes=[
            pltpu.VMEM((2 * width, width), jnp.float32),
            pltpu.SemaphoreType.DMA((8,)),
        ],
        compiler_params=pltpu.CompilerParams(vmem_limit_bytes=24 * MIB),
        cost_estimate=pl.CostEstimate(flops=0, bytes_accessed=6 * MIB, transcendentals=0),
    )
    written = halves(own_half_kernel, in_specs=[in_smem(), in_vmem()], name="own_half")(scalars, total)
    first_grad, second_grad = halves(
        other_half_kernel,
        in_specs=[in_smem(), in_vmem()] + [in_hbm()] * 2,
        input_output_aliases={2: 0, 3: 1},
        name="other_half",
    )(scalars, other, *written)
    return (
        grid_grad[None],
        mesh_grad[None],
        edge_grad[None],
        first_grad,
        second_grad,
        gain_grad[0],
    )


def solution(mesh):
    bands, meshes, cores = mesh.devices.shape
    mesh = jax.sharding.Mesh(
        mesh.devices.reshape(bands, 4, meshes // 4, cores), ("band", "hi", "lo", "rep")
    )
    in_specs = (
        P("rep", SHARDS, None),
        P("rep", SHARDS, None),
        P("rep", SHARDS, None),
        P("rep", SHARDS, None),
        P(),
        P(),
        P(),
        P(SHARDS),
        P(SHARDS),
        P(SHARDS),
    )
    out_specs = (
        P("rep", SHARDS, None),
        P("rep", SHARDS, None),
        P("rep", SHARDS, None),
        P(),
        P(),
        P(),
    )
    return jax.shard_map(
        per_device, mesh=mesh, in_specs=in_specs, out_specs=out_specs, check_vma=False
    )
```

```python
import functools
import math

import jax
import jax.numpy as jnp
from jax import lax
from jax.experimental import pallas as pl
from jax.experimental.pallas import tpu as pltpu
from jax.sharding import PartitionSpec as P

NORM_EPS = 1e-05
SHARDS = ("x_far", "x_near", "y_far", "y_near", "z_far", "z_near")
GROUP = ("x_near", "y_near", "z_near")
FAR = ("x_far", "y_far", "z_far")
TILE = 256
EDGE_TILE = 1024
LANES = 128
MIB = 1 << 20


def dot(left, right, left_dim=1, right_dim=0):
    return lax.dot_general(
        left,
        right,
        (((left_dim,), (right_dim,)), ((), ())),
        preferred_element_type=jnp.float32,
    )


def picks(row, width):
    edges = row.shape[1]
    column = jnp.transpose(jnp.broadcast_to(row, (LANES, edges)))
    lane = lax.broadcasted_iota(jnp.int32, (edges, LANES), 1)
    return jnp.concatenate(
        [(column == lane + start).astype(jnp.float32).astype(jnp.bfloat16) for start in range(0, width, LANES)],
        axis=1,
    )


def spreads(row, width):
    edges = row.shape[1]
    place = lax.broadcasted_iota(jnp.int32, (width, edges), 0)
    return (place == row).astype(jnp.float32).astype(jnp.bfloat16)


def upper_lower(value):
    upper = value.astype(jnp.bfloat16)
    return upper, (value - upper.astype(jnp.float32)).astype(jnp.bfloat16)


def gain_rows(gain, lanes):
    terms = [term.astype(jnp.float32) for term in upper_lower(gain)]
    count = gain.shape[1] // lanes
    return jnp.concatenate(
        [term[:, g * lanes : (g + 1) * lanes] for term in terms for g in range(count)], axis=0
    )


def gain_of(rows):
    count = rows.shape[0] // 2
    return jnp.concatenate([rows[g : g + 1] + rows[count + g : count + g + 1] for g in range(count)], axis=1)


def narrow(rows):
    return jnp.concatenate(
        [rows[:, g : g + LANES] for g in range(0, rows.shape[1], LANES)], axis=0
    )


def anywhere():
    return pl.BlockSpec(memory_space=pl.ANY)


def in_vmem():
    return pl.BlockSpec(memory_space=pltpu.VMEM)


def in_hbm():
    return pl.BlockSpec(memory_space=pltpu.HBM)


def in_smem():
    return pl.BlockSpec(memory_space=pltpu.SMEM)


def call(kernel, name, specs, outs, operands, flops, scratch=(), limit=24 * MIB):
    operands = [
        pltpu.with_memory_space_constraint(o, pltpu.HBM) if spec.memory_space == pltpu.HBM else o
        for o, spec in zip(operands, specs)
    ]
    size = sum(math.prod(o.shape) * jnp.dtype(o.dtype).itemsize for o in outs)
    size += sum(math.prod(o.shape) * jnp.dtype(o.dtype).itemsize for o in operands)
    return pl.pallas_call(
        kernel,
        out_shape=outs,
        in_specs=specs,
        out_specs=[in_vmem()] * len(outs),
        scratch_shapes=list(scratch),
        compiler_params=pltpu.CompilerParams(vmem_limit_bytes=limit),
        cost_estimate=pl.CostEstimate(flops=int(flops), bytes_accessed=size, transcendentals=0),
        name=name,
    )(*operands)


def stack_kernel(mesh, cot, stacked, sems):
    rows = mesh.shape[0]
    copies = [
        pltpu.make_async_copy(mesh, stacked.at[pl.ds(0, rows)], sems.at[0]),
        pltpu.make_async_copy(cot, stacked.at[pl.ds(rows, rows)], sems.at[1]),
    ]
    for copy in copies:
        copy.start()
    for copy in copies:
        copy.wait()


def near_kernel(
    scalars,
    senders,
    grid,
    edge,
    w_first,
    w_second,
    partial,
    grid_picked,
    edge_here,
    w_first_here,
    w_second_here,
    senders_here,
    grid_here,
    sems,
):
    rows_grid, width = grid.shape
    tiles = range(0, edge.shape[0], TILE)
    pairs = [(senders, senders_here), (grid, grid_here)]
    for first in (width, 0):
        rows = pl.ds(first, width)
        pairs.append((w_first.at[rows], w_first_here.at[rows]))
    for start in tiles:
        rows = pl.ds(start, TILE)
        pairs.append((edge.at[rows], edge_here.at[rows]))
    rows = pl.ds(2 * width, width)
    pairs += [(w_first.at[rows], w_first_here.at[rows]), (w_second, w_second_here)]
    copies = [
        pltpu.make_async_copy(source, target, sems.at[place])
        for place, (source, target) in enumerate(pairs)
    ]
    for copy in copies:
        copy.start()
    for copy in copies[:4]:
        copy.wait()
    for start, copy in zip(tiles, copies[4:]):
        rows = pl.ds(start, TILE)
        table = picks(senders_here[:, rows] - scalars[0], rows_grid)
        picked = dot(table, grid_here[...]).astype(jnp.bfloat16)
        grid_picked[rows, :] = picked
        copy.wait()
        partial[rows, :] = dot(edge_here[rows, :], w_first_here[0:width, :]) + dot(
            picked, w_first_here[width : 2 * width, :]
        )
    for copy in copies[-2:]:
        copy.wait()


def live_receivers(scalars, receivers, start, tile, rows_mesh):
    row = receivers[:, pl.ds(start, tile)] - scalars[1]
    row = jnp.where(
        row < rows_mesh,
        row + scalars[4],
        jnp.where(row >= 2 * rows_mesh, row - scalars[4], row),
    )
    slot = start + lax.broadcasted_iota(jnp.int32, (1, tile), 1)
    return jnp.where(slot < scalars[2], row, -1)


def edge_kernel(
    scalars,
    receivers,
    partial,
    grid_picked,
    edge,
    stack_first,
    stack_own,
    stack_second,
    w_first,
    w_second,
    norm_gain,
    sent,
    gain_term,
    grad_pre,
    grad_output,
    hidden,
    mesh_picked,
):
    width = w_second.shape[0]
    rows_mesh = stack_own.shape[0] // 2
    gain_sum = jnp.zeros((1, width), jnp.float32)
    for start in range(0, edge.shape[0], EDGE_TILE):
        rows = pl.ds(start, EDGE_TILE)
        table = picks(live_receivers(scalars, receivers, start, EDGE_TILE, rows_mesh), 3 * rows_mesh)

        def picked_rows(first):
            part = pl.ds(first, rows_mesh)
            near = jnp.concatenate([stack_first[part, :], stack_own[part, :], stack_second[part, :]], axis=0)
            return dot(table, near)

        latents = picked_rows(0).astype(jnp.bfloat16)
        upstream = picked_rows(rows_mesh)
        mesh_picked[rows, :] = latents
        pre_act = partial[rows, :] + dot(latents, w_first[2 * width : 3 * width, :])
        sigmoid = 0.5 * jnp.tanh(0.5 * pre_act) + 0.5
        hid = (pre_act * sigmoid).astype(jnp.bfloat16)
        hidden[rows, :] = hid
        output = dot(hid, w_second[...])
        centered = output - jnp.mean(output, axis=1, keepdims=True)
        inverse = lax.rsqrt(jnp.mean(centered * centered, axis=1, keepdims=True) + NORM_EPS)
        normed = centered * inverse
        gain_sum = gain_sum + jnp.sum(upstream * normed, axis=0, keepdims=True)
        scaled = upstream * norm_gain[...]
        grad_out = (
            inverse
            * (
                scaled
                - jnp.mean(scaled, axis=1, keepdims=True)
                - normed * jnp.mean(scaled * normed, axis=1, keepdims=True)
            )
        ).astype(jnp.bfloat16)
        grad_output[rows, :] = grad_out
        grad_hidden = dot(grad_out, w_second[...], 1, 1)
        grad_pre[rows, :] = (grad_hidden * sigmoid * (1.0 + pre_act * (1.0 - sigmoid))).astype(
            jnp.bfloat16
        )
    gain_term[...] = jnp.broadcast_to(gain_sum, gain_term.shape)
    sent[2 * width : 2 * width + 16, :] = jnp.concatenate(
        [gain_rows(gain_sum, width), jnp.zeros((14, width), jnp.float32)], axis=0
    ).astype(jnp.bfloat16)

    @pl.when(scalars[3] == 0)
    def _():
        sent[0:width, :] = dot(mesh_picked[...], grad_pre[...], 0, 0).astype(jnp.bfloat16)
        sent[width : 2 * width, :] = dot(hidden[...], grad_output[...], 0, 0).astype(jnp.bfloat16)

    @pl.when(scalars[3] != 0)
    def _():
        sent[0:width, :] = dot(edge[...], grad_pre[...], 0, 0).astype(jnp.bfloat16)
        sent[width : 2 * width, :] = dot(grid_picked[...], grad_pre[...], 0, 0).astype(jnp.bfloat16)


def kept_kernel(scalars, edge, grid_picked, mesh_picked, hidden, grad_pre, grad_output, kept):
    width = grad_pre.shape[1]

    @pl.when(scalars[3] != 0)
    def _():
        kept[0:width, :] = dot(mesh_picked[...], grad_pre[...], 0, 0)
        kept[width : 2 * width, :] = dot(hidden[...], grad_output[...], 0, 0)

    @pl.when(scalars[3] == 0)
    def _():
        kept[0:width, :] = dot(edge[...], grad_pre[...], 0, 0)
        kept[width : 2 * width, :] = dot(grid_picked[...], grad_pre[...], 0, 0)


def pack_kernel(kept, got, gain_term, packed, done):
    count = packed.shape[0]
    half, width = kept.shape
    part = half // count
    tail = got[half : half + 16, :].astype(jnp.float32)
    gain = gain_rows(gain_term[0:1, :] + gain_of(tail[0:2]), LANES)
    for place in range(count):
        rows = pl.ds(place * part, part)
        data = narrow(kept[rows, :] + got[rows, :].astype(jnp.float32))
        packed[place] = jnp.concatenate([data, gain], axis=0).astype(jnp.bfloat16)
    done[...] = jnp.zeros(done.shape, jnp.float32)


def group_sum_kernel(shares, after, packed):
    total = shares[0].astype(jnp.float32)
    for place in range(1, shares.shape[0]):
        total = total + shares[place].astype(jnp.float32)
    count = packed.shape[0]
    rows = packed.shape[1] - 8
    gain = gain_rows(gain_of(total[rows * count :]), LANES)
    for place in range(count):
        data = total[place * rows : (place + 1) * rows]
        packed[place] = jnp.concatenate([data, gain], axis=0).astype(jnp.bfloat16)


def whole_sum_kernel(factor, pieces, copies, gain_grad):
    total = pieces[0].astype(jnp.float32)
    for place in range(1, pieces.shape[0]):
        total = total + pieces[place].astype(jnp.float32)
    total = total * factor
    data = copies.shape[1]
    gain_grad[...] = jnp.broadcast_to(gain_of(total[data:]), gain_grad.shape)
    piece = total[:data].astype(jnp.bfloat16)
    for place in range(copies.shape[0]):
        copies[place] = piece


def copies_kernel(share, after, copies):
    for place in range(copies.shape[0]):
        copies[place] = share[...]


def node_kernel(
    scalars,
    senders,
    receivers,
    grad_pre,
    w_first,
    after,
    edge_grad,
    grid_grad,
    mesh_own,
    to_first,
    to_second,
):
    edges, width = grad_pre.shape
    rows_grid, rows_mesh = grid_grad.shape[0], mesh_own.shape[0]

    def through(sums, first):
        upper, lower = upper_lower(sums)
        weights = w_first[first : first + width, :]
        return dot(upper, weights, 1, 1) + dot(lower, weights, 1, 1)

    near = jnp.zeros((3 * rows_mesh, width), jnp.float32)
    here = jnp.zeros((rows_grid, width), jnp.float32)
    for start in range(0, edges, TILE):
        rows = pl.ds(start, TILE)
        terms = grad_pre[rows, :]
        near = near + dot(
            spreads(live_receivers(scalars, receivers, start, TILE, rows_mesh), 3 * rows_mesh), terms
        )
        here = here + dot(spreads(senders[:, rows] - scalars[0], rows_grid), terms)
        edge_grad[rows, :] = dot(terms, w_first[0:width, :], 1, 1).astype(jnp.bfloat16)
    mesh_terms = through(near, 2 * width)
    to_first[...] = mesh_terms[0:rows_mesh].astype(jnp.bfloat16)
    mesh_own[...] = mesh_terms[rows_mesh : 2 * rows_mesh]
    to_second[...] = mesh_terms[2 * rows_mesh : 3 * rows_mesh].astype(jnp.bfloat16)
    grid_grad[...] = through(here, width).astype(jnp.bfloat16)


def put_half(scalars, flip, shares, first, second, wide, sems):
    half, width = wide.shape
    count = shares.shape[0]
    part = half // count
    half_index = 1 - scalars[3] if flip else scalars[3]
    size = sems.shape[0]
    rows = half // size

    def each(place, act):
        source = wide.at[pl.ds(place * rows, rows)]

        @pl.when(half_index == 0)
        def _():
            act(pltpu.make_async_copy(source, first.at[pl.ds(place * rows, rows)], sems.at[place]))

        @pl.when(half_index != 0)
        def _():
            start = half + place * rows
            if start < first.shape[0]:
                target = first.at[pl.ds(start, rows)]
            else:
                target = second.at[pl.ds(start - first.shape[0], rows)]
            act(pltpu.make_async_copy(source, target, sems.at[place]))

    for place in range(size):
        for index in range(place * count // size, (place + 1) * count // size):
            share = shares[index].astype(jnp.float32)
            for g in range(width // LANES):
                wide[index * part : (index + 1) * part, g * LANES : (g + 1) * LANES] = share[
                    g * part : (g + 1) * part
                ]
        each(place, lambda copy: copy.start())
    for place in range(size):
        each(place, lambda copy: copy.wait())


def own_half_kernel(scalars, shares, first, second, wide, sems):
    put_half(scalars, False, shares, first, second, wide, sems)


def other_half_kernel(scalars, shares, first_in, second_in, first, second, wide, sems):
    put_half(scalars, True, shares, first, second, wide, sems)


def swap_pairs(value, axis, pairs):
    return lax.ppermute(value, axis, pairs + [(d, s) for s, d in pairs])


def exchanged(value, turn):
    count = lax.axis_size(SHARDS)
    return swap_pairs(value, SHARDS, [(s, s + 1) for s in range(turn, count - 1, 2)])


def swapped(value):
    return swap_pairs(value, "rep", [(0, 1)])


def per_device(
    grid_latent,
    mesh_latent,
    edge_latent,
    mesh_cotangent,
    w_first,
    w_second,
    norm_gain,
    senders,
    receivers,
    live_counts,
):
    width = w_second.shape[0]
    rows_grid = grid_latent.shape[1]
    rows_mesh = mesh_latent.shape[1]
    slots = senders.shape[0]
    group, groups = lax.axis_size(GROUP), lax.axis_size(FAR)
    factor = 1.0 / math.sqrt(slots * group * groups * lax.axis_size("rep"))
    shard = lax.axis_index(SHARDS)
    scalars = jnp.stack(
        [
            shard * rows_grid,
            (shard - 1) * rows_mesh,
            live_counts[0],
            lax.axis_index("rep").astype(jnp.int32),
            jnp.where(shard % 2 == 0, 2 * rows_mesh, 0),
        ]
    ).astype(jnp.int32)
    senders, receivers = senders[None], receivers[None]
    gain = norm_gain[None]
    grid, mesh, edge, cot = grid_latent[0], mesh_latent[0], edge_latent[0], mesh_cotangent[0]
    matrix = functools.partial(jax.ShapeDtypeStruct, dtype=jnp.bfloat16)
    floats = functools.partial(jax.ShapeDtypeStruct, dtype=jnp.float32)
    unit = 2.0 * slots * width * width

    (stacked,) = call(
        stack_kernel,
        "stack",
        [in_hbm()] * 2,
        [matrix((2 * rows_mesh, width))],
        (mesh, cot),
        0,
        [pltpu.SemaphoreType.DMA((2,))],
    )
    stack_first, stack_second = exchanged(stacked, 0), exchanged(stacked, 1)
    partial, grid_picked, edge, w_first, w_second = call(
        near_kernel,
        "near",
        [in_smem()] + [in_hbm()] * 5,
        [
            floats((slots, width)),
            matrix((slots, width)),
            pltpu.VMEM((slots, width), jnp.bfloat16),
            pltpu.VMEM((3 * width, width), jnp.bfloat16),
            pltpu.VMEM((width, width), jnp.bfloat16),
        ],
        (scalars, senders, grid, edge, w_first, w_second),
        3 * unit,
        [
            pltpu.VMEM((1, slots), jnp.int32),
            pltpu.VMEM((rows_grid, width), jnp.bfloat16),
            pltpu.SemaphoreType.DMA((6 + slots // TILE,)),
        ],
    )
    sent, gain_term, grad_pre, grad_output, hidden, mesh_picked = call(
        edge_kernel,
        "edges",
        [in_smem()] + [in_vmem()] * 10,
        [
            matrix((2 * width + 16, width)),
            floats((8, width)),
            pltpu.VMEM((slots, width), jnp.bfloat16),
        ]
        + [matrix((slots, width))] * 3,
        (
            scalars,
            receivers,
            partial,
            grid_picked,
            edge,
            stack_first,
            stacked,
            stack_second,
            w_first,
            w_second,
            gain,
        ),
        7 * unit,
    )
    got = swapped(sent)
    (kept,) = call(
        kept_kernel,
        "kept",
        [in_smem()] + [in_vmem()] * 6,
        [floats((2 * width, width))],
        (scalars, edge, grid_picked, mesh_picked, hidden, grad_pre, grad_output),
        2 * unit,
    )
    part = 2 * width // group * width // LANES
    extra = 2 * width // LANES
    packed, done = call(
        pack_kernel,
        "pack",
        [in_vmem()] * 3,
        [matrix((group, part + extra, LANES)), floats((8, LANES))],
        (kept, got, gain_term),
        0,
    )
    edge_grad, grid_grad, mesh_own, to_first, to_second = call(
        node_kernel,
        "nodes",
        [in_smem()] + [in_vmem()] * 4 + [anywhere()],
        [
            matrix((slots, width)),
            matrix((rows_grid, width)),
            floats((rows_mesh, width)),
            matrix((rows_mesh, width)),
            matrix((rows_mesh, width)),
        ],
        (scalars, senders, receivers, grad_pre, w_first, done),
        4 * unit,
    )
    from_first = exchanged(to_first, 0).astype(jnp.float32)
    from_second = exchanged(to_second, 1).astype(jnp.float32)
    mesh_grad = mesh_own + from_first + from_second
    shares = lax.all_to_all(packed, GROUP, 0, 0)
    (packed,) = call(
        group_sum_kernel,
        "group_sum",
        [in_vmem(), anywhere()],
        [matrix((groups, part // groups + extra, LANES))],
        (shares, mesh_own),
        0,
    )
    pieces = lax.all_to_all(packed, FAR, 0, 0)
    copies, gain_grad = call(
        functools.partial(whole_sum_kernel, factor),
        "whole_sum",
        [in_vmem()],
        [matrix((groups, part // groups, LANES)), floats((8, width))],
        (pieces,),
        0,
    )
    share = lax.all_to_all(copies, FAR, 0, 0).reshape(part, LANES)
    (copies,) = call(
        copies_kernel,
        "copies",
        [in_vmem(), anywhere()],
        [matrix((group, part, LANES))],
        (share, mesh_grad),
        0,
    )
    total = lax.all_to_all(copies, GROUP, 0, 0)
    other = swapped(total)
    outs = [floats((3 * width, width)), floats((width, width))]
    halves = functools.partial(
        pl.pallas_call,
        out_shape=outs,
        out_specs=[in_hbm()] * 2,
        scratch_shapes=[
            pltpu.VMEM((2 * width, width), jnp.float32),
            pltpu.SemaphoreType.DMA((8,)),
        ],
        compiler_params=pltpu.CompilerParams(vmem_limit_bytes=24 * MIB),
        cost_estimate=pl.CostEstimate(flops=0, bytes_accessed=6 * MIB, transcendentals=0),
    )
    written = halves(own_half_kernel, in_specs=[in_smem(), in_vmem()], name="own_half")(scalars, total)
    first_grad, second_grad = halves(
        other_half_kernel,
        in_specs=[in_smem(), in_vmem()] + [in_hbm()] * 2,
        input_output_aliases={2: 0, 3: 1},
        name="other_half",
    )(scalars, other, *written)
    return (
        grid_grad[None],
        mesh_grad[None],
        edge_grad[None],
        first_grad,
        second_grad,
        gain_grad[0],
    )


def solution(mesh):
    bands, meshes, cores = mesh.devices.shape
    side = math.isqrt(bands) // 2
    mesh = jax.sharding.Mesh(
        mesh.devices.reshape(side, 2, side, 2, meshes // 2, 2, cores), SHARDS + ("rep",)
    )
    in_specs = (
        P("rep", SHARDS, None),
        P("rep", SHARDS, None),
        P("rep", SHARDS, None),
        P("rep", SHARDS, None),
        P(),
        P(),
        P(),
        P(SHARDS),
        P(SHARDS),
        P(SHARDS),
    )
    out_specs = (
        P("rep", SHARDS, None),
        P("rep", SHARDS, None),
        P("rep", SHARDS, None),
        P(),
        P(),
        P(),
    )
    return jax.shard_map(
        per_device, mesh=mesh, in_specs=in_specs, out_specs=out_specs, check_vma=False
    )
```

```python
import functools
import math

import jax
import jax.numpy as jnp
from jax import lax
from jax.experimental import pallas as pl
from jax.experimental.pallas import tpu as pltpu
from jax.sharding import PartitionSpec as P

NORM_EPS = 1e-05
SHARDS = ("band", "hi", "lo")
GROUP = ("band", "lo")
TILE = 256
EDGE_TILE = 1024
LANES = 128
MIB = 1 << 20


def dot(left, right, left_dim=1, right_dim=0):
    return lax.dot_general(
        left,
        right,
        (((left_dim,), (right_dim,)), ((), ())),
        preferred_element_type=jnp.float32,
    )


def picks(row, width):
    edges = row.shape[1]
    column = jnp.transpose(jnp.broadcast_to(row, (LANES, edges)))
    lane = lax.broadcasted_iota(jnp.int32, (edges, LANES), 1)
    return jnp.concatenate(
        [(column == lane + start).astype(jnp.float32).astype(jnp.bfloat16) for start in range(0, width, LANES)],
        axis=1,
    )


def spreads(row, width):
    edges = row.shape[1]
    place = lax.broadcasted_iota(jnp.int32, (width, edges), 0)
    return (place == row).astype(jnp.float32).astype(jnp.bfloat16)


def upper_lower(value):
    upper = value.astype(jnp.bfloat16)
    return upper, (value - upper.astype(jnp.float32)).astype(jnp.bfloat16)


def gain_rows(gain, lanes):
    terms = [term.astype(jnp.float32) for term in upper_lower(gain)]
    count = gain.shape[1] // lanes
    return jnp.concatenate(
        [term[:, g * lanes : (g + 1) * lanes] for term in terms for g in range(count)], axis=0
    )


def gain_of(rows):
    count = rows.shape[0] // 2
    return jnp.concatenate([rows[g : g + 1] + rows[count + g : count + g + 1] for g in range(count)], axis=1)


def narrow(rows):
    return jnp.concatenate(
        [rows[:, g : g + LANES] for g in range(0, rows.shape[1], LANES)], axis=0
    )


def anywhere():
    return pl.BlockSpec(memory_space=pl.ANY)


def in_vmem():
    return pl.BlockSpec(memory_space=pltpu.VMEM)


def in_hbm():
    return pl.BlockSpec(memory_space=pltpu.HBM)


def in_smem():
    return pl.BlockSpec(memory_space=pltpu.SMEM)


def call(kernel, name, specs, outs, operands, flops, scratch=(), limit=24 * MIB):
    operands = [
        pltpu.with_memory_space_constraint(o, pltpu.HBM) if spec.memory_space == pltpu.HBM else o
        for o, spec in zip(operands, specs)
    ]
    size = sum(math.prod(o.shape) * jnp.dtype(o.dtype).itemsize for o in outs)
    size += sum(math.prod(o.shape) * jnp.dtype(o.dtype).itemsize for o in operands)
    return pl.pallas_call(
        kernel,
        out_shape=outs,
        in_specs=specs,
        out_specs=[in_vmem()] * len(outs),
        scratch_shapes=list(scratch),
        compiler_params=pltpu.CompilerParams(vmem_limit_bytes=limit),
        cost_estimate=pl.CostEstimate(flops=int(flops), bytes_accessed=size, transcendentals=0),
        name=name,
    )(*operands)


def stack_kernel(mesh, cot, stacked, sems):
    rows = mesh.shape[0]
    copies = [
        pltpu.make_async_copy(mesh, stacked.at[pl.ds(0, rows)], sems.at[0]),
        pltpu.make_async_copy(cot, stacked.at[pl.ds(rows, rows)], sems.at[1]),
    ]
    for copy in copies:
        copy.start()
    for copy in copies:
        copy.wait()


def near_kernel(
    scalars,
    senders,
    grid,
    edge,
    w_first,
    w_second,
    partial,
    grid_picked,
    edge_here,
    w_first_here,
    w_second_here,
    senders_here,
    grid_here,
    sems,
):
    rows_grid, width = grid.shape
    tiles = range(0, edge.shape[0], TILE)
    pairs = [(senders, senders_here), (grid, grid_here)]
    for first in (width, 0):
        rows = pl.ds(first, width)
        pairs.append((w_first.at[rows], w_first_here.at[rows]))
    for start in tiles:
        rows = pl.ds(start, TILE)
        pairs.append((edge.at[rows], edge_here.at[rows]))
    rows = pl.ds(2 * width, width)
    pairs += [(w_first.at[rows], w_first_here.at[rows]), (w_second, w_second_here)]
    copies = [
        pltpu.make_async_copy(source, target, sems.at[place])
        for place, (source, target) in enumerate(pairs)
    ]
    for copy in copies:
        copy.start()
    for copy in copies[:4]:
        copy.wait()
    for start, copy in zip(tiles, copies[4:]):
        rows = pl.ds(start, TILE)
        table = picks(senders_here[:, rows] - scalars[0], rows_grid)
        picked = dot(table, grid_here[...]).astype(jnp.bfloat16)
        grid_picked[rows, :] = picked
        copy.wait()
        partial[rows, :] = dot(edge_here[rows, :], w_first_here[0:width, :]) + dot(
            picked, w_first_here[width : 2 * width, :]
        )
    for copy in copies[-2:]:
        copy.wait()


def live_receivers(scalars, receivers, start, tile, rows_mesh):
    row = receivers[:, pl.ds(start, tile)] - scalars[1]
    row = jnp.where(
        row < rows_mesh,
        row + scalars[4],
        jnp.where(row >= 2 * rows_mesh, row - scalars[4], row),
    )
    slot = start + lax.broadcasted_iota(jnp.int32, (1, tile), 1)
    return jnp.where(slot < scalars[2], row, -1)


def edge_kernel(
    scalars,
    receivers,
    partial,
    grid_picked,
    edge,
    stack_first,
    stack_own,
    stack_second,
    w_first,
    w_second,
    norm_gain,
    sent,
    gain_term,
    grad_pre,
    grad_output,
    hidden,
    mesh_picked,
):
    width = w_second.shape[0]
    rows_mesh = stack_own.shape[0] // 2
    gain_sum = jnp.zeros((1, width), jnp.float32)
    for start in range(0, edge.shape[0], EDGE_TILE):
        rows = pl.ds(start, EDGE_TILE)
        table = picks(live_receivers(scalars, receivers, start, EDGE_TILE, rows_mesh), 3 * rows_mesh)

        def picked_rows(first):
            part = pl.ds(first, rows_mesh)
            near = jnp.concatenate([stack_first[part, :], stack_own[part, :], stack_second[part, :]], axis=0)
            return dot(table, near)

        latents = picked_rows(0).astype(jnp.bfloat16)
        upstream = picked_rows(rows_mesh)
        mesh_picked[rows, :] = latents
        pre_act = partial[rows, :] + dot(latents, w_first[2 * width : 3 * width, :])
        sigmoid = 0.5 * jnp.tanh(0.5 * pre_act) + 0.5
        hid = (pre_act * sigmoid).astype(jnp.bfloat16)
        hidden[rows, :] = hid
        output = dot(hid, w_second[...])
        centered = output - jnp.mean(output, axis=1, keepdims=True)
        inverse = lax.rsqrt(jnp.mean(centered * centered, axis=1, keepdims=True) + NORM_EPS)
        normed = centered * inverse
        gain_sum = gain_sum + jnp.sum(upstream * normed, axis=0, keepdims=True)
        scaled = upstream * norm_gain[...]
        grad_out = (
            inverse
            * (
                scaled
                - jnp.mean(scaled, axis=1, keepdims=True)
                - normed * jnp.mean(scaled * normed, axis=1, keepdims=True)
            )
        ).astype(jnp.bfloat16)
        grad_output[rows, :] = grad_out
        grad_hidden = dot(grad_out, w_second[...], 1, 1)
        grad_pre[rows, :] = (grad_hidden * sigmoid * (1.0 + pre_act * (1.0 - sigmoid))).astype(
            jnp.bfloat16
        )
    gain_term[...] = jnp.broadcast_to(gain_sum, gain_term.shape)
    sent[width : width + 16, :] = jnp.concatenate(
        [gain_rows(gain_sum, width), jnp.zeros((14, width), jnp.float32)], axis=0
    ).astype(jnp.bfloat16)

    @pl.when(scalars[3] == 0)
    def _():
        sent[0:width, :] = dot(mesh_picked[...], grad_pre[...], 0, 0).astype(jnp.bfloat16)

    @pl.when(scalars[3] != 0)
    def _():
        sent[0:width, :] = dot(edge[...], grad_pre[...], 0, 0).astype(jnp.bfloat16)


def rest_kernel(scalars, grid_picked, hidden, grad_pre, grad_output, sent):
    @pl.when(scalars[3] == 0)
    def _():
        sent[...] = dot(hidden[...], grad_output[...], 0, 0).astype(jnp.bfloat16)

    @pl.when(scalars[3] != 0)
    def _():
        sent[...] = dot(grid_picked[...], grad_pre[...], 0, 0).astype(jnp.bfloat16)


def kept_kernel(scalars, edge, grid_picked, mesh_picked, hidden, grad_pre, grad_output, kept):
    width = grad_pre.shape[1]

    @pl.when(scalars[3] != 0)
    def _():
        kept[0:width, :] = dot(mesh_picked[...], grad_pre[...], 0, 0)
        kept[width : 2 * width, :] = dot(hidden[...], grad_output[...], 0, 0)

    @pl.when(scalars[3] == 0)
    def _():
        kept[0:width, :] = dot(edge[...], grad_pre[...], 0, 0)
        kept[width : 2 * width, :] = dot(grid_picked[...], grad_pre[...], 0, 0)


def pack_kernel(kept, got, got_rest, gain_term, packed, done):
    count = packed.shape[0]
    half, width = kept.shape
    part = half // count
    tail = got[width : width + 16, :].astype(jnp.float32)
    gain = gain_rows(gain_term[0:1, :] + gain_of(tail[0:2]), LANES)
    for place in range(count):
        rows = pl.ds(place * part, part)
        first = place * part
        other = got[rows, :] if first < width else got_rest[pl.ds(first - width, part), :]
        data = narrow(kept[rows, :] + other.astype(jnp.float32))
        packed[place] = jnp.concatenate([data, gain], axis=0).astype(jnp.bfloat16)
    done[...] = jnp.zeros(done.shape, jnp.float32)


def group_sum_kernel(shares, after, packed):
    total = shares[0].astype(jnp.float32)
    for place in range(1, shares.shape[0]):
        total = total + shares[place].astype(jnp.float32)
    data = total.shape[0] - 8
    gain = gain_rows(gain_of(total[data:]), LANES)
    packed[...] = jnp.concatenate([total[:data], gain], axis=0).astype(jnp.bfloat16)


def whole_sum_kernel(factor, own, near, across, far, after, copies, gain_grad):
    own, near, across, far = [part[...].astype(jnp.float32) for part in (own, near, across, far)]
    total = ((own + across) + (near + far)) * factor
    data = copies.shape[1]
    gain_grad[...] = gain_of(total[data:])
    share = total[:data].astype(jnp.bfloat16)
    for place in range(copies.shape[0]):
        copies[place] = share


def node_kernel(
    scalars,
    senders,
    receivers,
    grad_pre,
    w_first,
    after,
    edge_grad,
    grid_grad,
    mesh_own,
    to_first,
    to_second,
):
    edges, width = grad_pre.shape
    rows_grid, rows_mesh = grid_grad.shape[0], mesh_own.shape[0]

    def through(sums, first):
        upper, lower = upper_lower(sums)
        weights = w_first[first : first + width, :]
        return dot(upper, weights, 1, 1) + dot(lower, weights, 1, 1)

    near = jnp.zeros((3 * rows_mesh, width), jnp.float32)
    here = jnp.zeros((rows_grid, width), jnp.float32)
    for start in range(0, edges, TILE):
        rows = pl.ds(start, TILE)
        terms = grad_pre[rows, :]
        near = near + dot(
            spreads(live_receivers(scalars, receivers, start, TILE, rows_mesh), 3 * rows_mesh), terms
        )
        here = here + dot(spreads(senders[:, rows] - scalars[0], rows_grid), terms)
        edge_grad[rows, :] = dot(terms, w_first[0:width, :], 1, 1).astype(jnp.bfloat16)
    mesh_terms = through(near, 2 * width)
    to_first[...] = mesh_terms[0:rows_mesh].astype(jnp.bfloat16)
    mesh_own[...] = mesh_terms[rows_mesh : 2 * rows_mesh]
    to_second[...] = mesh_terms[2 * rows_mesh : 3 * rows_mesh].astype(jnp.bfloat16)
    grid_grad[...] = through(here, width).astype(jnp.bfloat16)


def put_half(scalars, flip, shares, first, second, wide, sems):
    half, width = wide.shape
    count = shares.shape[0]
    part = half // count
    half_index = 1 - scalars[3] if flip else scalars[3]
    size = sems.shape[0]
    rows = half // size

    def each(place, act):
        source = wide.at[pl.ds(place * rows, rows)]

        @pl.when(half_index == 0)
        def _():
            act(pltpu.make_async_copy(source, first.at[pl.ds(place * rows, rows)], sems.at[place]))

        @pl.when(half_index != 0)
        def _():
            start = half + place * rows
            if start < first.shape[0]:
                target = first.at[pl.ds(start, rows)]
            else:
                target = second.at[pl.ds(start - first.shape[0], rows)]
            act(pltpu.make_async_copy(source, target, sems.at[place]))

    for place in range(size):
        for index in range(place * count // size, (place + 1) * count // size):
            share = shares[index].astype(jnp.float32)
            for g in range(width // LANES):
                wide[index * part : (index + 1) * part, g * LANES : (g + 1) * LANES] = share[
                    g * part : (g + 1) * part
                ]
        each(place, lambda copy: copy.start())
    for place in range(size):
        each(place, lambda copy: copy.wait())


def own_half_kernel(scalars, shares, first, second, wide, sems):
    put_half(scalars, False, shares, first, second, wide, sems)


def other_half_kernel(scalars, shares, first_in, second_in, first, second, wide, sems):
    put_half(scalars, True, shares, first, second, wide, sems)


def swap_pairs(value, axis, pairs):
    return lax.ppermute(value, axis, pairs + [(d, s) for s, d in pairs])


def exchanged(value, turn):
    count = lax.axis_size(SHARDS)
    return swap_pairs(value, SHARDS, [(s, s + 1) for s in range(turn, count - 1, 2)])


def swapped(value):
    return swap_pairs(value, "rep", [(0, 1)])


def per_device(
    grid_latent,
    mesh_latent,
    edge_latent,
    mesh_cotangent,
    w_first,
    w_second,
    norm_gain,
    senders,
    receivers,
    live_counts,
):
    width = w_second.shape[0]
    rows_grid = grid_latent.shape[1]
    rows_mesh = mesh_latent.shape[1]
    slots = senders.shape[0]
    group, groups = lax.axis_size(GROUP), lax.axis_size("hi")
    factor = 1.0 / math.sqrt(slots * group * groups * lax.axis_size("rep"))
    shard = lax.axis_index(SHARDS)
    scalars = jnp.stack(
        [
            shard * rows_grid,
            (shard - 1) * rows_mesh,
            live_counts[0],
            lax.axis_index("rep").astype(jnp.int32),
            jnp.where(shard % 2 == 0, 2 * rows_mesh, 0),
        ]
    ).astype(jnp.int32)
    senders, receivers = senders[None], receivers[None]
    gain = norm_gain[None]
    grid, mesh, edge, cot = grid_latent[0], mesh_latent[0], edge_latent[0], mesh_cotangent[0]
    matrix = functools.partial(jax.ShapeDtypeStruct, dtype=jnp.bfloat16)
    floats = functools.partial(jax.ShapeDtypeStruct, dtype=jnp.float32)
    unit = 2.0 * slots * width * width

    (stacked,) = call(
        stack_kernel,
        "stack",
        [in_hbm()] * 2,
        [matrix((2 * rows_mesh, width))],
        (mesh, cot),
        0,
        [pltpu.SemaphoreType.DMA((2,))],
    )
    stack_first, stack_second = exchanged(stacked, 0), exchanged(stacked, 1)
    partial, grid_picked, edge, w_first, w_second = call(
        near_kernel,
        "near",
        [in_smem()] + [in_hbm()] * 5,
        [
            floats((slots, width)),
            matrix((slots, width)),
            pltpu.VMEM((slots, width), jnp.bfloat16),
            pltpu.VMEM((3 * width, width), jnp.bfloat16),
            pltpu.VMEM((width, width), jnp.bfloat16),
        ],
        (scalars, senders, grid, edge, w_first, w_second),
        3 * unit,
        [
            pltpu.VMEM((1, slots), jnp.int32),
            pltpu.VMEM((rows_grid, width), jnp.bfloat16),
            pltpu.SemaphoreType.DMA((6 + slots // TILE,)),
        ],
    )
    sent, gain_term, grad_pre, grad_output, hidden, mesh_picked = call(
        edge_kernel,
        "edges",
        [in_smem()] + [in_vmem()] * 10,
        [
            matrix((width + 16, width)),
            floats((8, width)),
            pltpu.VMEM((slots, width), jnp.bfloat16),
        ]
        + [matrix((slots, width))] * 3,
        (
            scalars,
            receivers,
            partial,
            grid_picked,
            edge,
            stack_first,
            stacked,
            stack_second,
            w_first,
            w_second,
            gain,
        ),
        7 * unit,
    )
    got = swapped(sent)
    (rest,) = call(
        rest_kernel,
        "rest",
        [in_smem()] + [in_vmem()] * 4,
        [matrix((width, width))],
        (scalars, grid_picked, hidden, grad_pre, grad_output),
        unit,
    )
    got_rest = swapped(rest)
    (kept,) = call(
        kept_kernel,
        "kept",
        [in_smem()] + [in_vmem()] * 6,
        [floats((2 * width, width))],
        (scalars, edge, grid_picked, mesh_picked, hidden, grad_pre, grad_output),
        2 * unit,
    )
    part = 2 * width // group * width // LANES
    extra = 2 * width // LANES
    packed, done = call(
        pack_kernel,
        "pack",
        [in_vmem()] * 4,
        [matrix((group, part + extra, LANES)), floats((8, LANES))],
        (kept, got, got_rest, gain_term),
        0,
    )
    edge_grad, grid_grad, mesh_own, to_first, to_second = call(
        node_kernel,
        "nodes",
        [in_smem()] + [in_vmem()] * 4 + [anywhere()],
        [
            matrix((slots, width)),
            matrix((rows_grid, width)),
            floats((rows_mesh, width)),
            matrix((rows_mesh, width)),
            matrix((rows_mesh, width)),
        ],
        (scalars, senders, receivers, grad_pre, w_first, done),
        4 * unit,
    )
    from_first = exchanged(to_first, 0).astype(jnp.float32)
    from_second = exchanged(to_second, 1).astype(jnp.float32)
    mesh_grad = mesh_own + from_first + from_second
    shares = lax.all_to_all(packed, GROUP, 0, 0)
    (packed,) = call(
        group_sum_kernel,
        "group_sum",
        [in_vmem(), anywhere()],
        [matrix((part + extra, LANES))],
        (shares, mesh_own),
        0,
    )
    turns = [
        swap_pairs(packed, "hi", pairs)
        for pairs in ([(0, 1), (2, 3)], [(0, 2), (1, 3)], [(0, 3), (1, 2)])
    ]
    copies, gain_grad = call(
        functools.partial(whole_sum_kernel, factor),
        "whole_sum",
        [in_vmem()] * 4 + [anywhere()],
        [matrix((group, part, LANES)), floats((1, width))],
        (packed, *turns, mesh_grad),
        0,
    )
    total = lax.all_to_all(copies, GROUP, 0, 0)
    other = swapped(total)
    outs = [floats((3 * width, width)), floats((width, width))]
    halves = functools.partial(
        pl.pallas_call,
        out_shape=outs,
        out_specs=[in_hbm()] * 2,
        scratch_shapes=[
            pltpu.VMEM((2 * width, width), jnp.float32),
            pltpu.SemaphoreType.DMA((8,)),
        ],
        compiler_params=pltpu.CompilerParams(vmem_limit_bytes=24 * MIB),
        cost_estimate=pl.CostEstimate(flops=0, bytes_accessed=6 * MIB, transcendentals=0),
    )
    written = halves(own_half_kernel, in_specs=[in_smem(), in_vmem()], name="own_half")(scalars, total)
    first_grad, second_grad = halves(
        other_half_kernel,
        in_specs=[in_smem(), in_vmem()] + [in_hbm()] * 2,
        input_output_aliases={2: 0, 3: 1},
        name="other_half",
    )(scalars, other, *written)
    return (
        grid_grad[None],
        mesh_grad[None],
        edge_grad[None],
        first_grad,
        second_grad,
        gain_grad[0],
    )


def solution(mesh):
    bands, meshes, cores = mesh.devices.shape
    mesh = jax.sharding.Mesh(
        mesh.devices.reshape(bands, 4, meshes // 4, cores), ("band", "hi", "lo", "rep")
    )
    in_specs = (
        P("rep", SHARDS, None),
        P("rep", SHARDS, None),
        P("rep", SHARDS, None),
        P("rep", SHARDS, None),
        P(),
        P(),
        P(),
        P(SHARDS),
        P(SHARDS),
        P(SHARDS),
    )
    out_specs = (
        P("rep", SHARDS, None),
        P("rep", SHARDS, None),
        P("rep", SHARDS, None),
        P(),
        P(),
        P(),
    )
    return jax.shard_map(
        per_device, mesh=mesh, in_specs=in_specs, out_specs=out_specs, check_vma=False
    )
```

```python
import functools
import math

import jax
import jax.numpy as jnp
from jax import lax
from jax.experimental import pallas as pl
from jax.experimental.pallas import tpu as pltpu
from jax.sharding import PartitionSpec as P

NORM_EPS = 1e-05
SHARDS = ("band", "hi", "lo")
GROUP = ("band", "lo")
TILE = 256
EDGE_TILE = 1024
LANES = 128
MIB = 1 << 20


def dot(left, right, left_dim=1, right_dim=0):
    return lax.dot_general(
        left,
        right,
        (((left_dim,), (right_dim,)), ((), ())),
        preferred_element_type=jnp.float32,
    )


def picks(row, width):
    edges = row.shape[1]
    column = jnp.transpose(jnp.broadcast_to(row, (LANES, edges)))
    lane = lax.broadcasted_iota(jnp.int32, (edges, LANES), 1)
    return jnp.concatenate(
        [(column == lane + start).astype(jnp.float32).astype(jnp.bfloat16) for start in range(0, width, LANES)],
        axis=1,
    )


def spreads(row, width):
    edges = row.shape[1]
    place = lax.broadcasted_iota(jnp.int32, (width, edges), 0)
    return (place == row).astype(jnp.float32).astype(jnp.bfloat16)


def upper_lower(value):
    upper = value.astype(jnp.bfloat16)
    return upper, (value - upper.astype(jnp.float32)).astype(jnp.bfloat16)


def gain_rows(gain, lanes):
    terms = [term.astype(jnp.float32) for term in upper_lower(gain)]
    count = gain.shape[1] // lanes
    return jnp.concatenate(
        [term[:, g * lanes : (g + 1) * lanes] for term in terms for g in range(count)], axis=0
    )


def gain_of(rows):
    count = rows.shape[0] // 2
    return jnp.concatenate([rows[g : g + 1] + rows[count + g : count + g + 1] for g in range(count)], axis=1)


def narrow(rows):
    return jnp.concatenate(
        [rows[:, g : g + LANES] for g in range(0, rows.shape[1], LANES)], axis=0
    )


def anywhere():
    return pl.BlockSpec(memory_space=pl.ANY)


def in_vmem():
    return pl.BlockSpec(memory_space=pltpu.VMEM)


def in_hbm():
    return pl.BlockSpec(memory_space=pltpu.HBM)


def in_smem():
    return pl.BlockSpec(memory_space=pltpu.SMEM)


def call(kernel, name, specs, outs, operands, flops, scratch=(), limit=24 * MIB):
    operands = [
        pltpu.with_memory_space_constraint(o, pltpu.HBM) if spec.memory_space == pltpu.HBM else o
        for o, spec in zip(operands, specs)
    ]
    size = sum(math.prod(o.shape) * jnp.dtype(o.dtype).itemsize for o in outs)
    size += sum(math.prod(o.shape) * jnp.dtype(o.dtype).itemsize for o in operands)
    return pl.pallas_call(
        kernel,
        out_shape=outs,
        in_specs=specs,
        out_specs=[in_vmem()] * len(outs),
        scratch_shapes=list(scratch),
        compiler_params=pltpu.CompilerParams(vmem_limit_bytes=limit),
        cost_estimate=pl.CostEstimate(flops=int(flops), bytes_accessed=size, transcendentals=0),
        name=name,
    )(*operands)


def stack_kernel(mesh, cot, stacked, sems):
    rows = mesh.shape[0]
    copies = [
        pltpu.make_async_copy(mesh, stacked.at[pl.ds(0, rows)], sems.at[0]),
        pltpu.make_async_copy(cot, stacked.at[pl.ds(rows, rows)], sems.at[1]),
    ]
    for copy in copies:
        copy.start()
    for copy in copies:
        copy.wait()


def near_kernel(
    scalars,
    senders,
    grid,
    edge,
    w_first,
    w_second,
    partial,
    grid_picked,
    edge_here,
    w_first_here,
    w_second_here,
    senders_here,
    grid_here,
    sems,
):
    rows_grid, width = grid.shape
    tiles = range(0, edge.shape[0], TILE)
    pairs = [(senders, senders_here), (grid, grid_here)]
    for first in (width, 0):
        rows = pl.ds(first, width)
        pairs.append((w_first.at[rows], w_first_here.at[rows]))
    for start in tiles:
        rows = pl.ds(start, TILE)
        pairs.append((edge.at[rows], edge_here.at[rows]))
    rows = pl.ds(2 * width, width)
    pairs += [(w_first.at[rows], w_first_here.at[rows]), (w_second, w_second_here)]
    copies = [
        pltpu.make_async_copy(source, target, sems.at[place])
        for place, (source, target) in enumerate(pairs)
    ]
    for copy in copies:
        copy.start()
    for copy in copies[:4]:
        copy.wait()
    for start, copy in zip(tiles, copies[4:]):
        rows = pl.ds(start, TILE)
        table = picks(senders_here[:, rows] - scalars[0], rows_grid)
        picked = dot(table, grid_here[...]).astype(jnp.bfloat16)
        grid_picked[rows, :] = picked
        copy.wait()
        partial[rows, :] = dot(edge_here[rows, :], w_first_here[0:width, :]) + dot(
            picked, w_first_here[width : 2 * width, :]
        )
    for copy in copies[-2:]:
        copy.wait()


def live_receivers(scalars, receivers, start, tile, rows_mesh):
    row = receivers[:, pl.ds(start, tile)] - scalars[1]
    row = jnp.where(
        row < rows_mesh,
        row + scalars[4],
        jnp.where(row >= 2 * rows_mesh, row - scalars[4], row),
    )
    slot = start + lax.broadcasted_iota(jnp.int32, (1, tile), 1)
    return jnp.where(slot < scalars[2], row, -1)


def edge_kernel(
    scalars,
    receivers,
    partial,
    grid_picked,
    edge,
    stack_first,
    stack_own,
    stack_second,
    w_first,
    w_second,
    norm_gain,
    sent,
    gain_term,
    grad_pre,
    grad_output,
    hidden,
    mesh_picked,
):
    width = w_second.shape[0]
    rows_mesh = stack_own.shape[0] // 2
    gain_sum = jnp.zeros((1, width), jnp.float32)
    for start in range(0, edge.shape[0], EDGE_TILE):
        rows = pl.ds(start, EDGE_TILE)
        table = picks(live_receivers(scalars, receivers, start, EDGE_TILE, rows_mesh), 3 * rows_mesh)

        def picked_rows(first):
            part = pl.ds(first, rows_mesh)
            near = jnp.concatenate([stack_first[part, :], stack_own[part, :], stack_second[part, :]], axis=0)
            return dot(table, near)

        latents = picked_rows(0).astype(jnp.bfloat16)
        upstream = picked_rows(rows_mesh)
        mesh_picked[rows, :] = latents
        pre_act = partial[rows, :] + dot(latents, w_first[2 * width : 3 * width, :])
        sigmoid = 0.5 * jnp.tanh(0.5 * pre_act) + 0.5
        hid = (pre_act * sigmoid).astype(jnp.bfloat16)
        hidden[rows, :] = hid
        output = dot(hid, w_second[...])
        centered = output - jnp.mean(output, axis=1, keepdims=True)
        inverse = lax.rsqrt(jnp.mean(centered * centered, axis=1, keepdims=True) + NORM_EPS)
        normed = centered * inverse
        gain_sum = gain_sum + jnp.sum(upstream * normed, axis=0, keepdims=True)
        scaled = upstream * norm_gain[...]
        grad_out = (
            inverse
            * (
                scaled
                - jnp.mean(scaled, axis=1, keepdims=True)
                - normed * jnp.mean(scaled * normed, axis=1, keepdims=True)
            )
        ).astype(jnp.bfloat16)
        grad_output[rows, :] = grad_out
        grad_hidden = dot(grad_out, w_second[...], 1, 1)
        grad_pre[rows, :] = (grad_hidden * sigmoid * (1.0 + pre_act * (1.0 - sigmoid))).astype(
            jnp.bfloat16
        )
    gain_term[...] = jnp.broadcast_to(gain_sum, gain_term.shape)
    sent[2 * width : 2 * width + 16, :] = jnp.concatenate(
        [gain_rows(gain_sum, width), jnp.zeros((14, width), jnp.float32)], axis=0
    ).astype(jnp.bfloat16)

    @pl.when(scalars[3] == 0)
    def _():
        sent[0:width, :] = dot(mesh_picked[...], grad_pre[...], 0, 0).astype(jnp.bfloat16)
        sent[width : 2 * width, :] = dot(hidden[...], grad_output[...], 0, 0).astype(jnp.bfloat16)

    @pl.when(scalars[3] != 0)
    def _():
        sent[0:width, :] = dot(edge[...], grad_pre[...], 0, 0).astype(jnp.bfloat16)
        sent[width : 2 * width, :] = dot(grid_picked[...], grad_pre[...], 0, 0).astype(jnp.bfloat16)


def kept_kernel(scalars, edge, grid_picked, mesh_picked, hidden, grad_pre, grad_output, kept):
    width = grad_pre.shape[1]

    @pl.when(scalars[3] != 0)
    def _():
        kept[0:width, :] = dot(mesh_picked[...], grad_pre[...], 0, 0)
        kept[width : 2 * width, :] = dot(hidden[...], grad_output[...], 0, 0)

    @pl.when(scalars[3] == 0)
    def _():
        kept[0:width, :] = dot(edge[...], grad_pre[...], 0, 0)
        kept[width : 2 * width, :] = dot(grid_picked[...], grad_pre[...], 0, 0)


def pack_kernel(kept, got, gain_term, packed):
    count = packed.shape[0]
    half, width = kept.shape
    part = half // count
    tail = got[half : half + 16, :].astype(jnp.float32)
    gain = gain_rows(gain_term[0:1, :] + gain_of(tail[0:2]), LANES)
    for place in range(count):
        rows = pl.ds(place * part, part)
        data = narrow(kept[rows, :] + got[rows, :].astype(jnp.float32))
        packed[place] = jnp.concatenate([data, gain], axis=0).astype(jnp.bfloat16)


def group_sum_kernel(shares, packed):
    total = shares[0].astype(jnp.float32)
    for place in range(1, shares.shape[0]):
        total = total + shares[place].astype(jnp.float32)
    data = total.shape[0] - 8
    gain = gain_rows(gain_of(total[data:]), LANES)
    packed[...] = jnp.concatenate([total[:data], gain], axis=0).astype(jnp.bfloat16)


def whole_sum_kernel(factor, own, near, across, far, after, copies, gain_grad):
    own, near, across, far = [part[...].astype(jnp.float32) for part in (own, near, across, far)]
    total = ((own + across) + (near + far)) * factor
    data = copies.shape[1]
    gain_grad[...] = jnp.broadcast_to(gain_of(total[data:]), gain_grad.shape)
    share = total[:data].astype(jnp.bfloat16)
    for place in range(copies.shape[0]):
        copies[place] = share


def node_kernel(
    scalars,
    senders,
    receivers,
    grad_pre,
    w_first,
    after,
    edge_grad,
    grid_grad,
    mesh_own,
    to_first,
    to_second,
):
    edges, width = grad_pre.shape
    rows_grid, rows_mesh = grid_grad.shape[0], mesh_own.shape[0]

    def through(sums, first):
        upper, lower = upper_lower(sums)
        weights = w_first[first : first + width, :]
        return dot(upper, weights, 1, 1) + dot(lower, weights, 1, 1)

    near = jnp.zeros((3 * rows_mesh, width), jnp.float32)
    here = jnp.zeros((rows_grid, width), jnp.float32)
    for start in range(0, edges, TILE):
        rows = pl.ds(start, TILE)
        terms = grad_pre[rows, :]
        near = near + dot(
            spreads(live_receivers(scalars, receivers, start, TILE, rows_mesh), 3 * rows_mesh), terms
        )
        here = here + dot(spreads(senders[:, rows] - scalars[0], rows_grid), terms)
        edge_grad[rows, :] = dot(terms, w_first[0:width, :], 1, 1).astype(jnp.bfloat16)
    mesh_terms = through(near, 2 * width)
    to_first[...] = mesh_terms[0:rows_mesh].astype(jnp.bfloat16)
    mesh_own[...] = mesh_terms[rows_mesh : 2 * rows_mesh]
    to_second[...] = mesh_terms[2 * rows_mesh : 3 * rows_mesh].astype(jnp.bfloat16)
    grid_grad[...] = through(here, width).astype(jnp.bfloat16)


def put_half(scalars, flip, shares, first, second, wide, sems):
    half, width = wide.shape
    count = shares.shape[0]
    part = half // count
    half_index = 1 - scalars[3] if flip else scalars[3]
    size = sems.shape[0]
    rows = half // size

    def each(place, act):
        source = wide.at[pl.ds(place * rows, rows)]

        @pl.when(half_index == 0)
        def _():
            act(pltpu.make_async_copy(source, first.at[pl.ds(place * rows, rows)], sems.at[place]))

        @pl.when(half_index != 0)
        def _():
            start = half + place * rows
            if start < first.shape[0]:
                target = first.at[pl.ds(start, rows)]
            else:
                target = second.at[pl.ds(start - first.shape[0], rows)]
            act(pltpu.make_async_copy(source, target, sems.at[place]))

    for place in range(size):
        for index in range(place * count // size, (place + 1) * count // size):
            share = shares[index].astype(jnp.float32)
            for g in range(width // LANES):
                wide[index * part : (index + 1) * part, g * LANES : (g + 1) * LANES] = share[
                    g * part : (g + 1) * part
                ]
        each(place, lambda copy: copy.start())
    for place in range(size):
        each(place, lambda copy: copy.wait())


def own_half_kernel(scalars, shares, first, second, wide, sems):
    put_half(scalars, False, shares, first, second, wide, sems)


def other_half_kernel(scalars, shares, first_in, second_in, first, second, wide, sems):
    put_half(scalars, True, shares, first, second, wide, sems)


def swap_pairs(value, axis, pairs):
    return lax.ppermute(value, axis, pairs + [(d, s) for s, d in pairs])


def exchanged(value, turn):
    count = lax.axis_size(SHARDS)
    return swap_pairs(value, SHARDS, [(s, s + 1) for s in range(turn, count - 1, 2)])


def swapped(value):
    return swap_pairs(value, "rep", [(0, 1)])


def per_device(
    grid_latent,
    mesh_latent,
    edge_latent,
    mesh_cotangent,
    w_first,
    w_second,
    norm_gain,
    senders,
    receivers,
    live_counts,
):
    width = w_second.shape[0]
    rows_grid = grid_latent.shape[1]
    rows_mesh = mesh_latent.shape[1]
    slots = senders.shape[0]
    group, groups = lax.axis_size(GROUP), lax.axis_size("hi")
    factor = 1.0 / math.sqrt(slots * group * groups * lax.axis_size("rep"))
    shard = lax.axis_index(SHARDS)
    scalars = jnp.stack(
        [
            shard * rows_grid,
            (shard - 1) * rows_mesh,
            live_counts[0],
            lax.axis_index("rep").astype(jnp.int32),
            jnp.where(shard % 2 == 0, 2 * rows_mesh, 0),
        ]
    ).astype(jnp.int32)
    senders, receivers = senders[None], receivers[None]
    gain = norm_gain[None]
    grid, mesh, edge, cot = grid_latent[0], mesh_latent[0], edge_latent[0], mesh_cotangent[0]
    matrix = functools.partial(jax.ShapeDtypeStruct, dtype=jnp.bfloat16)
    floats = functools.partial(jax.ShapeDtypeStruct, dtype=jnp.float32)
    unit = 2.0 * slots * width * width

    (stacked,) = call(
        stack_kernel,
        "stack",
        [in_hbm()] * 2,
        [matrix((2 * rows_mesh, width))],
        (mesh, cot),
        0,
        [pltpu.SemaphoreType.DMA((2,))],
    )
    stack_first, stack_second = exchanged(stacked, 0), exchanged(stacked, 1)
    partial, grid_picked, edge, w_first, w_second = call(
        near_kernel,
        "near",
        [in_smem()] + [in_hbm()] * 5,
        [
            floats((slots, width)),
            matrix((slots, width)),
            pltpu.VMEM((slots, width), jnp.bfloat16),
            pltpu.VMEM((3 * width, width), jnp.bfloat16),
            pltpu.VMEM((width, width), jnp.bfloat16),
        ],
        (scalars, senders, grid, edge, w_first, w_second),
        3 * unit,
        [
            pltpu.VMEM((1, slots), jnp.int32),
            pltpu.VMEM((rows_grid, width), jnp.bfloat16),
            pltpu.SemaphoreType.DMA((6 + slots // TILE,)),
        ],
    )
    sent, gain_term, grad_pre, grad_output, hidden, mesh_picked = call(
        edge_kernel,
        "edges",
        [in_smem()] + [in_vmem()] * 10,
        [
            matrix((2 * width + 16, width)),
            floats((8, width)),
            pltpu.VMEM((slots, width), jnp.bfloat16),
        ]
        + [matrix((slots, width))] * 3,
        (
            scalars,
            receivers,
            partial,
            grid_picked,
            edge,
            stack_first,
            stacked,
            stack_second,
            w_first,
            w_second,
            gain,
        ),
        7 * unit,
    )
    got = swapped(sent)
    (kept,) = call(
        kept_kernel,
        "kept",
        [in_smem()] + [in_vmem()] * 6,
        [floats((2 * width, width))],
        (scalars, edge, grid_picked, mesh_picked, hidden, grad_pre, grad_output),
        2 * unit,
    )
    part = 2 * width // group * width // LANES
    extra = 2 * width // LANES
    (packed,) = call(
        pack_kernel,
        "pack",
        [in_vmem()] * 3,
        [matrix((group, part + extra, LANES))],
        (kept, got, gain_term),
        0,
    )
    shares = lax.all_to_all(packed, GROUP, 0, 0)
    (packed,) = call(
        group_sum_kernel,
        "group_sum",
        [in_vmem()],
        [matrix((part + extra, LANES))],
        (shares,),
        0,
    )
    turns = [
        swap_pairs(packed, "hi", pairs)
        for pairs in ([(0, 1), (2, 3)], [(0, 2), (1, 3)], [(0, 3), (1, 2)])
    ]
    edge_grad, grid_grad, mesh_own, to_first, to_second = call(
        node_kernel,
        "nodes",
        [in_smem()] + [in_vmem()] * 4 + [anywhere()],
        [
            matrix((slots, width)),
            matrix((rows_grid, width)),
            floats((rows_mesh, width)),
            matrix((rows_mesh, width)),
            matrix((rows_mesh, width)),
        ],
        (scalars, senders, receivers, grad_pre, w_first, packed),
        4 * unit,
    )
    from_first = exchanged(to_first, 0).astype(jnp.float32)
    from_second = exchanged(to_second, 1).astype(jnp.float32)
    mesh_grad = mesh_own + from_first + from_second
    copies, gain_grad = call(
        functools.partial(whole_sum_kernel, factor),
        "whole_sum",
        [in_vmem()] * 4 + [anywhere()],
        [matrix((group, part, LANES)), floats((8, width))],
        (packed, *turns, mesh_own),
        0,
    )
    total = lax.all_to_all(copies, GROUP, 0, 0)
    other = swapped(total)
    outs = [floats((3 * width, width)), floats((width, width))]
    halves = functools.partial(
        pl.pallas_call,
        out_shape=outs,
        out_specs=[in_hbm()] * 2,
        scratch_shapes=[
            pltpu.VMEM((2 * width, width), jnp.float32),
            pltpu.SemaphoreType.DMA((8,)),
        ],
        compiler_params=pltpu.CompilerParams(vmem_limit_bytes=24 * MIB),
        cost_estimate=pl.CostEstimate(flops=0, bytes_accessed=6 * MIB, transcendentals=0),
    )
    written = halves(own_half_kernel, in_specs=[in_smem(), in_vmem()], name="own_half")(scalars, total)
    first_grad, second_grad = halves(
        other_half_kernel,
        in_specs=[in_smem(), in_vmem()] + [in_hbm()] * 2,
        input_output_aliases={2: 0, 3: 1},
        name="other_half",
    )(scalars, other, *written)
    return (
        grid_grad[None],
        mesh_grad[None],
        edge_grad[None],
        first_grad,
        second_grad,
        gain_grad[0],
    )


def solution(mesh):
    bands, meshes, cores = mesh.devices.shape
    mesh = jax.sharding.Mesh(
        mesh.devices.reshape(bands, 4, meshes // 4, cores), ("band", "hi", "lo", "rep")
    )
    in_specs = (
        P("rep", SHARDS, None),
        P("rep", SHARDS, None),
        P("rep", SHARDS, None),
        P("rep", SHARDS, None),
        P(),
        P(),
        P(),
        P(SHARDS),
        P(SHARDS),
        P(SHARDS),
    )
    out_specs = (
        P("rep", SHARDS, None),
        P("rep", SHARDS, None),
        P("rep", SHARDS, None),
        P(),
        P(),
        P(),
    )
    return jax.shard_map(
        per_device, mesh=mesh, in_specs=in_specs, out_specs=out_specs, check_vma=False
    )
```

```python
import functools
import math

import jax
import jax.numpy as jnp
from jax import lax
from jax.experimental import pallas as pl
from jax.experimental.pallas import tpu as pltpu
from jax.sharding import PartitionSpec as P

NORM_EPS = 1e-05
SHARDS = ("band", "hi", "lo")
GROUP = ("band", "lo")
TILE = 256
EDGE_TILE = 1024
LANES = 128
MIB = 1 << 20


def dot(left, right, left_dim=1, right_dim=0):
    return lax.dot_general(
        left,
        right,
        (((left_dim,), (right_dim,)), ((), ())),
        preferred_element_type=jnp.float32,
    )


def picks(row, width):
    edges = row.shape[1]
    column = jnp.transpose(jnp.broadcast_to(row, (LANES, edges)))
    lane = lax.broadcasted_iota(jnp.int32, (edges, LANES), 1)
    return jnp.concatenate(
        [(column == lane + start).astype(jnp.float32).astype(jnp.bfloat16) for start in range(0, width, LANES)],
        axis=1,
    )


def spreads(row, width):
    edges = row.shape[1]
    place = lax.broadcasted_iota(jnp.int32, (width, edges), 0)
    return (place == row).astype(jnp.float32).astype(jnp.bfloat16)


def upper_lower(value):
    upper = value.astype(jnp.bfloat16)
    return upper, (value - upper.astype(jnp.float32)).astype(jnp.bfloat16)


def gain_rows(gain, lanes):
    terms = [term.astype(jnp.float32) for term in upper_lower(gain)]
    count = gain.shape[1] // lanes
    return jnp.concatenate(
        [term[:, g * lanes : (g + 1) * lanes] for term in terms for g in range(count)], axis=0
    )


def gain_of(rows):
    count = rows.shape[0] // 2
    return jnp.concatenate([rows[g : g + 1] + rows[count + g : count + g + 1] for g in range(count)], axis=1)


def narrow(rows):
    return jnp.concatenate(
        [rows[:, g : g + LANES] for g in range(0, rows.shape[1], LANES)], axis=0
    )


def anywhere():
    return pl.BlockSpec(memory_space=pl.ANY)


def in_vmem():
    return pl.BlockSpec(memory_space=pltpu.VMEM)


def in_hbm():
    return pl.BlockSpec(memory_space=pltpu.HBM)


def in_smem():
    return pl.BlockSpec(memory_space=pltpu.SMEM)


def call(kernel, name, specs, outs, operands, flops, scratch=(), limit=24 * MIB):
    operands = [
        pltpu.with_memory_space_constraint(o, pltpu.HBM) if spec.memory_space == pltpu.HBM else o
        for o, spec in zip(operands, specs)
    ]
    size = sum(math.prod(o.shape) * jnp.dtype(o.dtype).itemsize for o in outs)
    size += sum(math.prod(o.shape) * jnp.dtype(o.dtype).itemsize for o in operands)
    return pl.pallas_call(
        kernel,
        out_shape=outs,
        in_specs=specs,
        out_specs=[in_vmem()] * len(outs),
        scratch_shapes=list(scratch),
        compiler_params=pltpu.CompilerParams(vmem_limit_bytes=limit),
        cost_estimate=pl.CostEstimate(flops=int(flops), bytes_accessed=size, transcendentals=0),
        name=name,
    )(*operands)


def stack_kernel(mesh, cot, stacked, sems):
    rows = mesh.shape[0]
    copies = [
        pltpu.make_async_copy(mesh, stacked.at[pl.ds(0, rows)], sems.at[0]),
        pltpu.make_async_copy(cot, stacked.at[pl.ds(rows, rows)], sems.at[1]),
    ]
    for copy in copies:
        copy.start()
    for copy in copies:
        copy.wait()


def near_kernel(
    scalars,
    senders,
    grid,
    edge,
    w_first,
    w_second,
    partial,
    grid_picked,
    edge_here,
    w_first_here,
    w_second_here,
    senders_here,
    grid_here,
    sems,
):
    rows_grid, width = grid.shape
    tiles = range(0, edge.shape[0], TILE)
    pairs = [(senders, senders_here), (grid, grid_here)]
    for first in (width, 0):
        rows = pl.ds(first, width)
        pairs.append((w_first.at[rows], w_first_here.at[rows]))
    for start in tiles:
        rows = pl.ds(start, TILE)
        pairs.append((edge.at[rows], edge_here.at[rows]))
    rows = pl.ds(2 * width, width)
    pairs += [(w_first.at[rows], w_first_here.at[rows]), (w_second, w_second_here)]
    copies = [
        pltpu.make_async_copy(source, target, sems.at[place])
        for place, (source, target) in enumerate(pairs)
    ]
    for copy in copies:
        copy.start()
    for copy in copies[:4]:
        copy.wait()
    for start, copy in zip(tiles, copies[4:]):
        rows = pl.ds(start, TILE)
        table = picks(senders_here[:, rows] - scalars[0], rows_grid)
        picked = dot(table, grid_here[...]).astype(jnp.bfloat16)
        grid_picked[rows, :] = picked
        copy.wait()
        partial[rows, :] = dot(edge_here[rows, :], w_first_here[0:width, :]) + dot(
            picked, w_first_here[width : 2 * width, :]
        )
    for copy in copies[-2:]:
        copy.wait()


def live_receivers(scalars, receivers, start, tile, rows_mesh):
    row = receivers[:, pl.ds(start, tile)] - scalars[1]
    row = jnp.where(
        row < rows_mesh,
        row + scalars[4],
        jnp.where(row >= 2 * rows_mesh, row - scalars[4], row),
    )
    slot = start + lax.broadcasted_iota(jnp.int32, (1, tile), 1)
    return jnp.where(slot < scalars[2], row, -1)


def edge_kernel(
    scalars,
    receivers,
    partial,
    grid_picked,
    edge,
    stack_first,
    stack_own,
    stack_second,
    w_first,
    w_second,
    norm_gain,
    sent,
    gain_term,
    grad_pre,
    grad_output,
    hidden,
    mesh_picked,
):
    width = w_second.shape[0]
    rows_mesh = stack_own.shape[0] // 2
    gain_sum = jnp.zeros((1, width), jnp.float32)
    for start in range(0, edge.shape[0], EDGE_TILE):
        rows = pl.ds(start, EDGE_TILE)
        table = picks(live_receivers(scalars, receivers, start, EDGE_TILE, rows_mesh), 3 * rows_mesh)

        def picked_rows(first):
            part = pl.ds(first, rows_mesh)
            near = jnp.concatenate([stack_first[part, :], stack_own[part, :], stack_second[part, :]], axis=0)
            return dot(table, near)

        latents = picked_rows(0).astype(jnp.bfloat16)
        upstream = picked_rows(rows_mesh)
        mesh_picked[rows, :] = latents
        pre_act = partial[rows, :] + dot(latents, w_first[2 * width : 3 * width, :])
        sigmoid = 0.5 * jnp.tanh(0.5 * pre_act) + 0.5
        hid = (pre_act * sigmoid).astype(jnp.bfloat16)
        hidden[rows, :] = hid
        output = dot(hid, w_second[...])
        centered = output - jnp.mean(output, axis=1, keepdims=True)
        inverse = lax.rsqrt(jnp.mean(centered * centered, axis=1, keepdims=True) + NORM_EPS)
        normed = centered * inverse
        gain_sum = gain_sum + jnp.sum(upstream * normed, axis=0, keepdims=True)
        scaled = upstream * norm_gain[...]
        grad_out = (
            inverse
            * (
                scaled
                - jnp.mean(scaled, axis=1, keepdims=True)
                - normed * jnp.mean(scaled * normed, axis=1, keepdims=True)
            )
        ).astype(jnp.bfloat16)
        grad_output[rows, :] = grad_out
        grad_hidden = dot(grad_out, w_second[...], 1, 1)
        grad_pre[rows, :] = (grad_hidden * sigmoid * (1.0 + pre_act * (1.0 - sigmoid))).astype(
            jnp.bfloat16
        )
    gain_term[...] = jnp.broadcast_to(gain_sum, gain_term.shape)
    sent[2 * width : 2 * width + 16, :] = jnp.concatenate(
        [gain_rows(gain_sum, width), jnp.zeros((14, width), jnp.float32)], axis=0
    ).astype(jnp.bfloat16)

    @pl.when(scalars[3] == 0)
    def _():
        sent[0:width, :] = dot(mesh_picked[...], grad_pre[...], 0, 0).astype(jnp.bfloat16)
        sent[width : 2 * width, :] = dot(hidden[...], grad_output[...], 0, 0).astype(jnp.bfloat16)

    @pl.when(scalars[3] != 0)
    def _():
        sent[0:width, :] = dot(edge[...], grad_pre[...], 0, 0).astype(jnp.bfloat16)
        sent[width : 2 * width, :] = dot(grid_picked[...], grad_pre[...], 0, 0).astype(jnp.bfloat16)


def kept_kernel(scalars, edge, grid_picked, mesh_picked, hidden, grad_pre, grad_output, kept):
    width = grad_pre.shape[1]

    @pl.when(scalars[3] != 0)
    def _():
        kept[0:width, :] = dot(mesh_picked[...], grad_pre[...], 0, 0)
        kept[width : 2 * width, :] = dot(hidden[...], grad_output[...], 0, 0)

    @pl.when(scalars[3] == 0)
    def _():
        kept[0:width, :] = dot(edge[...], grad_pre[...], 0, 0)
        kept[width : 2 * width, :] = dot(grid_picked[...], grad_pre[...], 0, 0)


def pack_kernel(kept, got, gain_term, packed, done):
    count = packed.shape[0]
    half, width = kept.shape
    part = half // count
    tail = got[half : half + 16, :].astype(jnp.float32)
    gain = gain_rows(gain_term[0:1, :] + gain_of(tail[0:2]), LANES)
    for place in range(count):
        rows = pl.ds(place * part, part)
        data = narrow(kept[rows, :] + got[rows, :].astype(jnp.float32))
        packed[place] = jnp.concatenate([data, gain], axis=0).astype(jnp.bfloat16)
    done[...] = jnp.zeros(done.shape, jnp.float32)


def group_sum_kernel(shares, after, packed):
    total = shares[0].astype(jnp.float32)
    for place in range(1, shares.shape[0]):
        total = total + shares[place].astype(jnp.float32)
    data = total.shape[0] - 8
    gain = gain_rows(gain_of(total[data:]), LANES)
    packed[...] = jnp.concatenate([total[:data], gain], axis=0).astype(jnp.bfloat16)


def whole_sum_kernel(factor, own, near, far, across, after, copies, gain_grad):
    own, near, far, across = [part[...].astype(jnp.float32) for part in (own, near, far, across)]
    total = ((own + across) + (near + far)) * factor
    data = copies.shape[1]
    gain_grad[...] = jnp.broadcast_to(gain_of(total[data:]), gain_grad.shape)
    share = total[:data].astype(jnp.bfloat16)
    for place in range(copies.shape[0]):
        copies[place] = share


def node_kernel(
    scalars,
    senders,
    receivers,
    grad_pre,
    w_first,
    after,
    edge_grad,
    grid_grad,
    mesh_own,
    to_first,
    to_second,
):
    edges, width = grad_pre.shape
    rows_grid, rows_mesh = grid_grad.shape[0], mesh_own.shape[0]

    def through(sums, first):
        upper, lower = upper_lower(sums)
        weights = w_first[first : first + width, :]
        return dot(upper, weights, 1, 1) + dot(lower, weights, 1, 1)

    near = jnp.zeros((3 * rows_mesh, width), jnp.float32)
    here = jnp.zeros((rows_grid, width), jnp.float32)
    for start in range(0, edges, TILE):
        rows = pl.ds(start, TILE)
        terms = grad_pre[rows, :]
        near = near + dot(
            spreads(live_receivers(scalars, receivers, start, TILE, rows_mesh), 3 * rows_mesh), terms
        )
        here = here + dot(spreads(senders[:, rows] - scalars[0], rows_grid), terms)
        edge_grad[rows, :] = dot(terms, w_first[0:width, :], 1, 1).astype(jnp.bfloat16)
    mesh_terms = through(near, 2 * width)
    to_first[...] = mesh_terms[0:rows_mesh].astype(jnp.bfloat16)
    mesh_own[...] = mesh_terms[rows_mesh : 2 * rows_mesh]
    to_second[...] = mesh_terms[2 * rows_mesh : 3 * rows_mesh].astype(jnp.bfloat16)
    grid_grad[...] = through(here, width).astype(jnp.bfloat16)


def put_half(scalars, flip, shares, first, second, wide, sems):
    half, width = wide.shape
    count = shares.shape[0]
    part = half // count
    half_index = 1 - scalars[3] if flip else scalars[3]
    size = sems.shape[0]
    rows = half // size

    def each(place, act):
        source = wide.at[pl.ds(place * rows, rows)]

        @pl.when(half_index == 0)
        def _():
            act(pltpu.make_async_copy(source, first.at[pl.ds(place * rows, rows)], sems.at[place]))

        @pl.when(half_index != 0)
        def _():
            start = half + place * rows
            if start < first.shape[0]:
                target = first.at[pl.ds(start, rows)]
            else:
                target = second.at[pl.ds(start - first.shape[0], rows)]
            act(pltpu.make_async_copy(source, target, sems.at[place]))

    for place in range(size):
        for index in range(place * count // size, (place + 1) * count // size):
            share = shares[index].astype(jnp.float32)
            for g in range(width // LANES):
                wide[index * part : (index + 1) * part, g * LANES : (g + 1) * LANES] = share[
                    g * part : (g + 1) * part
                ]
        each(place, lambda copy: copy.start())
    for place in range(size):
        each(place, lambda copy: copy.wait())


def own_half_kernel(scalars, shares, first, second, wide, sems):
    put_half(scalars, False, shares, first, second, wide, sems)


def other_half_kernel(scalars, shares, first_in, second_in, first, second, wide, sems):
    put_half(scalars, True, shares, first, second, wide, sems)


def swap_pairs(value, axis, pairs):
    return lax.ppermute(value, axis, pairs + [(d, s) for s, d in pairs])


def exchanged(value, turn):
    count = lax.axis_size(SHARDS)
    return swap_pairs(value, SHARDS, [(s, s + 1) for s in range(turn, count - 1, 2)])


def swapped(value):
    return swap_pairs(value, "rep", [(0, 1)])


def per_device(
    grid_latent,
    mesh_latent,
    edge_latent,
    mesh_cotangent,
    w_first,
    w_second,
    norm_gain,
    senders,
    receivers,
    live_counts,
):
    width = w_second.shape[0]
    rows_grid = grid_latent.shape[1]
    rows_mesh = mesh_latent.shape[1]
    slots = senders.shape[0]
    group, groups = lax.axis_size(GROUP), lax.axis_size("hi")
    factor = 1.0 / math.sqrt(slots * group * groups * lax.axis_size("rep"))
    shard = lax.axis_index(SHARDS)
    scalars = jnp.stack(
        [
            shard * rows_grid,
            (shard - 1) * rows_mesh,
            live_counts[0],
            lax.axis_index("rep").astype(jnp.int32),
            jnp.where(shard % 2 == 0, 2 * rows_mesh, 0),
        ]
    ).astype(jnp.int32)
    senders, receivers = senders[None], receivers[None]
    gain = norm_gain[None]
    grid, mesh, edge, cot = grid_latent[0], mesh_latent[0], edge_latent[0], mesh_cotangent[0]
    matrix = functools.partial(jax.ShapeDtypeStruct, dtype=jnp.bfloat16)
    floats = functools.partial(jax.ShapeDtypeStruct, dtype=jnp.float32)
    unit = 2.0 * slots * width * width

    (stacked,) = call(
        stack_kernel,
        "stack",
        [in_hbm()] * 2,
        [matrix((2 * rows_mesh, width))],
        (mesh, cot),
        0,
        [pltpu.SemaphoreType.DMA((2,))],
    )
    stack_first, stack_second = exchanged(stacked, 0), exchanged(stacked, 1)
    partial, grid_picked, edge, w_first, w_second = call(
        near_kernel,
        "near",
        [in_smem()] + [in_hbm()] * 5,
        [
            floats((slots, width)),
            matrix((slots, width)),
            pltpu.VMEM((slots, width), jnp.bfloat16),
            pltpu.VMEM((3 * width, width), jnp.bfloat16),
            pltpu.VMEM((width, width), jnp.bfloat16),
        ],
        (scalars, senders, grid, edge, w_first, w_second),
        3 * unit,
        [
            pltpu.VMEM((1, slots), jnp.int32),
            pltpu.VMEM((rows_grid, width), jnp.bfloat16),
            pltpu.SemaphoreType.DMA((6 + slots // TILE,)),
        ],
    )
    sent, gain_term, grad_pre, grad_output, hidden, mesh_picked = call(
        edge_kernel,
        "edges",
        [in_smem()] + [in_vmem()] * 10,
        [
            matrix((2 * width + 16, width)),
            floats((8, width)),
            pltpu.VMEM((slots, width), jnp.bfloat16),
        ]
        + [matrix((slots, width))] * 3,
        (
            scalars,
            receivers,
            partial,
            grid_picked,
            edge,
            stack_first,
            stacked,
            stack_second,
            w_first,
            w_second,
            gain,
        ),
        7 * unit,
    )
    got = swapped(sent)
    (kept,) = call(
        kept_kernel,
        "kept",
        [in_smem()] + [in_vmem()] * 6,
        [floats((2 * width, width))],
        (scalars, edge, grid_picked, mesh_picked, hidden, grad_pre, grad_output),
        2 * unit,
    )
    part = 2 * width // group * width // LANES
    extra = 2 * width // LANES
    packed, done = call(
        pack_kernel,
        "pack",
        [in_vmem()] * 3,
        [matrix((group, part + extra, LANES)), floats((8, LANES))],
        (kept, got, gain_term),
        0,
    )
    edge_grad, grid_grad, mesh_own, to_first, to_second = call(
        node_kernel,
        "nodes",
        [in_smem()] + [in_vmem()] * 4 + [anywhere()],
        [
            matrix((slots, width)),
            matrix((rows_grid, width)),
            floats((rows_mesh, width)),
            matrix((rows_mesh, width)),
            matrix((rows_mesh, width)),
        ],
        (scalars, senders, receivers, grad_pre, w_first, done),
        4 * unit,
    )
    from_first = exchanged(to_first, 0).astype(jnp.float32)
    from_second = exchanged(to_second, 1).astype(jnp.float32)
    mesh_grad = mesh_own + from_first + from_second
    shares = lax.all_to_all(packed, GROUP, 0, 0)
    (packed,) = call(
        group_sum_kernel,
        "group_sum",
        [in_vmem(), anywhere()],
        [matrix((part + extra, LANES))],
        (shares, mesh_own),
        0,
    )
    turns = [
        swap_pairs(packed, "hi", pairs)
        for pairs in ([(0, 1), (2, 3)], [(0, 3), (1, 2)], [(0, 2), (1, 3)])
    ]
    copies, gain_grad = call(
        functools.partial(whole_sum_kernel, factor),
        "whole_sum",
        [in_vmem()] * 4 + [anywhere()],
        [matrix((group, part, LANES)), floats((8, width))],
        (packed, *turns, mesh_grad),
        0,
    )
    total = lax.all_to_all(copies, GROUP, 0, 0)
    other = swapped(total)
    outs = [floats((3 * width, width)), floats((width, width))]
    halves = functools.partial(
        pl.pallas_call,
        out_shape=outs,
        out_specs=[in_hbm()] * 2,
        scratch_shapes=[
            pltpu.VMEM((2 * width, width), jnp.float32),
            pltpu.SemaphoreType.DMA((8,)),
        ],
        compiler_params=pltpu.CompilerParams(vmem_limit_bytes=24 * MIB),
        cost_estimate=pl.CostEstimate(flops=0, bytes_accessed=6 * MIB, transcendentals=0),
    )
    written = halves(own_half_kernel, in_specs=[in_smem(), in_vmem()], name="own_half")(scalars, total)
    first_grad, second_grad = halves(
        other_half_kernel,
        in_specs=[in_smem(), in_vmem()] + [in_hbm()] * 2,
        input_output_aliases={2: 0, 3: 1},
        name="other_half",
    )(scalars, other, *written)
    return (
        grid_grad[None],
        mesh_grad[None],
        edge_grad[None],
        first_grad,
        second_grad,
        gain_grad[0],
    )


def solution(mesh):
    bands, meshes, cores = mesh.devices.shape
    mesh = jax.sharding.Mesh(
        mesh.devices.reshape(bands, 4, meshes // 4, cores), ("band", "hi", "lo", "rep")
    )
    in_specs = (
        P("rep", SHARDS, None),
        P("rep", SHARDS, None),
        P("rep", SHARDS, None),
        P("rep", SHARDS, None),
        P(),
        P(),
        P(),
        P(SHARDS),
        P(SHARDS),
        P(SHARDS),
    )
    out_specs = (
        P("rep", SHARDS, None),
        P("rep", SHARDS, None),
        P("rep", SHARDS, None),
        P(),
        P(),
        P(),
    )
    return jax.shard_map(
        per_device, mesh=mesh, in_specs=in_specs, out_specs=out_specs, check_vma=False
    )
```
